128 devices in a mesh: tiles: 64 (over y_hi, z, x, core), chan: 2 (over y_lo).
Axes of the slice: x: 4, y: 4 (y_hi: 2, y_lo: 2; y = y_hi * 2 + y_lo), z: 4, core: 2. Of those that a mesh axis runs over, the one named last changes fastest.
Arguments:
- inputs: bfloat16 [64, 96, 96, 256], P('tiles', None, None, 'chan'), may hold values from -6 to 6
- cotangent: bfloat16 [64, 96, 96, 256], P('tiles', None, None, 'chan'), may hold values from -6 to 6
- wet: int32 [64, 96, 96], P('tiles'), may hold values from 0 to 1, as said below
- neighbours: int32 [64, 8], replicated, may hold values from -1 to 63, as said below
- depth_weight: float32 [7, 7, 256], P(None, None, 'chan'), may hold values from -0.875 to 0.875
- gamma: bfloat16 [256], P('chan'), may hold values from 0.5 to 1.5
- up_weight: bfloat16 [256, 1024], P(None, 'chan'), may hold values from -0.375 to 0.375
- up_bias: bfloat16 [1024], P('chan'), may hold values from -3 to 3
- down_weight: bfloat16 [1024, 256], P('chan'), may hold values from -0.1875 to 0.1875
- layer_scale: bfloat16 [256], P('chan'), may hold values from 0.29882812 to 1
Outputs:
- input_grad: bfloat16 [64, 96, 96, 256], P('tiles', None, None, 'chan')
- depth_weight_grad: float32 [7, 7, 256], P(None, None, 'chan')
- gamma_grad: float32 [256], P('chan')
- up_weight_grad: float32 [256, 1024], P(None, 'chan')
- up_bias_grad: float32 [1024], P('chan')
- down_weight_grad: float32 [1024, 256], P('chan')
- layer_scale_grad: float32 [256], P('chan')
The draws below stay inside these ranges and needn't reach their ends.
Inputs may be any that keep to these rules, and one draw needn't show every extreme that they name: 1 on wet cells, 0 on land. `neighbours`: wet tiles are numbered in row order of a window of 24 x 4 tiles; entry d of tile t is the number of the wet tile beside t in direction d, or -1 where that tile is land or outside the window. Every listed neighbour is at most 5 numbers away from t, and some are exactly that far.
All inputs are finite; a program needn't handle non-finite values.
Results may differ from the reference program's by a relative error of at most 0.0095.
Values may be sent and summed in bfloat16 or wider, within the bound.
A program may use at most 320 MiB of HBM per device.

```python
import math
import jax
import jax.numpy as jnp
from jax import lax

C = 256
H = 1024
KERNEL = 7
S = 96
TILE_COLS = 4
TILES = 64
TILE_ROWS = 24


def draw_wet(key, part):
    key = jax.random.fold_in(key, 11)
    key_open, key_base, key_jitter = jax.random.split(key, 3)
    open_tile = jax.random.randint(key_open, (TILES,), 0, 4) == 0
    open_tile = open_tile.at[0].set(True)
    coast_base = jax.random.randint(key_base, (TILES,), S // 10, S // 2)
    jitter = jax.random.randint(key_jitter, (TILES, S), 0, S // 8 + 1)
    height = jnp.where(open_tile[:, None], S, coast_base[:, None] + jitter)
    row_index = jnp.arange(S, dtype=jnp.int32)
    return (row_index[None, :, None] < height[:, None, :]).astype(jnp.int32)


def draw_neighbours(key, part):
    key = jax.random.fold_in(key, 23)
    remaining = (TILE_ROWS - 2) * TILE_COLS
    shuffled = jax.random.permutation(key, remaining)
    chosen = jnp.zeros((remaining,), jnp.int32).at[shuffled[:TILES - 2 * TILE_COLS]].set(1)
    occupied = jnp.concatenate([jnp.ones((2 * TILE_COLS,), jnp.int32), chosen])
    ranks = jnp.cumsum(occupied) - 1
    number_grid = jnp.where(occupied == 1, ranks, -1).reshape(TILE_ROWS, TILE_COLS).astype(jnp.int32)
    framed = jnp.pad(number_grid, 1, constant_values=-1)
    steps_list = [(-1, 0), (1, 0), (0, -1), (0, 1), (-1, -1), (-1, 1), (1, -1), (1, 1)]
    beside = jnp.stack([framed[1 + row_step:1 + row_step + TILE_ROWS, 1 + col_step:1 + col_step + TILE_COLS] for row_step, col_step in steps_list], -1)
    positions = jnp.nonzero(occupied, size=TILES)[0]
    return beside.reshape(TILE_ROWS * TILE_COLS, 8)[positions].astype(jnp.int32)


def levels(rng, dims, shards, smallest, high):
    level, own = 1.0, jax.random.fold_in(rng, 6)
    for position, blocks in shards:
        steps = jnp.exp(jax.random.uniform(jax.random.fold_in(own, position), (blocks,), jnp.float32, smallest / len(shards), high / len(shards)))
        level = level * jnp.repeat(steps, dims[position] // blocks).reshape([-1 if axis == position else 1 for axis in range(len(dims))])
    return level


def bell_draw(stream_key, extent, spread, most, cuts=(), kind=jnp.bfloat16):
    loudness = levels(stream_key, extent, cuts, -0.22, 0.18) if cuts else 1.0
    values = jax.random.normal(stream_key, extent, jnp.float32) * spread * loudness
    return jnp.minimum(jnp.maximum(values, -most), most).astype(kind)


def setup_inputs(seed: int = 0) -> dict:
    seeds = jax.random.split(jax.random.key(seed), 11)
    inputs = bell_draw(seeds[0], (TILES, S, S, C), 1.0, 6.0, ((0, 64), (3, 2)))
    cotangent = bell_draw(seeds[1], (TILES, S, S, C), 1.0, 6.0, ((0, 64), (3, 2)))
    wet = draw_wet(jax.random.fold_in(seeds[10], 71), 0)
    neighbours = draw_neighbours(jax.random.fold_in(seeds[10], 71), 0)
    depth_weight = bell_draw(seeds[4], (KERNEL, KERNEL, C), (KERNEL * KERNEL) ** -0.5, 0.875, ((2, 2),), jnp.float32)
    gamma = jnp.clip(0.5 + 1.0 * jax.random.uniform(seeds[5], (C,), jnp.float32) ** levels(seeds[5], (C,), ((0, 2),), -0.2, 0.2), 0.5, 1.5).astype(jnp.bfloat16)
    up_weight = bell_draw(seeds[6], (C, H), C ** -0.5, 0.375, ((1, 2),))
    up_bias = bell_draw(seeds[7], (H,), 0.5, 3.0, ((0, 2),))
    down_weight = bell_draw(seeds[8], (H, C), H ** -0.5, 0.1875, ((0, 2),))
    layer_scale = jnp.clip(0.29882812 + 0.7011719 * jax.random.uniform(seeds[9], (C,), jnp.float32) ** levels(seeds[9], (C,), ((0, 2),), -0.2, 0.2), 0.29882812, 1.0).astype(jnp.bfloat16)
    return {"inputs": inputs, "cotangent": cotangent, "wet": wet, "neighbours": neighbours, "depth_weight": depth_weight, "gamma": gamma, "up_weight": up_weight, "up_bias": up_bias, "down_weight": down_weight, "layer_scale": layer_scale}


root_half = 0.7071067811865476
density = 0.3989422804014327

def gelu_pieces(hidden):
    normal_cdf = 0.5 * (1.0 + lax.erf(hidden * root_half))
    activated = hidden * normal_cdf
    slope = normal_cdf + hidden * jnp.exp(-0.5 * hidden * hidden) * density
    return (activated, slope)

def mlp_backward(normed, wet_grad, up_weight, down_weight, up_bias, layer_scale, grad_scale):
    hidden = jnp.dot(normed, up_weight, preferred_element_type=jnp.float32) + up_bias.astype(jnp.float32)
    activated, slope = gelu_pieces(hidden)
    activated = activated.astype(jnp.bfloat16)
    branch = jnp.dot(activated, down_weight, preferred_element_type=jnp.float32)
    scale_part = grad_scale * lax.optimization_barrier(jnp.sum(wet_grad.astype(jnp.float32) * branch, 0))
    branch_grad = (wet_grad.astype(jnp.float32) * layer_scale.astype(jnp.float32)).astype(jnp.bfloat16)
    down_part = grad_scale * jnp.dot(activated.T, branch_grad, preferred_element_type=jnp.float32)
    hidden_grad = (jnp.dot(branch_grad, down_weight.T, preferred_element_type=jnp.float32) * slope).astype(jnp.bfloat16)
    bias_part = grad_scale * lax.optimization_barrier(jnp.sum(hidden_grad.astype(jnp.float32), 0))
    up_part = grad_scale * jnp.dot(normed.T, hidden_grad, preferred_element_type=jnp.float32)
    norm_grad = jnp.dot(hidden_grad, up_weight.T, preferred_element_type=jnp.float32)
    return (norm_grad, up_part, down_part, bias_part, scale_part)

def depth_forward(padded, weight):
    width = padded.shape[0] - KERNEL + 1
    total = jnp.zeros((width, width, padded.shape[2]), jnp.float32)
    for row_off in range(KERNEL):
        for col_off in range(KERNEL):
            total = total + padded[row_off:row_off + width, col_off:col_off + width].astype(jnp.float32) * weight[row_off, col_off]
    return total

def depth_backward(grad_padded, weight):
    width = grad_padded.shape[0] - KERNEL + 1
    total = jnp.zeros((width, width, grad_padded.shape[2]), jnp.float32)
    for row_off in range(KERNEL):
        for col_off in range(KERNEL):
            row_at = KERNEL - 1 - row_off
            col_at = KERNEL - 1 - col_off
            total = total + grad_padded[row_at:row_at + width, col_at:col_at + width].astype(jnp.float32) * weight[row_off, col_off]
    return total

def filter_gradient(conv_grad, padded):
    width = conv_grad.shape[0]
    grad_float = conv_grad.astype(jnp.float32)
    rows_out = []
    for row_off in range(KERNEL):
        entries = []
        for col_off in range(KERNEL):
            window = padded[row_off:row_off + width, col_off:col_off + width].astype(jnp.float32)
            entries.append(lax.optimization_barrier(jnp.sum(grad_float * window, (0, 1))))
        rows_out.append(jnp.stack(entries))
    return jnp.stack(rows_out)

def padded_tile(own, every_tile, tile_links):
    margin = KERNEL // 2

    def nearby(direction):
        index = jnp.maximum(tile_links[direction], 0).astype(jnp.int32)
        piece = lax.dynamic_index_in_dim(every_tile, index, 0, keepdims=False)
        return jnp.where(tile_links[direction] >= 0, piece, jnp.zeros_like(piece))
    north_side, south_side, west_side, east_side, north_west, north_east, south_west, south_east = [nearby(d) for d in range(8)]
    upper = jnp.concatenate([north_west[S - margin:, S - margin:], north_side[S - margin:, :], north_east[S - margin:, :margin]], 1)
    middle = jnp.concatenate([west_side[:, S - margin:], own, east_side[:, :margin]], 1)
    lower = jnp.concatenate([south_west[:margin, S - margin:], south_side[:margin, :], south_east[:margin, :margin]], 1)
    return jnp.concatenate([upper, middle, lower], 0)

def reference(inputs, cotangent, wet, neighbours, depth_weight, gamma, up_weight, up_bias, down_weight, layer_scale):
    grad_scale = 1.0 / (S * math.sqrt(TILES))
    wet_cells = wet.astype(jnp.bfloat16)[..., None]
    wet_input = inputs * wet_cells
    wet_grad = cotangent * wet_cells
    gamma_float = gamma.astype(jnp.float32)

    def first_pass(carry, index):
        padded = padded_tile(wet_input[index], wet_input, neighbours[index])
        filtered = depth_forward(padded, depth_weight)
        average = lax.optimization_barrier(jnp.mean(filtered, -1, keepdims=True))
        variance = lax.optimization_barrier(jnp.mean(filtered * filtered, -1, keepdims=True)) - average * average
        inv_spread = lax.rsqrt(variance + 1e-06)
        unit_norm = (filtered - average) * inv_spread
        normed = (unit_norm * gamma_float).astype(jnp.bfloat16)
        norm_grad, up_part, down_part, bias_part, scale_part = mlp_backward(normed.reshape(S * S, C), wet_grad[index].reshape(S * S, C), up_weight, down_weight, up_bias, layer_scale, grad_scale)
        norm_grad = norm_grad.reshape(S, S, C)
        gain_part = grad_scale * lax.optimization_barrier(jnp.sum(norm_grad * unit_norm, (0, 1)))
        scaled_grad = norm_grad * gamma_float
        conv_grad = (inv_spread * (scaled_grad - lax.optimization_barrier(jnp.mean(scaled_grad, -1, keepdims=True)) - unit_norm * lax.optimization_barrier(jnp.mean(scaled_grad * unit_norm, -1, keepdims=True)))).astype(jnp.bfloat16)
        up_total, down_total, bias_total, gain_total, scale_total = carry
        carry = (up_total + up_part, down_total + down_part, bias_total + bias_part, gain_total + gain_part, scale_total + scale_part)
        return (carry, conv_grad)
    start = (jnp.zeros((C, H), jnp.float32), jnp.zeros((H, C), jnp.float32), jnp.zeros((H,), jnp.float32), jnp.zeros((C,), jnp.float32), jnp.zeros((C,), jnp.float32))
    sums, conv_grads = lax.scan(first_pass, start, jnp.arange(TILES, dtype=jnp.int32))

    def second_pass(filter_total, index):
        padded = padded_tile(wet_input[index], wet_input, neighbours[index])
        grad_padded = padded_tile(conv_grads[index], conv_grads, neighbours[index])
        spread_back = depth_backward(grad_padded, depth_weight)
        filter_total = filter_total + filter_gradient(conv_grads[index], padded)
        input_tile = (wet_grad[index].astype(jnp.float32) + wet_cells[index].astype(jnp.float32) * spread_back).astype(jnp.bfloat16)
        return (filter_total, input_tile)
    filter_total, input_grad = lax.scan(second_pass, jnp.zeros((KERNEL, KERNEL, C), jnp.float32), jnp.arange(TILES, dtype=jnp.int32))
    up_total, down_total, bias_total, gain_total, scale_total = sums
    return (input_grad, grad_scale * filter_total, gain_total, up_total, bias_total, down_total, scale_total)
```

```python
import functools
import math

import jax
import jax.numpy as jnp
from jax import lax
from jax.experimental import pallas as pl
from jax.experimental.pallas import tpu as pltpu
from jax.sharding import PartitionSpec as P

KERNEL = 7
MARGIN = 3
LANES = 128
CHAN = 256
HIDDEN = 1024
HALF_HIDDEN = 512
BLOCK = 256
ROWS = 8
COLS = 2
MLP_ROWS = 8
REACH = 5
F32 = jnp.float32
BF16 = jnp.bfloat16
MESH = pl.DeviceIdType.MESH
density = 0.3989422804014327


def gelu_pieces(hidden):
    size = jnp.abs(hidden)
    denom = 1.0 + 0.2316419 * size
    inverse = pl.reciprocal(denom, approx=True)
    inverse = inverse * (2.0 - denom * inverse)
    bell = jnp.exp(-0.5 * hidden * hidden)
    poly = 0.5 * 1.061405429
    for factor in (-1.453152027, 1.421413741, -0.284496736, 0.254829592):
        poly = poly * inverse + 0.5 * factor
    tail = poly * inverse * bell
    normal_cdf = jnp.where(hidden >= 0.0, 1.0 - tail, tail)
    activated = hidden * normal_cdf
    slope = normal_cdf + hidden * bell * density
    return activated, slope


def nn(a, b):
    return lax.dot_general(a, b, (((1,), (0,)), ((), ())), preferred_element_type=F32)


def nt(a, b):
    return lax.dot_general(a, b, (((1,), (1,)), ((), ())), preferred_element_type=F32)


def kernel(
    side, shape4,
    links, x_ref, c_ref, mask_ref, depth_ref, gamma_ref, up_ref, bias_ref, down_ref, scale_ref,
    out_ref, mats_ref, small_ref,
    pf, pg, taps, taps_acc, strips, corners, rows_in, cols_in, corners_in,
    wu, wd, pars, pars_in,
    grad_own, grad_send, grad_in, y_own, y_send, y_in, conv_send, conv_in,
    sums, gamma_acc, bias_acc, ring_core, ring_a, ring_b, ring_y, total,
    small_a, small_peer, small_peer_in, small_core, small_x, small_z, small_y,
    halo_send, halo_recv, weight_sem, weight_recv, grad_sem, grad_recv, y_sem, y_recv, conv_sem, conv_recv,
    rs_send, rs_recv, ag_send, ag_recv, sm_send, sm_recv,
):
    n_yh, n_z, n_x, n_core = shape4
    tiles = n_yh * n_z * n_x * n_core
    half = side // 2
    width = side + 16
    cells = half * side
    steps = half // MLP_ROWS
    chunk = MLP_ROWS * side
    me = lax.axis_index("tiles")
    h = lax.axis_index("chan")
    other = 1 - h
    core = me % n_core
    at_x = (me // n_core) % n_x
    at_z = (me // (n_core * n_x)) % n_z
    at_yh = me // (n_core * n_x * n_z)
    q = 1.0 / (side * math.sqrt(tiles))

    def tile_at(yh, z, x, c):
        return ((yh * n_z + z) * n_x + x) * n_core + c

    def dev(tile, chan=None):
        return {"tiles": tile, "chan": h if chan is None else chan}

    def remote(src, dst, send, recv, device):
        return pltpu.make_async_remote_copy(
            src_ref=src, dst_ref=dst, send_sem=send, recv_sem=recv, device_id=device, device_id_type=MESH
        )

    first = core * at_z + (1 - core) * at_x
    second = core * at_x + (1 - core) * at_z

    def ring_tile(a, b):
        return tile_at(at_yh, core * a + (1 - core) * b, core * b + (1 - core) * a, core)

    peer = dev(me, other)
    core_peer = dev(tile_at(at_yh, at_z, at_x, 1 - core))
    halo = [(sign, d) for sign in (1, -1) for d in range(1, REACH + 1)]

    def halo_tile(sign, d):
        return (me + sign * d + tiles) % tiles

    a_peers = [(first + k) % n_x for k in range(1, n_x)]
    b_peers = [(second + k) % n_x for k in range(1, n_x)]
    y_peers = [(0, 1), (1, 0), (1, 1)]

    def y_dev(dy, dc):
        return dev(tile_at((at_yh + dy) % 2, at_z, at_x, core), (h + dc) % 2)

    barrier = pltpu.get_barrier_semaphore()
    targets = [dev(halo_tile(s, d)) for s, d in halo]
    targets += [core_peer]
    targets += [dev(ring_tile(a, second)) for a in a_peers]
    targets += [dev(ring_tile(first, b)) for b in b_peers]
    targets += [y_dev(dy, dc) for dy, dc in y_peers]
    for target in targets:
        pl.semaphore_signal(barrier, inc=1, device_id=target, device_id_type=MESH)
    pl.semaphore_wait(barrier, len(targets))

    pars[...] = jnp.zeros_like(pars)
    pars[0:1, :] = bias_ref[...].astype(F32)
    pars[1:2, 0:LANES] = gamma_ref[...].astype(F32)
    pars[2:3, 0:LANES] = scale_ref[...].astype(F32)
    weight_copies = [
        remote(pars, pars_in, weight_sem.at[0], weight_recv.at[0], peer),
        remote(up_ref, wu.at[h], weight_sem.at[1], weight_recv.at[1], peer),
        remote(down_ref, wd.at[h], weight_sem.at[2], weight_recv.at[2], peer),
    ]
    weight_arrivals = [
        remote(pars, pars_in, weight_sem.at[0], weight_recv.at[0], peer),
        remote(up_ref, wu.at[other], weight_sem.at[1], weight_recv.at[1], peer),
        remote(down_ref, wd.at[other], weight_sem.at[2], weight_recv.at[2], peer),
    ]
    for copy in weight_copies:
        copy.start()

    def fill_input(i, _):
        at = pl.multiple_of(i * side, side)
        to = pl.multiple_of((i + MARGIN) * width + 8, 8)
        pf[pl.ds(to, side), :] = (x_ref[pl.ds(at, side), :] * mask_ref[pl.ds(at, side), :]).astype(F32)
        return 0

    lax.fori_loop(0, side, fill_input, 0)

    def make_strips(padded):
        for side_at, row in enumerate((MARGIN, side)):
            for k in range(MARGIN):
                base = (row + k) * width + 8
                strips[side_at, k * side : (k + 1) * side, :] = padded[base : base + side, :].astype(BF16)
                near = base if side_at == 0 else base + side - 16
                corners[side_at, k * 16 : (k + 1) * 16, :] = padded[near : near + 16, :].astype(BF16)
        for side_at, col in enumerate((8, 8 + side - MARGIN)):
            for k in range(MARGIN):
                line = padded[pl.ds(MARGIN * width + col + k, side, stride=width), :]
                strips[2 + side_at, k * side : (k + 1) * side, :] = line.astype(BF16)

    def halo_copies(phase):
        copies = []
        for n, (sign, d) in enumerate(halo):
            device = dev(halo_tile(sign, d))
            way = 0 if sign > 0 else 1
            send = halo_send.at[phase, n]
            recv = halo_recv.at[phase, n]
            if d < REACH:
                copies.append(remote(strips.at[1 - way], rows_in.at[phase, way, d - 1], send, recv, device))
            else:
                copies.append(remote(corners.at[1 - way], corners_in.at[phase, way], send, recv, device))
        for way, sign in enumerate((1, -1)):
            device = dev(halo_tile(sign, 1))
            n = len(halo) + way
            copies.append(
                remote(strips.at[3 - way], cols_in.at[phase, way], halo_send.at[phase, n], halo_recv.at[phase, n], device)
            )
        return copies

    def match(direction, source):
        return jnp.logical_and(links[me, direction] == source, source >= 0).astype(F32)

    def fill_halo(padded, phase):
        for way, sign in enumerate((-1, 1)):
            straight, left, right, beside = ((0, 4, 5, 2), (1, 6, 7, 3))[way]
            row = 0 if way == 0 else side + MARGIN
            straight_hit = [match(straight, me + sign * d) for d in range(1, 5)]
            left_hit = [match(left, me + sign * d) for d in range(1, 6)]
            right_hit = [match(right, me + sign * d) for d in range(1, 6)]
            far_hit = left_hit[4] if way == 0 else right_hit[4]
            for k in range(MARGIN):
                base = (row + k) * width
                lines = [rows_in[phase, way, d, k * side : (k + 1) * side, :].astype(F32) for d in range(4)]
                far = corners_in[phase, way, k * 16 : (k + 1) * 16, :].astype(F32)
                middle = sum(hit * line for hit, line in zip(straight_hit, lines))
                west = sum(hit * line[side - 8 :] for hit, line in zip(left_hit[:4], lines))
                east = sum(hit * line[:8] for hit, line in zip(right_hit[:4], lines))
                if way == 0:
                    west = west + far_hit * far[8:]
                else:
                    east = east + far_hit * far[:8]
                padded[base : base + 8, :] = west
                padded[base + 8 : base + 8 + side, :] = middle
                padded[base + 8 + side : base + 16 + side, :] = east
            hit = match(beside, me + sign)
            col = 8 - MARGIN if way == 0 else 8 + side
            for k in range(MARGIN):
                line = cols_in[phase, way, k * side : (k + 1) * side, :].astype(F32)
                padded[pl.ds(MARGIN * width + col + k, side, stride=width), :] = line * hit

    make_strips(pf)
    forward_halo = halo_copies(0)
    for copy in forward_halo:
        copy.start()

    def grad_copy(k):
        at = pl.ds(pl.multiple_of(k * chunk, chunk), chunk)
        return remote(grad_send.at[at, :], grad_in.at[at, :], grad_sem.at[k], grad_recv.at[k], peer)

    def fill_grad(k, _):
        there = pl.ds(pl.multiple_of(other * cells + k * chunk, chunk), chunk)
        here = pl.ds(pl.multiple_of(h * cells + k * chunk, chunk), chunk)
        at = pl.ds(pl.multiple_of(k * chunk, chunk), chunk)
        grad_send[at, :] = c_ref[there, :] * mask_ref[there, :]
        grad_copy(k).start()
        grad_own[at, :] = c_ref[here, :] * mask_ref[here, :]
        return 0

    lax.fori_loop(0, steps, fill_grad, 0)

    for a in range(KERNEL):
        for b in range(KERNEL):
            n = (a * KERNEL + b) * 8
            taps[n : n + 8, :] = jnp.broadcast_to(depth_ref[a, b : b + 1, :], (8, LANES))

    for copy in forward_halo:
        copy.wait_recv()
    fill_halo(pf, 0)

    def conv_block(padded, row, col, flip):
        base = row * width + col + 8 - MARGIN
        acc = [[None] * COLS for _ in range(ROWS)]
        for b in range(KERNEL):
            weights = []
            for a in range(KERNEL):
                n = a * KERNEL + b
                n = (KERNEL * KERNEL - 1 - n if flip else n) * 8
                weights.append(taps[n : n + 8, :])
            for r in range(ROWS + KERNEL - 1):
                for v in range(COLS):
                    value = padded[pl.ds(base + (r * width + v * 8 + b), 8), :]
                    for a in range(KERNEL):
                        i = r - a
                        if 0 <= i < ROWS:
                            term = value * weights[a]
                            acc[i][v] = term if acc[i][v] is None else acc[i][v] + term
        return acc

    col_steps = side // (8 * COLS)

    def conv_rows(start, put):
        def one(c, _):
            col = pl.multiple_of(c * (8 * COLS), 8 * COLS)
            acc = conv_block(pf, start, col, False)
            for i in range(ROWS):
                put(i, col, jnp.concatenate(acc[i], 0))
            return 0

        lax.fori_loop(0, col_steps, one, 0)

    def y_copy(k):
        at = pl.ds(pl.multiple_of(k * chunk, chunk), chunk)
        return remote(y_send.at[at, :], y_in.at[at, :], y_sem.at[k], y_recv.at[k], peer)

    def conv_there(k, _):
        def put(i, col, value):
            at = pl.multiple_of((k * ROWS + i) * side + col, 8 * COLS)
            y_send[pl.ds(at, 8 * COLS), :] = value.astype(BF16)

        conv_rows(other * half + k * ROWS, put)
        y_copy(k).start()
        return 0

    lax.fori_loop(0, steps, conv_there, 0)

    def conv_here(k, _):
        def put(i, col, value):
            at = pl.multiple_of((k * ROWS + i) * side + col, 8 * COLS)
            y_own[pl.ds(at, 8 * COLS), :] = value.astype(BF16)

        conv_rows(h * half + k * ROWS, put)
        return 0

    lax.fori_loop(0, steps, conv_here, 0)

    for copy in weight_arrivals:
        copy.wait_recv()
    wu[h] = up_ref[...]
    wd[h] = down_ref[...]
    mine = h == 0

    def ordered(own, others):
        return jnp.where(mine, own, others), jnp.where(mine, others, own)

    def row_of(n):
        own, others = pars[n : n + 1, 0:LANES], pars_in[n : n + 1, 0:LANES]
        return jnp.concatenate(ordered(own, others), 1)

    gamma_row = row_of(1)
    scale_row = row_of(2)
    bias_rows = ordered(pars[0:1, :], pars_in[0:1, :])

    sums[...] = jnp.zeros_like(sums)
    gamma_acc[...] = jnp.zeros_like(gamma_acc)
    bias_acc[...] = jnp.zeros_like(bias_acc)

    def conv_copy(k):
        at = pl.ds(pl.multiple_of(k * chunk, chunk), chunk)
        return remote(conv_send.at[at, :], conv_in.at[at, :], conv_sem.at[k], conv_recv.at[k], peer)

    def mlp(k, _):
        at = pl.ds(pl.multiple_of(k * chunk, chunk), chunk)
        y_copy(k).wait_recv()
        grad_copy(k).wait_recv()
        low, high = ordered(y_own[at, :].astype(F32), y_in[at, :].astype(F32))
        y = jnp.concatenate((low, high), 1)
        centred = y - jnp.sum(y, 1, keepdims=True) * (1.0 / CHAN)
        spread = jnp.sum(centred * centred, 1, keepdims=True) * (1.0 / CHAN)
        inv_spread = lax.rsqrt(spread + 1e-06)
        unit = centred * inv_spread
        normed = (unit * gamma_row).astype(BF16)
        low, high = ordered(grad_own[at, :].astype(F32), grad_in[at, :].astype(F32))
        branch_grad = (jnp.concatenate((low, high), 1) * scale_row).astype(BF16)
        branch_t = branch_grad.T
        normed_t = normed.T
        norm_grad = jnp.zeros((chunk, CHAN), F32)
        for block in range(HIDDEN // BLOCK):
            slot, off = divmod(block * BLOCK, HALF_HIDDEN)
            w_up = wu[slot, :, off : off + BLOCK]
            w_down = wd[slot, off : off + BLOCK, :]
            cols = slice(block * BLOCK, (block + 1) * BLOCK)
            hidden = nn(normed, w_up) + bias_rows[slot][:, off : off + BLOCK]
            activated, slope = gelu_pieces(hidden)
            hidden_grad = (nt(branch_grad, w_down) * slope).astype(BF16)
            sums[1, :, cols] += nn(branch_t, activated.astype(BF16))
            sums[0, :, cols] += nn(normed_t, hidden_grad)
            bias_acc[:, cols] += jnp.sum(hidden_grad.astype(F32).reshape(chunk // 8, 8, BLOCK), 0)
            norm_grad = norm_grad + nt(hidden_grad, w_up)
        gamma_acc[...] += jnp.sum((norm_grad * unit).reshape(chunk // 8, 8, CHAN), 0)
        scaled = norm_grad * gamma_row
        mean = jnp.sum(scaled, 1, keepdims=True) * (1.0 / CHAN)
        tilt = jnp.sum(scaled * unit, 1, keepdims=True) * (1.0 / CHAN)
        conv_grad = (inv_spread * (scaled - mean - unit * tilt)).astype(BF16).astype(F32)
        own, away = ordered(conv_grad[:, :LANES], conv_grad[:, LANES:])
        conv_send[at, :] = away.astype(BF16)
        conv_copy(k).start()
        for i in range(MLP_ROWS):
            to = pl.multiple_of((MARGIN + h * half + k * MLP_ROWS + i) * width + 8, 8)
            pg[pl.ds(to, side), :] = own[i * side : (i + 1) * side]
        return 0

    lax.fori_loop(0, steps, mlp, 0)

    rs_core = remote(sums.at[1 - core], ring_core, rs_send.at[0], rs_recv.at[0], core_peer)
    rs_core.start()

    ident = lax.broadcasted_iota(jnp.int32, (CHAN, CHAN), 0) == lax.broadcasted_iota(jnp.int32, (CHAN, CHAN), 1)
    down_sums = sums[1]
    down_high = down_sums.astype(BF16)
    down_low = (down_sums - down_high.astype(F32)).astype(BF16)
    paired = jnp.zeros((CHAN, CHAN), F32)
    for slot in range(2):
        cols = slice(slot * HALF_HIDDEN, (slot + 1) * HALF_HIDDEN)
        paired = paired + nn(down_high[:, cols], wd[slot]) + nn(down_low[:, cols], wd[slot])
    scale_sum = jnp.sum(jnp.where(ident, paired, 0.0), 0, keepdims=True) / scale_row
    gamma_sum = jnp.sum(gamma_acc[...], 0, keepdims=True)
    bias_sum = jnp.sum(bias_acc[...], 0, keepdims=True)
    small_peer[...] = jnp.zeros_like(small_peer)
    small_a[...] = jnp.zeros_like(small_a)
    n_taps = KERNEL * KERNEL

    def put_small(ref, at, value, n):
        own, away = ordered(value[:, : n * LANES], value[:, n * LANES :])
        for i in range(n):
            ref[0][ref[1] + at + i : ref[1] + at + i + 1, :] = own[:, i * LANES : (i + 1) * LANES]
            small_peer[at + i : at + i + 1, :] = away[:, i * LANES : (i + 1) * LANES]

    place = (small_a, n_taps)
    put_small(place, 0, gamma_sum, 1)
    put_small(place, 1, scale_sum, 1)
    put_small(place, 2, bias_sum, 4)
    small_chan = remote(small_peer, small_peer_in, sm_send.at[0], sm_recv.at[0], peer)
    small_chan.start()

    def take_conv(k, _):
        conv_copy(k).wait_recv()
        for i in range(MLP_ROWS):
            at = pl.multiple_of((k * MLP_ROWS + i) * side, side)
            to = pl.multiple_of((MARGIN + other * half + k * MLP_ROWS + i) * width + 8, 8)
            pg[pl.ds(to, side), :] = conv_in[pl.ds(at, side), :].astype(F32)
        return 0

    lax.fori_loop(0, steps, take_conv, 0)
    for copy in forward_halo:
        copy.wait_send()
    make_strips(pg)
    backward_halo = halo_copies(1)
    for copy in backward_halo:
        copy.start()

    rs_core.wait_recv()
    sums[core] = sums[core] + ring_core[...]
    a_rows, b_rows, y_rows = CHAN // n_x, CHAN // n_x // n_z, CHAN // n_x // n_z // 2
    rs_a = []
    for k, a in enumerate(a_peers):
        piece = sums.at[core, pl.ds(pl.multiple_of(a * a_rows, a_rows), a_rows), :]
        rs_a.append(remote(piece, ring_a.at[k], rs_send.at[1 + k], rs_recv.at[1 + k], dev(ring_tile(a, second))))
    for copy in rs_a:
        copy.start()

    taps_acc[...] = jnp.zeros_like(taps_acc)

    def filter_block(n, _):
        row = (n // col_steps) * ROWS
        col = (n % col_steps) * (8 * COLS)
        inner = (row + MARGIN) * width + col + 8
        base = row * width + col + 8 - MARGIN
        grads = [
            [pg[pl.ds(pl.multiple_of(inner, 8) + (i * width + v * 8), 8), :] for v in range(COLS)] for i in range(ROWS)
        ]
        for b in range(KERNEL):
            acc = [None] * KERNEL
            for r in range(ROWS + KERNEL - 1):
                for v in range(COLS):
                    value = pf[pl.ds(base + (r * width + v * 8 + b), 8), :]
                    for a in range(KERNEL):
                        i = r - a
                        if 0 <= i < ROWS:
                            term = value * grads[i][v]
                            acc[a] = term if acc[a] is None else acc[a] + term
            for a in range(KERNEL):
                n = (a * KERNEL + b) * 8
                taps_acc[n : n + 8, :] += acc[a]
        return 0

    blocks = (side // ROWS) * col_steps
    lax.fori_loop(0, blocks // 2, filter_block, 0)

    for copy in rs_a:
        copy.wait_recv()
    a_at = pl.ds(pl.multiple_of(first * a_rows, a_rows), a_rows)
    sums[core, a_at, :] = sums[core, a_at, :] + sum(ring_a[k] for k in range(n_x - 1))
    rs_b = []
    for k, b in enumerate(b_peers):
        piece = sums.at[core, pl.ds(pl.multiple_of(first * a_rows + b * b_rows, b_rows), b_rows), :]
        rs_b.append(remote(piece, ring_b.at[k], rs_send.at[4 + k], rs_recv.at[4 + k], dev(ring_tile(first, b))))
    for copy in rs_b:
        copy.start()

    lax.fori_loop(blocks // 2, blocks, filter_block, 0)

    for copy in rs_b:
        copy.wait_recv()
    b_start = first * a_rows + second * b_rows
    b_at = pl.ds(pl.multiple_of(b_start, b_rows), b_rows)
    sums[core, b_at, :] = sums[core, b_at, :] + sum(ring_b[k] for k in range(n_x - 1))

    def y_piece(yh, chan):
        rows = pl.ds(pl.multiple_of(b_start + yh * y_rows, y_rows), y_rows)
        return (core, rows, pl.ds(pl.multiple_of(chan * HALF_HIDDEN, HALF_HIDDEN), HALF_HIDDEN))

    rs_y = []
    for k, (dy, dc) in enumerate(y_peers):
        piece = sums.at[y_piece((at_yh + dy) % 2, (h + dc) % 2)]
        rs_y.append(remote(piece, ring_y.at[k], rs_send.at[7 + k], rs_recv.at[7 + k], y_dev(dy, dc)))
    for copy in rs_y:
        copy.start()

    for n in range(n_taps):
        small_a[n : n + 1, :] = jnp.sum(taps_acc[n * 8 : n * 8 + 8, :], 0, keepdims=True)
    small_chan.wait_recv()
    for n in range(6):
        small_a[n_taps + n : n_taps + n + 1, :] += small_peer_in[n : n + 1, :]
    sm_core = remote(small_a, small_core, sm_send.at[1], sm_recv.at[1], core_peer)
    sm_core.start()

    for copy in backward_halo:
        copy.wait_recv()
    fill_halo(pg, 1)

    def input_rows(k, _):
        row = k * ROWS

        def one(c, _):
            col = pl.multiple_of(c * (8 * COLS), 8 * COLS)
            acc = conv_block(pg, row, col, True)
            for i in range(ROWS):
                at = pl.ds(pl.multiple_of((row + i) * side + col, 8 * COLS), 8 * COLS)
                wet = mask_ref[at, :].astype(F32)
                grad = c_ref[at, :].astype(F32)
                out_ref[at, :] = (wet * (grad + jnp.concatenate(acc[i], 0))).astype(BF16)
            return 0

        lax.fori_loop(0, col_steps, one, 0)
        return 0

    row_steps = side // ROWS
    marks = [row_steps * n // 4 for n in range(5)]
    lax.fori_loop(marks[0], marks[1], input_rows, 0)

    for copy in rs_y:
        copy.wait_recv()
    y_start = b_start + at_yh * y_rows
    y_at = pl.ds(pl.multiple_of(y_start, y_rows), y_rows)
    total[core, y_at, :] = sums[y_piece(at_yh, h)] + (ring_y[0] + ring_y[1] + ring_y[2])
    y_mate = dev(tile_at((at_yh + 1) % 2, at_z, at_x, core))
    ag_y = remote(total.at[core, y_at, :], total.at[core, y_at, :], ag_send.at[0], ag_recv.at[0], y_mate)
    ag_y.start()
    sm_core.wait_recv()

    def small_stage(ref, value, at, size, base, tile):
        ref[at] = value
        copies = []
        for k in range(1, size):
            there = (at + k) % size
            copies.append(
                remote(ref.at[at], ref.at[at], sm_send.at[base + k - 1], sm_recv.at[base + k - 1], dev(tile(there)))
            )
        for copy in copies:
            copy.start()
        return copies

    sm_x = small_stage(
        small_x, small_a[...] + small_core[...], at_x, n_x, 2, lambda x: tile_at(at_yh, at_z, x, core)
    )
    lax.fori_loop(marks[1], marks[2], input_rows, 0)

    ag_y.wait_recv()
    ag_b = []
    for k, b in enumerate(b_peers):
        block = total.at[core, b_at, :]
        ag_b.append(remote(block, block, ag_send.at[1 + k], ag_recv.at[1 + k], dev(ring_tile(first, b))))
    for copy in ag_b:
        copy.start()
    for copy in sm_x:
        copy.wait_recv()
    sm_z = small_stage(
        small_z, sum(small_x[k] for k in range(n_x)), at_z, n_z, 5, lambda z: tile_at(at_yh, z, at_x, core)
    )
    lax.fori_loop(marks[2], marks[3], input_rows, 0)

    for copy in ag_b:
        copy.wait_recv()
    ag_a = []
    for k, a in enumerate(a_peers):
        block = total.at[core, a_at, :]
        ag_a.append(remote(block, block, ag_send.at[4 + k], ag_recv.at[4 + k], dev(ring_tile(a, second))))
    for copy in ag_a:
        copy.start()
    for copy in sm_z:
        copy.wait_recv()
    sm_y = small_stage(
        small_y, sum(small_z[k] for k in range(n_z)), at_yh, 2, 8, lambda yh: tile_at(yh, at_z, at_x, core)
    )
    lax.fori_loop(marks[3], marks[4], input_rows, 0)

    for copy in ag_a:
        copy.wait_recv()
    ag_core = remote(total.at[core], total.at[core], ag_send.at[7], ag_recv.at[7], core_peer)
    ag_core.start()
    for copy in sm_y:
        copy.wait_recv()
    small_ref[...] = (small_y[0] + small_y[1]) * q
    mats_ref[core] = total[core] * q
    ag_core.wait_recv()
    mats_ref[1 - core] = total[1 - core] * q

    for copy in weight_copies + backward_halo + [rs_core, small_chan, sm_core, ag_y, ag_core]:
        copy.wait_send()
    for copy in rs_a + rs_b + rs_y + ag_a + ag_b + sm_x + sm_z + sm_y:
        copy.wait_send()

    def finish(k, _):
        grad_copy(k).wait_send()
        y_copy(k).wait_send()
        conv_copy(k).wait_send()
        return 0

    lax.fori_loop(0, steps, finish, 0)


SHAPES = {64: (2, 4, 4, 2), 16: (2, 2, 2, 2)}


def block_call(inputs, cotangent, mask, neighbours, depth_weight, gamma, up_weight, up_bias, down_weight, layer_scale):
    side = inputs.shape[1]
    half_chan = inputs.shape[3]
    flat = (side * side, half_chan)
    shape4 = SHAPES[lax.axis_size("tiles")]
    n_yh, n_z, n_x, n_core = shape4
    width = side + 16
    cells = side * side // 2
    steps = side // 2 // MLP_ROWS
    a_rows = CHAN // n_x
    vmem, smem = pltpu.VMEM, pl.BlockSpec(memory_space=pltpu.SMEM)
    whole = pl.BlockSpec(memory_space=pltpu.VMEM)
    dma = pltpu.SemaphoreType.DMA
    padded = vmem(((side + 2 * MARGIN) * width, LANES), F32)
    taps = vmem((KERNEL * KERNEL * 8, LANES), F32)
    piece = vmem((cells, LANES), BF16)
    small = vmem((64, LANES), F32)
    pars = vmem((8, HALF_HIDDEN), F32)
    scratch = [
        padded, padded, taps, taps,
        vmem((4, MARGIN * side, LANES), BF16),
        vmem((2, MARGIN * 16, LANES), BF16),
        vmem((2, 2, 4, MARGIN * side, LANES), BF16),
        vmem((2, 2, MARGIN * side, LANES), BF16),
        vmem((2, 2, MARGIN * 16, LANES), BF16),
        vmem((2, CHAN, HALF_HIDDEN), BF16),
        vmem((2, HALF_HIDDEN, CHAN), BF16),
        pars, pars,
        piece, piece, piece, piece, piece, piece, piece, piece,
        vmem((2, CHAN, HIDDEN), F32),
        vmem((8, CHAN), F32),
        vmem((8, HIDDEN), F32),
        vmem((CHAN, HIDDEN), F32),
        vmem((n_x - 1, a_rows, HIDDEN), F32),
        vmem((n_x - 1, a_rows // n_z, HIDDEN), F32),
        vmem((3, a_rows // n_z // 2, HALF_HIDDEN), F32),
        vmem((2, CHAN, HALF_HIDDEN), F32),
        small, vmem((8, LANES), F32), vmem((8, LANES), F32), small,
        vmem((n_x, 64, LANES), F32), vmem((n_z, 64, LANES), F32), vmem((2, 64, LANES), F32),
        dma((2, 12)), dma((2, 12)), dma((3,)), dma((3,)),
        dma((steps,)), dma((steps,)), dma((steps,)), dma((steps,)), dma((steps,)), dma((steps,)),
        dma((10,)), dma((10,)), dma((8,)), dma((8,)), dma((9,)), dma((9,)),
    ]
    return pl.pallas_call(
        functools.partial(kernel, side, shape4),
        out_shape=(
            jax.ShapeDtypeStruct(flat, BF16),
            jax.ShapeDtypeStruct((2, CHAN, HALF_HIDDEN), F32),
            jax.ShapeDtypeStruct((64, LANES), F32),
        ),
        in_specs=[smem] + [whole] * 9,
        out_specs=(whole, whole, whole),
        scratch_shapes=scratch,
        compiler_params=pltpu.CompilerParams(
            collective_id=0, has_side_effects=True, vmem_limit_bytes=60 * 1024 * 1024
        ),
    )(
        neighbours,
        inputs.reshape(flat),
        cotangent.reshape(flat),
        mask,
        depth_weight,
        gamma.reshape(1, half_chan),
        up_weight,
        up_bias.reshape(1, -1),
        down_weight,
        layer_scale.reshape(1, half_chan),
    )


def body(
    inputs,
    cotangent,
    wet,
    neighbours,
    depth_weight,
    gamma,
    up_weight,
    up_bias,
    down_weight,
    layer_scale,
):
    side = inputs.shape[1]
    mask = jnp.broadcast_to(wet[0].astype(BF16)[..., None], (side, side, LANES)).reshape(side * side, LANES)
    grad, mats, small = block_call(
        inputs, cotangent, mask, neighbours, depth_weight, gamma, up_weight, up_bias, down_weight, layer_scale
    )
    taps = KERNEL * KERNEL
    return (
        grad.reshape(inputs.shape),
        small[:taps].reshape(KERNEL, KERNEL, LANES),
        small[taps],
        mats[0],
        small[taps + 2 : taps + 6].reshape(-1),
        mats[1].T,
        small[taps + 1],
    )


def solution(mesh):
    return jax.shard_map(
        body,
        mesh=mesh,
        in_specs=(
            P("tiles", None, None, "chan"),
            P("tiles", None, None, "chan"),
            P("tiles", None, None),
            P(),
            P(None, None, "chan"),
            P("chan"),
            P(None, "chan"),
            P("chan"),
            P("chan", None),
            P("chan"),
        ),
        out_specs=(
            P("tiles", None, None, "chan"),
            P(None, None, "chan"),
            P("chan"),
            P(None, "chan"),
            P("chan"),
            P("chan", None),
            P("chan"),
        ),
        check_vma=False,
    )
```

```python
import functools
import math

import jax
import jax.numpy as jnp
from jax import lax
from jax.experimental import pallas as pl
from jax.experimental.pallas import tpu as pltpu
from jax.sharding import PartitionSpec as P

KERNEL = 7
MARGIN = 3
LANES = 128
CHAN = 256
HIDDEN = 1024
HALF_HIDDEN = 512
BLOCK = 256
ROWS = 8
COLS = 2
MLP_ROWS = 8
REACH = 5
F32 = jnp.float32
BF16 = jnp.bfloat16
MESH = pl.DeviceIdType.MESH
density = 0.3989422804014327


def gelu_pieces(hidden):
    size = jnp.abs(hidden)
    denom = 1.0 + 0.2316419 * size
    inverse = pl.reciprocal(denom, approx=True)
    inverse = inverse * (2.0 - denom * inverse)
    bell = jnp.exp(-0.5 * hidden * hidden)
    poly = 0.5 * 1.061405429
    for factor in (-1.453152027, 1.421413741, -0.284496736, 0.254829592):
        poly = poly * inverse + 0.5 * factor
    tail = poly * inverse * bell
    normal_cdf = jnp.where(hidden >= 0.0, 1.0 - tail, tail)
    activated = hidden * normal_cdf
    slope = normal_cdf + hidden * bell * density
    return activated, slope


def nn(a, b):
    return lax.dot_general(a, b, (((1,), (0,)), ((), ())), preferred_element_type=F32)


def nt(a, b):
    return lax.dot_general(a, b, (((1,), (1,)), ((), ())), preferred_element_type=F32)


def kernel(
    side, shape4,
    links, x_ref, c_ref, wet_ref, depth_ref, gamma_ref, up_ref, bias_ref, down_ref, scale_ref,
    out_ref, mats_ref, small_ref,
    pf, pg, taps, taps_acc, strips, corners, rows_in, cols_in, corners_in,
    wu, wd, pars, pars_in,
    mask_ref, wet_turned, grad_own, grad_send, grad_in, y_all, y_in, conv_send, conv_in,
    sums, gamma_acc, bias_acc, ring_core, ring_a, ring_b, ring_y, total,
    small_a, small_peer, small_peer_in, small_core, small_x, small_z, small_y,
    halo_send, halo_recv, weight_sem, weight_recv, grad_sem, grad_recv, y_sem, y_recv, conv_sem, conv_recv,
    rs_send, rs_recv, ag_send, ag_recv, sm_send, sm_recv,
):
    n_yh, n_z, n_x, n_core = shape4
    tiles = n_yh * n_z * n_x * n_core
    half = side // 2
    width = side + 16
    cells = half * side
    steps = half // MLP_ROWS
    chunk = MLP_ROWS * side
    me = lax.axis_index("tiles")
    h = lax.axis_index("chan")
    other = 1 - h
    core = me % n_core
    at_x = (me // n_core) % n_x
    at_z = (me // (n_core * n_x)) % n_z
    at_yh = me // (n_core * n_x * n_z)
    q = 1.0 / (side * math.sqrt(tiles))

    def tile_at(yh, z, x, c):
        return ((yh * n_z + z) * n_x + x) * n_core + c

    def dev(tile, chan=None):
        return {"tiles": tile, "chan": h if chan is None else chan}

    def remote(src, dst, send, recv, device):
        return pltpu.make_async_remote_copy(
            src_ref=src, dst_ref=dst, send_sem=send, recv_sem=recv, device_id=device, device_id_type=MESH
        )

    first = core * at_z + (1 - core) * at_x
    second = core * at_x + (1 - core) * at_z

    def ring_tile(a, b):
        return tile_at(at_yh, core * a + (1 - core) * b, core * b + (1 - core) * a, core)

    peer = dev(me, other)
    core_peer = dev(tile_at(at_yh, at_z, at_x, 1 - core))
    halo = [(sign, d) for sign in (1, -1) for d in range(1, REACH + 1)]

    def halo_tile(sign, d):
        return (me + sign * d + tiles) % tiles

    a_peers = [(first + k) % n_x for k in range(1, n_x)]
    b_peers = [(second + k) % n_x for k in range(1, n_x)]
    y_peers = [(0, 1), (1, 0), (1, 1)]

    def y_dev(dy, dc):
        return dev(tile_at((at_yh + dy) % 2, at_z, at_x, core), (h + dc) % 2)

    barrier = pltpu.get_barrier_semaphore()
    targets = [dev(halo_tile(s, d)) for s, d in halo]
    targets += [core_peer]
    targets += [dev(ring_tile(a, second)) for a in a_peers]
    targets += [dev(ring_tile(first, b)) for b in b_peers]
    targets += [y_dev(dy, dc) for dy, dc in y_peers]
    for target in targets:
        pl.semaphore_signal(barrier, inc=1, device_id=target, device_id_type=MESH)
    pl.semaphore_wait(barrier, len(targets))

    pars[...] = jnp.zeros_like(pars)
    pars[0:1, :] = bias_ref[...].astype(F32)
    pars[1:2, 0:LANES] = gamma_ref[...].astype(F32)
    pars[2:3, 0:LANES] = scale_ref[...].astype(F32)
    diagonal = y_dev(1, 1)
    up_part, down_part = CHAN // 4, HALF_HIDDEN // 4

    def part(ref, size, at, count=1):
        return ref.at[pl.ds(pl.multiple_of(at * size, size), count * size), :]

    def weight_copy(n, device, quarter, slot):
        up = remote(
            part(up_ref, up_part, quarter), part(wu.at[slot], up_part, quarter),
            weight_sem.at[n], weight_recv.at[n], device,
        )
        down = remote(
            part(down_ref, down_part, quarter), part(wd.at[slot], down_part, quarter),
            weight_sem.at[n + 1], weight_recv.at[n + 1], device,
        )
        return [up, down]

    pars_copy = remote(pars, pars_in, weight_sem.at[0], weight_recv.at[0], peer)
    weight_copies = weight_copy(1, peer, 2 * core, h) + weight_copy(3, diagonal, 2 * core + 1, h)
    weight_arrivals = weight_copy(1, peer, 2 * core, other) + weight_copy(3, diagonal, 2 * core + 1, other)

    def weight_forward(half_at):
        return [
            remote(
                part(wu.at[other], up_part, 2 * half_at, 2), part(wu.at[other], up_part, 2 * half_at, 2),
                weight_sem.at[5], weight_recv.at[5], core_peer,
            ),
            remote(
                part(wd.at[other], down_part, 2 * half_at, 2), part(wd.at[other], down_part, 2 * half_at, 2),
                weight_sem.at[6], weight_recv.at[6], core_peer,
            ),
        ]

    pars_copy.start()
    for copy in weight_copies:
        copy.start()

    wet_turned[...] = jnp.zeros_like(wet_turned)
    wet_turned[0:side, 0:side] = wet_ref[...].astype(F32)
    wet_turned[...] = wet_turned[...].T

    def fill_input(g, _):
        columns = pltpu.roll(wet_turned[0:side, :], (LANES - g * ROWS) % LANES, 1)
        for t in range(ROWS):
            i = g * ROWS + t
            at = pl.ds(pl.multiple_of(i * side, side), side)
            to = pl.multiple_of((i + MARGIN) * width + 8, 8)
            wet = jnp.broadcast_to(columns[:, t : t + 1], (side, LANES))
            mask_ref[at, :] = wet.astype(BF16)
            pf[pl.ds(to, side), :] = x_ref[at, :].astype(F32) * wet
        return 0

    lax.fori_loop(0, side // ROWS, fill_input, 0)

    def make_strips(padded):
        for side_at, row in enumerate((MARGIN, side)):
            for k in range(MARGIN):
                base = (row + k) * width + 8
                strips[side_at, k * side : (k + 1) * side, :] = padded[base : base + side, :].astype(BF16)
                near = base if side_at == 0 else base + side - 16
                corners[side_at, k * 16 : (k + 1) * 16, :] = padded[near : near + 16, :].astype(BF16)
        for side_at, col in enumerate((8, 8 + side - MARGIN)):
            for k in range(MARGIN):
                line = padded[pl.ds(MARGIN * width + col + k, side, stride=width), :]
                strips[2 + side_at, k * side : (k + 1) * side, :] = line.astype(BF16)

    def halo_copies(phase):
        copies = []
        for n, (sign, d) in enumerate(halo):
            device = dev(halo_tile(sign, d))
            way = 0 if sign > 0 else 1
            send = halo_send.at[phase, n]
            recv = halo_recv.at[phase, n]
            if d < REACH:
                copies.append(remote(strips.at[1 - way], rows_in.at[phase, way, d - 1], send, recv, device))
            else:
                copies.append(remote(corners.at[1 - way], corners_in.at[phase, way], send, recv, device))
        for way, sign in enumerate((1, -1)):
            device = dev(halo_tile(sign, 1))
            n = len(halo) + way
            copies.append(
                remote(strips.at[3 - way], cols_in.at[phase, way], halo_send.at[phase, n], halo_recv.at[phase, n], device)
            )
        return copies

    def match(direction, source):
        link = links[pl.ds(me, 1), direction : direction + 1]
        return jnp.where(jnp.logical_and(link == source, link >= 0), 1.0, 0.0)

    def fill_halo(padded, phase):
        for way, sign in enumerate((-1, 1)):
            straight, left, right, beside = ((0, 4, 5, 2), (1, 6, 7, 3))[way]
            row = 0 if way == 0 else side + MARGIN
            straight_hit = [match(straight, me + sign * d) for d in range(1, 5)]
            left_hit = [match(left, me + sign * d) for d in range(1, 6)]
            right_hit = [match(right, me + sign * d) for d in range(1, 6)]
            far_hit = left_hit[4] if way == 0 else right_hit[4]
            for k in range(MARGIN):
                base = (row + k) * width
                lines = [rows_in[phase, way, d, k * side : (k + 1) * side, :].astype(F32) for d in range(4)]
                far = corners_in[phase, way, k * 16 : (k + 1) * 16, :].astype(F32)
                middle = sum(hit * line for hit, line in zip(straight_hit, lines))
                west = sum(hit * line[side - 8 :] for hit, line in zip(left_hit[:4], lines))
                east = sum(hit * line[:8] for hit, line in zip(right_hit[:4], lines))
                if way == 0:
                    west = west + far_hit * far[8:]
                else:
                    east = east + far_hit * far[:8]
                padded[base : base + 8, :] = west
                padded[base + 8 : base + 8 + side, :] = middle
                padded[base + 8 + side : base + 16 + side, :] = east
            hit = match(beside, me + sign)
            col = 8 - MARGIN if way == 0 else 8 + side
            for k in range(MARGIN):
                line = cols_in[phase, way, k * side : (k + 1) * side, :].astype(F32)
                padded[pl.ds(MARGIN * width + col + k, side, stride=width), :] = line * hit

    make_strips(pf)
    forward_halo = halo_copies(0)
    for copy in forward_halo:
        copy.start()

    def grad_copy(k):
        at = pl.ds(pl.multiple_of(k * chunk, chunk), chunk)
        return remote(grad_send.at[at, :], grad_in.at[at, :], grad_sem.at[k], grad_recv.at[k], peer)

    early = (steps + 1) // 2

    def fill_grad(k, _):
        there = pl.ds(pl.multiple_of(other * cells + k * chunk, chunk), chunk)
        here = pl.ds(pl.multiple_of(h * cells + k * chunk, chunk), chunk)
        at = pl.ds(pl.multiple_of(k * chunk, chunk), chunk)
        grad_send[at, :] = c_ref[there, :] * mask_ref[there, :]

        @pl.when(k < early)
        def _():
            grad_copy(k).start()

        grad_own[at, :] = c_ref[here, :] * mask_ref[here, :]
        return 0

    lax.fori_loop(0, steps, fill_grad, 0)

    for a in range(KERNEL):
        for b in range(KERNEL):
            n = (a * KERNEL + b) * 8
            taps[n : n + 8, :] = jnp.broadcast_to(depth_ref[a, b : b + 1, :], (8, LANES))

    for copy in weight_arrivals:
        copy.wait_recv()
    forwards = weight_forward(core)
    for copy in forwards:
        copy.start()

    def conv_block(padded, row, col, flip):
        base = row * width + col + 8 - MARGIN
        acc = [[None] * COLS for _ in range(ROWS)]
        for b in range(KERNEL):
            weights = []
            for a in range(KERNEL):
                n = a * KERNEL + b
                n = (KERNEL * KERNEL - 1 - n if flip else n) * 8
                weights.append(taps[n : n + 8, :])
            for r in range(ROWS + KERNEL - 1):
                for v in range(COLS):
                    value = padded[pl.ds(base + (r * width + v * 8 + b), 8), :]
                    for a in range(KERNEL):
                        i = r - a
                        if 0 <= i < ROWS:
                            term = value * weights[a]
                            acc[i][v] = term if acc[i][v] is None else acc[i][v] + term
        return acc

    col_steps = side // (8 * COLS)

    row_steps = side // ROWS
    half_steps = row_steps // 2

    def filter_forward(k, c):
        col = pl.multiple_of(c * (8 * COLS), 8 * COLS)
        acc = conv_block(pf, k * ROWS, col, False)
        for i in range(ROWS):
            at = pl.multiple_of((k * ROWS + i) * side + col, 8 * COLS)
            y_all[pl.ds(at, 8 * COLS), :] = jnp.concatenate(acc[i], 0).astype(BF16)

    def conv_inner(n, _):
        filter_forward(1 + n // (col_steps - 2), 1 + n % (col_steps - 2))
        return 0

    lax.fori_loop(0, (row_steps - 2) * (col_steps - 2), conv_inner, 0)
    for copy in forward_halo:
        copy.wait_recv()
    fill_halo(pf, 0)

    def y_copy(k):
        there = pl.ds(pl.multiple_of(other * cells + k * chunk, chunk), chunk)
        at = pl.ds(pl.multiple_of(k * chunk, chunk), chunk)
        return remote(y_all.at[there, :], y_in.at[at, :], y_sem.at[k], y_recv.at[k], peer)

    def conv_outer(n, _):
        away = n < half_steps
        k = jnp.where(away, other * half_steps + n, h * half_steps + n - half_steps)
        edge = jnp.logical_or(k == 0, k == row_steps - 1)

        def one(c, _):
            filter_forward(k, jnp.where(edge, c, c * (col_steps - 1)))
            return 0

        lax.fori_loop(0, jnp.where(edge, col_steps, 2), one, 0)

        @pl.when(away)
        def _():
            y_copy(n).start()

        @pl.when(n + early < steps)
        def _():
            grad_copy(n + early).start()

        return 0

    lax.fori_loop(0, row_steps, conv_outer, 0)

    pars_copy.wait_recv()
    for copy in weight_forward(1 - core):
        copy.wait_recv()
    wu[h] = up_ref[...]
    wd[h] = down_ref[...]
    mine = h == 0

    def ordered(own, others):
        return jnp.where(mine, own, others), jnp.where(mine, others, own)

    def row_of(n):
        own, others = pars[n : n + 1, 0:LANES], pars_in[n : n + 1, 0:LANES]
        return jnp.concatenate(ordered(own, others), 1)

    gamma_row = row_of(1)
    scale_row = row_of(2)
    bias_rows = ordered(pars[0:1, :], pars_in[0:1, :])

    sums[...] = jnp.zeros_like(sums)
    gamma_acc[...] = jnp.zeros_like(gamma_acc)
    bias_acc[...] = jnp.zeros_like(bias_acc)

    def conv_copy(k):
        at = pl.ds(pl.multiple_of(k * chunk, chunk), chunk)
        return remote(conv_send.at[at, :], conv_in.at[at, :], conv_sem.at[k], conv_recv.at[k], peer)

    def mlp(k, _):
        at = pl.ds(pl.multiple_of(k * chunk, chunk), chunk)
        y_copy(k).wait_recv()
        grad_copy(k).wait_recv()
        low, high = ordered(y_all[pl.ds(pl.multiple_of(h * cells + k * chunk, chunk), chunk), :].astype(F32), y_in[at, :].astype(F32))
        y = jnp.concatenate((low, high), 1)
        centred = y - jnp.sum(y, 1, keepdims=True) * (1.0 / CHAN)
        spread = jnp.sum(centred * centred, 1, keepdims=True) * (1.0 / CHAN)
        inv_spread = lax.rsqrt(spread + 1e-06)
        unit = centred * inv_spread
        normed = (unit * gamma_row).astype(BF16)
        low, high = ordered(grad_own[at, :].astype(F32), grad_in[at, :].astype(F32))
        branch_grad = (jnp.concatenate((low, high), 1) * scale_row).astype(BF16)
        branch_t = branch_grad.T
        normed_t = normed.T
        norm_grad = jnp.zeros((chunk, CHAN), F32)
        for block in range(HIDDEN // BLOCK):
            slot, off = divmod(block * BLOCK, HALF_HIDDEN)
            w_up = wu[slot, :, off : off + BLOCK]
            w_down = wd[slot, off : off + BLOCK, :]
            cols = slice(block * BLOCK, (block + 1) * BLOCK)
            hidden = nn(normed, w_up) + bias_rows[slot][:, off : off + BLOCK]
            activated, slope = gelu_pieces(hidden)
            hidden_grad = (nt(branch_grad, w_down) * slope).astype(BF16)
            sums[1, :, cols] += nn(branch_t, activated.astype(BF16))
            sums[0, :, cols] += nn(normed_t, hidden_grad)
            bias_acc[:, cols] += jnp.sum(hidden_grad.astype(F32).reshape(chunk // 8, 8, BLOCK), 0)
            norm_grad = norm_grad + nt(hidden_grad, w_up)
        gamma_acc[...] += jnp.sum((norm_grad * unit).reshape(chunk // 8, 8, CHAN), 0)
        scaled = norm_grad * gamma_row
        mean = jnp.sum(scaled, 1, keepdims=True) * (1.0 / CHAN)
        tilt = jnp.sum(scaled * unit, 1, keepdims=True) * (1.0 / CHAN)
        conv_grad = (inv_spread * (scaled - mean - unit * tilt)).astype(BF16).astype(F32)
        own, away = ordered(conv_grad[:, :LANES], conv_grad[:, LANES:])
        conv_send[at, :] = away.astype(BF16)
        conv_copy(k).start()
        for i in range(MLP_ROWS):
            to = pl.multiple_of((MARGIN + h * half + k * MLP_ROWS + i) * width + 8, 8)
            pg[pl.ds(to, side), :] = own[i * side : (i + 1) * side]
        return 0

    lax.fori_loop(0, steps, mlp, 0)

    rs_core = remote(sums.at[1 - core], ring_core, rs_send.at[0], rs_recv.at[0], core_peer)
    rs_core.start()

    ident = lax.broadcasted_iota(jnp.int32, (CHAN, CHAN), 0) == lax.broadcasted_iota(jnp.int32, (CHAN, CHAN), 1)
    down_sums = sums[1]
    down_high = down_sums.astype(BF16)
    down_low = (down_sums - down_high.astype(F32)).astype(BF16)
    paired = jnp.zeros((CHAN, CHAN), F32)
    for slot in range(2):
        cols = slice(slot * HALF_HIDDEN, (slot + 1) * HALF_HIDDEN)
        paired = paired + nn(down_high[:, cols], wd[slot]) + nn(down_low[:, cols], wd[slot])
    scale_sum = jnp.sum(jnp.where(ident, paired, 0.0), 0, keepdims=True) / scale_row
    gamma_sum = jnp.sum(gamma_acc[...], 0, keepdims=True)
    bias_sum = jnp.sum(bias_acc[...], 0, keepdims=True)
    small_peer[...] = jnp.zeros_like(small_peer)
    small_a[...] = jnp.zeros_like(small_a)
    n_taps = KERNEL * KERNEL

    def put_small(ref, at, value, n):
        own, away = ordered(value[:, : n * LANES], value[:, n * LANES :])
        for i in range(n):
            ref[0][ref[1] + at + i : ref[1] + at + i + 1, :] = own[:, i * LANES : (i + 1) * LANES]
            small_peer[at + i : at + i + 1, :] = away[:, i * LANES : (i + 1) * LANES]

    place = (small_a, n_taps)
    put_small(place, 0, gamma_sum, 1)
    put_small(place, 1, scale_sum, 1)
    put_small(place, 2, bias_sum, 4)
    small_chan = remote(small_peer, small_peer_in, sm_send.at[0], sm_recv.at[0], peer)
    small_chan.start()

    taps_acc[...] = jnp.zeros_like(taps_acc)

    def filter_block(n, _):
        line = n // col_steps
        row = ((line + h * half_steps) % row_steps) * ROWS
        col = (n % col_steps) * (8 * COLS)
        inner = (row + MARGIN) * width + col + 8
        base = row * width + col + 8 - MARGIN
        grads = [
            [pg[pl.ds(pl.multiple_of(inner, 8) + (i * width + v * 8), 8), :] for v in range(COLS)] for i in range(ROWS)
        ]
        for b in range(KERNEL):
            acc = [None] * KERNEL
            for r in range(ROWS + KERNEL - 1):
                for v in range(COLS):
                    value = pf[pl.ds(base + (r * width + v * 8 + b), 8), :]
                    for a in range(KERNEL):
                        i = r - a
                        if 0 <= i < ROWS:
                            term = value * grads[i][v]
                            acc[a] = term if acc[a] is None else acc[a] + term
            for a in range(KERNEL):
                n = (a * KERNEL + b) * 8
                taps_acc[n : n + 8, :] += acc[a]
        return 0

    blocks = row_steps * col_steps
    cuts = [blocks * n // 6 for n in range(7)]
    lax.fori_loop(cuts[0], cuts[1], filter_block, 0)

    rs_core.wait_recv()
    sums[core] = sums[core] + ring_core[...]
    a_rows, b_rows, y_rows = CHAN // n_x, CHAN // n_x // n_z, CHAN // n_x // n_z // 2
    rs_a = []
    for k, a in enumerate(a_peers):
        piece = sums.at[core, pl.ds(pl.multiple_of(a * a_rows, a_rows), a_rows), :]
        rs_a.append(remote(piece, ring_a.at[k], rs_send.at[1 + k], rs_recv.at[1 + k], dev(ring_tile(a, second))))
    for copy in rs_a:
        copy.start()

    lax.fori_loop(cuts[1], cuts[2], filter_block, 0)

    def take_conv(k, _):
        conv_copy(k).wait_recv()
        for i in range(MLP_ROWS):
            at = pl.multiple_of((k * MLP_ROWS + i) * side, side)
            to = pl.multiple_of((MARGIN + other * half + k * MLP_ROWS + i) * width + 8, 8)
            pg[pl.ds(to, side), :] = conv_in[pl.ds(at, side), :].astype(F32)
        return 0

    lax.fori_loop(0, steps, take_conv, 0)
    for copy in forward_halo:
        copy.wait_send()
    make_strips(pg)
    backward_halo = halo_copies(1)
    for copy in backward_halo:
        copy.start()

    for copy in rs_a:
        copy.wait_recv()
    a_at = pl.ds(pl.multiple_of(first * a_rows, a_rows), a_rows)
    sums[core, a_at, :] = sums[core, a_at, :] + sum(ring_a[k] for k in range(n_x - 1))
    rs_b = []
    for k, b in enumerate(b_peers):
        piece = sums.at[core, pl.ds(pl.multiple_of(first * a_rows + b * b_rows, b_rows), b_rows), :]
        rs_b.append(remote(piece, ring_b.at[k], rs_send.at[4 + k], rs_recv.at[4 + k], dev(ring_tile(first, b))))
    for copy in rs_b:
        copy.start()

    lax.fori_loop(cuts[2], cuts[3], filter_block, 0)

    for copy in rs_b:
        copy.wait_recv()
    b_start = first * a_rows + second * b_rows
    b_at = pl.ds(pl.multiple_of(b_start, b_rows), b_rows)
    sums[core, b_at, :] = sums[core, b_at, :] + sum(ring_b[k] for k in range(n_x - 1))

    def y_piece(yh, chan):
        rows = pl.ds(pl.multiple_of(b_start + yh * y_rows, y_rows), y_rows)
        return (core, rows, pl.ds(pl.multiple_of(chan * HALF_HIDDEN, HALF_HIDDEN), HALF_HIDDEN))

    rs_y = []
    for k, (dy, dc) in enumerate(y_peers):
        piece = sums.at[y_piece((at_yh + dy) % 2, (h + dc) % 2)]
        rs_y.append(remote(piece, ring_y.at[k], rs_send.at[7 + k], rs_recv.at[7 + k], y_dev(dy, dc)))
    for copy in rs_y:
        copy.start()

    lax.fori_loop(cuts[3], cuts[4], filter_block, 0)

    for copy in rs_y:
        copy.wait_recv()
    y_start = b_start + at_yh * y_rows
    y_at = pl.ds(pl.multiple_of(y_start, y_rows), y_rows)
    total[core, y_at, :] = sums[y_piece(at_yh, h)] + (ring_y[0] + ring_y[1] + ring_y[2])
    y_mate = dev(tile_at((at_yh + 1) % 2, at_z, at_x, core))
    ag_y = remote(total.at[core, y_at, :], total.at[core, y_at, :], ag_send.at[0], ag_recv.at[0], y_mate)
    ag_y.start()

    lax.fori_loop(cuts[4], cuts[5], filter_block, 0)

    ag_y.wait_recv()
    ag_b = []
    for k, b in enumerate(b_peers):
        block = total.at[core, b_at, :]
        ag_b.append(remote(block, block, ag_send.at[1 + k], ag_recv.at[1 + k], dev(ring_tile(first, b))))
    for copy in ag_b:
        copy.start()

    lax.fori_loop(cuts[5], cuts[6], filter_block, 0)

    for n in range(n_taps):
        small_a[n : n + 1, :] = jnp.sum(taps_acc[n * 8 : n * 8 + 8, :], 0, keepdims=True)
    small_chan.wait_recv()
    for n in range(6):
        small_a[n_taps + n : n_taps + n + 1, :] += small_peer_in[n : n + 1, :]
    sm_core = remote(small_a, small_core, sm_send.at[1], sm_recv.at[1], core_peer)
    sm_core.start()

    for copy in backward_halo:
        copy.wait_recv()
    fill_halo(pg, 1)

    def input_rows(k, _):
        row = k * ROWS

        def one(c, _):
            col = pl.multiple_of(c * (8 * COLS), 8 * COLS)
            acc = conv_block(pg, row, col, True)
            for i in range(ROWS):
                at = pl.ds(pl.multiple_of((row + i) * side + col, 8 * COLS), 8 * COLS)
                wet = mask_ref[at, :].astype(F32)
                grad = c_ref[at, :].astype(F32)
                out_ref[at, :] = (wet * (grad + jnp.concatenate(acc[i], 0))).astype(BF16)
            return 0

        lax.fori_loop(0, col_steps, one, 0)
        return 0

    marks = [row_steps * n // 4 for n in range(5)]
    lax.fori_loop(marks[0], marks[1], input_rows, 0)

    for copy in ag_b:
        copy.wait_recv()
    ag_a = []
    for k, a in enumerate(a_peers):
        block = total.at[core, a_at, :]
        ag_a.append(remote(block, block, ag_send.at[4 + k], ag_recv.at[4 + k], dev(ring_tile(a, second))))
    for copy in ag_a:
        copy.start()

    sm_core.wait_recv()

    def small_stage(ref, value, at, size, base, tile):
        ref[at] = value
        copies = []
        for k in range(1, size):
            there = (at + k) % size
            copies.append(
                remote(ref.at[at], ref.at[at], sm_send.at[base + k - 1], sm_recv.at[base + k - 1], dev(tile(there)))
            )
        for copy in copies:
            copy.start()
        return copies

    sm_x = small_stage(
        small_x, small_a[...] + small_core[...], at_x, n_x, 2, lambda x: tile_at(at_yh, at_z, x, core)
    )
    lax.fori_loop(marks[1], marks[2], input_rows, 0)

    for copy in ag_a:
        copy.wait_recv()
    ag_core = remote(total.at[core], total.at[core], ag_send.at[7], ag_recv.at[7], core_peer)
    ag_core.start()

    for copy in sm_x:
        copy.wait_recv()
    sm_z = small_stage(
        small_z, sum(small_x[k] for k in range(n_x)), at_z, n_z, 5, lambda z: tile_at(at_yh, z, at_x, core)
    )
    lax.fori_loop(marks[2], marks[3], input_rows, 0)

    for copy in sm_z:
        copy.wait_recv()
    sm_y = small_stage(
        small_y, sum(small_z[k] for k in range(n_z)), at_yh, 2, 8, lambda yh: tile_at(yh, at_z, at_x, core)
    )
    mats_ref[core] = total[core] * q
    ag_core.wait_recv()
    mats_ref[1 - core] = total[1 - core] * q
    lax.fori_loop(marks[3], marks[4], input_rows, 0)
    for copy in sm_y:
        copy.wait_recv()
    small_ref[...] = (small_y[0] + small_y[1]) * q

    for copy in weight_copies + forwards + backward_halo + [pars_copy, rs_core, small_chan, sm_core, ag_y, ag_core]:
        copy.wait_send()
    for copy in rs_a + rs_b + rs_y + ag_a + ag_b + sm_x + sm_z + sm_y:
        copy.wait_send()

    def finish(k, _):
        grad_copy(k).wait_send()
        y_copy(k).wait_send()
        conv_copy(k).wait_send()
        return 0

    lax.fori_loop(0, steps, finish, 0)


SHAPES = {64: (2, 4, 4, 2), 16: (2, 2, 2, 2)}


def block_call(inputs, cotangent, wet, neighbours, depth_weight, gamma, up_weight, up_bias, down_weight, layer_scale):
    side = inputs.shape[1]
    half_chan = inputs.shape[3]
    flat = (side * side, half_chan)
    shape4 = SHAPES[lax.axis_size("tiles")]
    n_yh, n_z, n_x, n_core = shape4
    width = side + 16
    cells = side * side // 2
    steps = side // 2 // MLP_ROWS
    a_rows = CHAN // n_x
    vmem = pltpu.VMEM
    whole = pl.BlockSpec(memory_space=pltpu.VMEM)
    dma = pltpu.SemaphoreType.DMA
    padded = vmem(((side + 2 * MARGIN) * width, LANES), F32)
    taps = vmem((KERNEL * KERNEL * 8, LANES), F32)
    piece = vmem((cells, LANES), BF16)
    small = vmem((64, LANES), F32)
    pars = vmem((8, HALF_HIDDEN), F32)
    scratch = [
        padded, padded, taps, taps,
        vmem((4, MARGIN * side, LANES), BF16),
        vmem((2, MARGIN * 16, LANES), BF16),
        vmem((2, 2, 4, MARGIN * side, LANES), BF16),
        vmem((2, 2, MARGIN * side, LANES), BF16),
        vmem((2, 2, MARGIN * 16, LANES), BF16),
        vmem((2, CHAN, HALF_HIDDEN), BF16),
        vmem((2, HALF_HIDDEN, CHAN), BF16),
        pars, pars,
        vmem((side * side, LANES), BF16), vmem((LANES, LANES), F32),
        piece, piece, piece, vmem((side * side, LANES), BF16), piece, piece, piece,
        vmem((2, CHAN, HIDDEN), F32),
        vmem((8, CHAN), F32),
        vmem((8, HIDDEN), F32),
        vmem((CHAN, HIDDEN), F32),
        vmem((n_x - 1, a_rows, HIDDEN), F32),
        vmem((n_x - 1, a_rows // n_z, HIDDEN), F32),
        vmem((3, a_rows // n_z // 2, HALF_HIDDEN), F32),
        vmem((2, CHAN, HALF_HIDDEN), F32),
        small, vmem((8, LANES), F32), vmem((8, LANES), F32), small,
        vmem((n_x, 64, LANES), F32), vmem((n_z, 64, LANES), F32), vmem((2, 64, LANES), F32),
        dma((2, 12)), dma((2, 12)), dma((7,)), dma((7,)),
        dma((steps,)), dma((steps,)), dma((steps,)), dma((steps,)), dma((steps,)), dma((steps,)),
        dma((10,)), dma((10,)), dma((8,)), dma((8,)), dma((9,)), dma((9,)),
    ]
    return pl.pallas_call(
        functools.partial(kernel, side, shape4),
        out_shape=(
            jax.ShapeDtypeStruct(flat, BF16),
            jax.ShapeDtypeStruct((2, CHAN, HALF_HIDDEN), F32),
            jax.ShapeDtypeStruct((64, LANES), F32),
        ),
        in_specs=[whole] * 10,
        out_specs=(whole, whole, whole),
        scratch_shapes=scratch,
        compiler_params=pltpu.CompilerParams(
            collective_id=0, has_side_effects=True, vmem_limit_bytes=60 * 1024 * 1024
        ),
    )(
        neighbours,
        inputs.reshape(flat),
        cotangent.reshape(flat),
        wet[0],
        depth_weight,
        gamma.reshape(1, half_chan),
        up_weight,
        up_bias.reshape(1, -1),
        down_weight,
        layer_scale.reshape(1, half_chan),
    )


def body(
    inputs,
    cotangent,
    wet,
    neighbours,
    depth_weight,
    gamma,
    up_weight,
    up_bias,
    down_weight,
    layer_scale,
):
    grad, mats, small = block_call(
        inputs, cotangent, wet, neighbours, depth_weight, gamma, up_weight, up_bias, down_weight, layer_scale
    )
    taps = KERNEL * KERNEL
    return (
        grad.reshape(inputs.shape),
        small[:taps].reshape(KERNEL, KERNEL, LANES),
        small[taps],
        mats[0],
        small[taps + 2 : taps + 6].reshape(-1),
        mats[1].T,
        small[taps + 1],
    )


def solution(mesh):
    return jax.shard_map(
        body,
        mesh=mesh,
        in_specs=(
            P("tiles", None, None, "chan"),
            P("tiles", None, None, "chan"),
            P("tiles", None, None),
            P(),
            P(None, None, "chan"),
            P("chan"),
            P(None, "chan"),
            P("chan"),
            P("chan", None),
            P("chan"),
        ),
        out_specs=(
            P("tiles", None, None, "chan"),
            P(None, None, "chan"),
            P("chan"),
            P(None, "chan"),
            P("chan"),
            P("chan", None),
            P("chan"),
        ),
        check_vma=False,
    )
```

```python
import functools
import math

import jax
import jax.numpy as jnp
from jax import lax
from jax.experimental import pallas as pl
from jax.experimental.pallas import tpu as pltpu
from jax.sharding import PartitionSpec as P

KERNEL = 7
MARGIN = 3
LANES = 128
CHAN = 256
HIDDEN = 1024
HALF_HIDDEN = 512
BLOCK = 256
ROWS = 8
COLS = 2
REACH = 5
F32 = jnp.float32
BF16 = jnp.bfloat16
MESH = pl.DeviceIdType.MESH
density = 0.3989422804014327
half_log2 = -0.7213475204444817


def gelu_pieces(hidden):
    size = jnp.abs(hidden)
    denom = 1.0 + 0.2316419 * size
    inverse = pl.reciprocal(denom, approx=True)
    inverse = inverse * (2.0 - denom * inverse)
    bell = jnp.exp2(hidden * hidden * half_log2)
    poly = 0.5 * 1.061405429
    for factor in (-1.453152027, 1.421413741, -0.284496736, 0.254829592):
        poly = poly * inverse + 0.5 * factor
    tail = poly * inverse * bell
    normal_cdf = jnp.where(hidden >= 0.0, 1.0 - tail, tail)
    activated = hidden * normal_cdf
    slope = normal_cdf + hidden * bell * density
    return activated, slope


def nn(a, b):
    return lax.dot_general(a, b, (((1,), (0,)), ((), ())), preferred_element_type=F32)


def nt(a, b):
    return lax.dot_general(a, b, (((1,), (1,)), ((), ())), preferred_element_type=F32)


def kernel(
    side, shape4,
    links_in, x_in, c_in, wet_ref, depth_ref, gamma_ref, up_ref, bias_ref, down_ref, scale_ref,
    out_ref, taps_ref, gain_ref, up_sum_ref, bias_sum_ref, down_sum_ref, scale_sum_ref,
    links, x_ref, c_ref, out_tile, load_sem, out_sem,
    pf, pg, taps, taps_acc, strips, corners, rows_in, cols_in, corners_in,
    wu, wd, pars, pars_in,
    mask_ref, wet_turned, grad_in, y_all, y_in, conv_send, conv_in,
    sums, gamma_acc, bias_acc, ring_core, ring_a, ring_b, ring_y, total,
    small_a, small_peer, small_peer_in, small_core, small_x, small_z, small_y,
    halo_send, halo_recv, weight_sem, weight_recv, grad_sem, grad_recv, y_sem, y_recv, conv_sem, conv_recv,
    rs_send, rs_recv, ag_send, ag_recv, sm_send, sm_recv,
):
    n_yh, n_z, n_x, n_core = shape4
    tiles = n_yh * n_z * n_x * n_core
    width = side + 16
    row_steps = side // ROWS
    steps = row_steps // 2
    chunk = ROWS * side
    me = lax.axis_index("tiles")
    h = lax.axis_index("chan")
    other = 1 - h
    core = me % n_core
    at_x = (me // n_core) % n_x
    at_z = (me // (n_core * n_x)) % n_z
    at_yh = me // (n_core * n_x * n_z)
    q = 1.0 / (side * math.sqrt(tiles))

    def tile_at(yh, z, x, c):
        return ((yh * n_z + z) * n_x + x) * n_core + c

    def dev(tile, chan=None):
        return {"tiles": tile, "chan": h if chan is None else chan}

    def remote(src, dst, send, recv, device):
        return pltpu.make_async_remote_copy(
            src_ref=src, dst_ref=dst, send_sem=send, recv_sem=recv, device_id=device, device_id_type=MESH
        )

    def line_at(which, k):
        return k + which * (row_steps - 1 - 2 * k)

    def chunk_rows(line):
        return pl.ds(pl.multiple_of(line * chunk, chunk), chunk)

    first = core * at_z + (1 - core) * at_x
    second = core * at_x + (1 - core) * at_z

    def ring_tile(a, b):
        return tile_at(at_yh, core * a + (1 - core) * b, core * b + (1 - core) * a, core)

    peer = dev(me, other)
    core_peer = dev(tile_at(at_yh, at_z, at_x, 1 - core))
    halo = [(sign, d) for sign in (1, -1) for d in range(1, REACH + 1)]

    def halo_tile(sign, d):
        return (me + sign * d + tiles) % tiles

    a_peers = [(first + k) % n_x for k in range(1, n_x)]
    b_peers = [(second + k) % n_x for k in range(1, n_x)]
    y_peers = [(0, 1), (1, 0), (1, 1)]

    def y_dev(dy, dc):
        return dev(tile_at((at_yh + dy) % 2, at_z, at_x, core), (h + dc) % 2)

    barrier = pltpu.get_barrier_semaphore()
    targets = [dev(halo_tile(s, d)) for s, d in halo]
    targets += [core_peer]
    targets += [dev(ring_tile(a, second)) for a in a_peers]
    targets += [dev(ring_tile(first, b)) for b in b_peers]
    targets += [y_dev(dy, dc) for dy, dc in y_peers]
    for target in targets:
        pl.semaphore_signal(barrier, inc=1, device_id=target, device_id_type=MESH)
    loads = [
        pltpu.make_async_copy(x_in, x_ref, load_sem.at[0]),
        pltpu.make_async_copy(c_in, c_ref, load_sem.at[1]),
        pltpu.make_async_copy(up_ref, wu.at[h], load_sem.at[2]),
        pltpu.make_async_copy(down_ref, wd.at[h], load_sem.at[3]),
        pltpu.make_async_copy(links_in, links, load_sem.at[4]),
    ]
    for copy in loads:
        copy.start()
    pars[...] = jnp.zeros_like(pars)
    pars[0:1, :] = bias_ref[...].astype(F32).reshape(1, HALF_HIDDEN)
    pars[1:2, 0:LANES] = gamma_ref[...].astype(F32).reshape(1, LANES)
    pars[2:3, 0:LANES] = scale_ref[...].astype(F32).reshape(1, LANES)
    wet_turned[...] = jnp.zeros_like(wet_turned)
    wet_turned[0:side, 0:side] = wet_ref[...].astype(F32)
    wet_turned[...] = wet_turned[...].T
    pl.semaphore_wait(barrier, len(targets))

    diagonal = y_dev(1, 1)
    up_part, down_part = CHAN // 4, HALF_HIDDEN // 4

    def part(ref, size, at, count=1):
        return ref.at[pl.ds(pl.multiple_of(at * size, size), count * size), :]

    def weight_copy(n, device, quarter, slot):
        up = remote(
            part(up_ref, up_part, quarter), part(wu.at[slot], up_part, quarter),
            weight_sem.at[n], weight_recv.at[n], device,
        )
        down = remote(
            part(down_ref, down_part, quarter), part(wd.at[slot], down_part, quarter),
            weight_sem.at[n + 1], weight_recv.at[n + 1], device,
        )
        return [up, down]

    pars_copy = remote(pars, pars_in, weight_sem.at[0], weight_recv.at[0], peer)
    weight_copies = weight_copy(1, peer, 2 * core, h) + weight_copy(3, diagonal, 2 * core + 1, h)
    weight_arrivals = weight_copy(1, peer, 2 * core, other) + weight_copy(3, diagonal, 2 * core + 1, other)

    def weight_forward(half_at):
        return [
            remote(
                part(wu.at[other], up_part, 2 * half_at, 2), part(wu.at[other], up_part, 2 * half_at, 2),
                weight_sem.at[5], weight_recv.at[5], core_peer,
            ),
            remote(
                part(wd.at[other], down_part, 2 * half_at, 2), part(wd.at[other], down_part, 2 * half_at, 2),
                weight_sem.at[6], weight_recv.at[6], core_peer,
            ),
        ]

    pars_copy.start()
    for copy in weight_copies:
        copy.start()

    early = min(4, steps)

    def grad_copy(k):
        return remote(
            c_in.at[chunk_rows(line_at(other, k)), :], grad_in.at[chunk_rows(k), :],
            grad_sem.at[k], grad_recv.at[k], peer,
        )

    for k in range(early):
        grad_copy(k).start()

    loads[0].wait()
    def fill_input(g, _):
        columns = pltpu.roll(wet_turned[0:side, :], (LANES - g * ROWS) % LANES, 1)
        for t in range(ROWS):
            i = g * ROWS + t
            at = pl.ds(pl.multiple_of(i * side, side), side)
            to = pl.multiple_of((i + MARGIN) * width + 8, 8)
            wet = jnp.broadcast_to(columns[:, t : t + 1], (side, LANES))
            mask_ref[at, :] = wet.astype(BF16)
            pf[pl.ds(to, side), :] = x_ref[at, :].astype(F32) * wet
        return 0

    lax.fori_loop(0, side // ROWS, fill_input, 0)

    def row_strips(padded):
        for side_at, row in enumerate((MARGIN, side)):
            for k in range(MARGIN):
                base = (row + k) * width + 8
                strips[side_at, k * side : (k + 1) * side, :] = padded[base : base + side, :].astype(BF16)
                near = base if side_at == 0 else base + side - 16
                corners[side_at, k * 16 : (k + 1) * 16, :] = padded[near : near + 16, :].astype(BF16)

    def col_strips(padded):
        for side_at, col in enumerate((8, 8 + side - MARGIN)):
            for k in range(MARGIN):
                line = padded[pl.ds(MARGIN * width + col + k, side, stride=width), :]
                strips[2 + side_at, k * side : (k + 1) * side, :] = line.astype(BF16)

    def row_copies(phase):
        copies = []
        for n, (sign, d) in enumerate(halo):
            device = dev(halo_tile(sign, d))
            way = 0 if sign > 0 else 1
            send = halo_send.at[phase, n]
            recv = halo_recv.at[phase, n]
            if d < REACH:
                copies.append(remote(strips.at[1 - way], rows_in.at[phase, way, d - 1], send, recv, device))
            else:
                copies.append(remote(corners.at[1 - way], corners_in.at[phase, way], send, recv, device))
        return copies

    def col_copies(phase):
        copies = []
        for way, sign in enumerate((1, -1)):
            device = dev(halo_tile(sign, 1))
            n = len(halo) + way
            copies.append(
                remote(strips.at[3 - way], cols_in.at[phase, way], halo_send.at[phase, n], halo_recv.at[phase, n], device)
            )
        return copies

    def match(direction, source):
        link = links[pl.ds(me, 1), direction : direction + 1]
        return jnp.where(jnp.logical_and(link == source, link >= 0), 1.0, 0.0)

    def fill_halo(padded, phase):
        for way, sign in enumerate((-1, 1)):
            straight, left, right, beside = ((0, 4, 5, 2), (1, 6, 7, 3))[way]
            row = 0 if way == 0 else side + MARGIN
            straight_hit = [match(straight, me + sign * d) for d in range(1, 5)]
            left_hit = [match(left, me + sign * d) for d in range(1, 6)]
            right_hit = [match(right, me + sign * d) for d in range(1, 6)]
            far_hit = left_hit[4] if way == 0 else right_hit[4]
            for k in range(MARGIN):
                base = (row + k) * width
                lines = [rows_in[phase, way, d, k * side : (k + 1) * side, :].astype(F32) for d in range(4)]
                far = corners_in[phase, way, k * 16 : (k + 1) * 16, :].astype(F32)
                middle = sum(hit * line for hit, line in zip(straight_hit, lines))
                west = sum(hit * line[side - 8 :] for hit, line in zip(left_hit[:4], lines))
                east = sum(hit * line[:8] for hit, line in zip(right_hit[:4], lines))
                if way == 0:
                    west = west + far_hit * far[8:]
                else:
                    east = east + far_hit * far[:8]
                padded[base : base + 8, :] = west
                padded[base + 8 : base + 8 + side, :] = middle
                padded[base + 8 + side : base + 16 + side, :] = east
            hit = match(beside, me + sign)
            col = 8 - MARGIN if way == 0 else 8 + side
            for k in range(MARGIN):
                line = cols_in[phase, way, k * side : (k + 1) * side, :].astype(F32)
                padded[pl.ds(MARGIN * width + col + k, side, stride=width), :] = line * hit

    row_strips(pf)
    col_strips(pf)
    forward_halo = row_copies(0) + col_copies(0)
    for copy in forward_halo:
        copy.start()
    loads[4].wait()

    for a in range(KERNEL):
        for b in range(KERNEL):
            n = (a * KERNEL + b) * 8
            taps[n : n + 8, :] = jnp.broadcast_to(depth_ref[a, b : b + 1, :], (8, LANES))

    for copy in weight_arrivals:
        copy.wait_recv()
    forwards = weight_forward(core)
    for copy in forwards:
        copy.start()

    def conv_block(padded, row, col, flip):
        base = row * width + col + 8 - MARGIN
        acc = [[None] * COLS for _ in range(ROWS)]
        for b in range(KERNEL):
            weights = []
            for a in range(KERNEL):
                n = a * KERNEL + b
                n = (KERNEL * KERNEL - 1 - n if flip else n) * 8
                weights.append(taps[n : n + 8, :])
            for r in range(ROWS + KERNEL - 1):
                for v in range(COLS):
                    value = padded[pl.ds(base + (r * width + v * 8 + b), 8), :]
                    for a in range(KERNEL):
                        i = r - a
                        if 0 <= i < ROWS:
                            term = value * weights[a]
                            acc[i][v] = term if acc[i][v] is None else acc[i][v] + term
        return acc

    col_steps = side // (8 * COLS)

    def filter_forward(k, c):
        col = pl.multiple_of(c * (8 * COLS), 8 * COLS)
        acc = conv_block(pf, k * ROWS, col, False)
        for i in range(ROWS):
            at = pl.multiple_of((k * ROWS + i) * side + col, 8 * COLS)
            y_all[pl.ds(at, 8 * COLS), :] = jnp.concatenate(acc[i], 0).astype(BF16)

    def conv_inner(n, _):
        filter_forward(1 + n // (col_steps - 2), 1 + n % (col_steps - 2))
        return 0

    lax.fori_loop(0, (row_steps - 2) * (col_steps - 2), conv_inner, 0)
    for copy in forward_halo:
        copy.wait_recv()
    fill_halo(pf, 0)

    def y_copy(k):
        return remote(
            y_all.at[chunk_rows(line_at(other, k)), :], y_in.at[chunk_rows(k), :], y_sem.at[k], y_recv.at[k], peer
        )

    def conv_outer(n, _):
        away = n < steps
        k = jnp.where(away, line_at(other, n), line_at(h, n - steps))
        edge = jnp.logical_or(k == 0, k == row_steps - 1)

        def one(c, _):
            filter_forward(k, jnp.where(edge, c, c * (col_steps - 1)))
            return 0

        lax.fori_loop(0, jnp.where(edge, col_steps, 2), one, 0)

        @pl.when(away)
        def _():
            y_copy(n).start()

        @pl.when(n + early < steps)
        def _():
            grad_copy(n + early).start()

        return 0

    lax.fori_loop(0, row_steps, conv_outer, 0)

    pars_copy.wait_recv()
    for copy in weight_forward(1 - core):
        copy.wait_recv()
    for copy in loads[1:4]:
        copy.wait()
    for copy in forward_halo:
        copy.wait_send()
    mine = h == 0

    def ordered(own, others):
        return jnp.where(mine, own, others), jnp.where(mine, others, own)

    def row_of(n):
        own, others = pars[n : n + 1, 0:LANES], pars_in[n : n + 1, 0:LANES]
        return jnp.concatenate(ordered(own, others), 1)

    gamma_row = row_of(1)
    scale_row = row_of(2)
    bias_rows = ordered(pars[0:1, :], pars_in[0:1, :])

    sums[...] = jnp.zeros_like(sums)
    gamma_acc[...] = jnp.zeros_like(gamma_acc)
    bias_acc[...] = jnp.zeros_like(bias_acc)
    taps_acc[...] = jnp.zeros_like(taps_acc)

    def conv_copy(k):
        at = chunk_rows(k)
        return remote(conv_send.at[at, :], conv_in.at[at, :], conv_sem.at[k], conv_recv.at[k], peer)

    def take_conv(k):
        conv_copy(k).wait_recv()
        for i in range(ROWS):
            at = pl.multiple_of((k * ROWS + i) * side, side)
            to = pl.multiple_of((MARGIN + line_at(other, k) * ROWS + i) * width + 8, 8)
            pg[pl.ds(to, side), :] = conv_in[pl.ds(at, side), :].astype(F32)

    def filter_line(line):
        row = line * ROWS

        def one(c, _):
            col = c * (8 * COLS)
            inner = (row + MARGIN) * width + col + 8
            base = row * width + col + 8 - MARGIN
            grads = [
                [pg[pl.ds(pl.multiple_of(inner, 8) + (i * width + v * 8), 8), :] for v in range(COLS)] for i in range(ROWS)
            ]
            for b in range(KERNEL):
                acc = [None] * KERNEL
                for r in range(ROWS + KERNEL - 1):
                    for v in range(COLS):
                        value = pf[pl.ds(base + (r * width + v * 8 + b), 8), :]
                        for a in range(KERNEL):
                            i = r - a
                            if 0 <= i < ROWS:
                                term = value * grads[i][v]
                                acc[a] = term if acc[a] is None else acc[a] + term
                for a in range(KERNEL):
                    n = (a * KERNEL + b) * 8
                    taps_acc[n : n + 8, :] += acc[a]
            return 0

        lax.fori_loop(0, col_steps, one, 0)

    def mlp(k, _):
        at = chunk_rows(k)
        line = line_at(h, k)
        own_at = chunk_rows(line)
        y_copy(k).wait_recv()
        grad_copy(k).wait_recv()
        low, high = ordered(y_all[own_at, :].astype(F32), y_in[at, :].astype(F32))
        y = jnp.concatenate((low, high), 1)
        centred = y - jnp.sum(y, 1, keepdims=True) * (1.0 / CHAN)
        spread = jnp.sum(centred * centred, 1, keepdims=True) * (1.0 / CHAN)
        inv_spread = lax.rsqrt(spread + 1e-06)
        unit = centred * inv_spread
        normed = (unit * gamma_row).astype(BF16)
        wet = mask_ref[own_at, :].astype(F32)
        low, high = ordered(c_ref[own_at, :].astype(F32), grad_in[at, :].astype(F32))
        branch_grad = (jnp.concatenate((low * wet, high * wet), 1) * scale_row).astype(BF16)
        branch_t = branch_grad.T
        normed_t = jnp.concatenate((normed.T, jnp.ones((16, chunk), BF16)), 0)
        norm_grad = jnp.zeros((chunk, CHAN), F32)
        for block in range(HIDDEN // BLOCK):
            slot, off = divmod(block * BLOCK, HALF_HIDDEN)
            w_up = wu[slot, :, off : off + BLOCK]
            w_down = wd[slot, off : off + BLOCK, :]
            cols = slice(block * BLOCK, (block + 1) * BLOCK)
            hidden = nn(normed, w_up) + bias_rows[slot][:, off : off + BLOCK]
            activated, slope = gelu_pieces(hidden)
            hidden_grad = (nt(branch_grad, w_down) * slope).astype(BF16)
            sums[1, :, cols] += nn(branch_t, activated.astype(BF16))
            up_terms = nn(normed_t, hidden_grad)
            sums[0, :, cols] += up_terms[:CHAN]
            bias_acc[:, cols] += up_terms[CHAN : CHAN + 8]
            norm_grad = norm_grad + nt(hidden_grad, w_up)
        gamma_acc[...] += jnp.sum((norm_grad * unit).reshape(chunk // 8, 8, CHAN), 0)
        scaled = norm_grad * gamma_row
        mean = jnp.sum(scaled, 1, keepdims=True) * (1.0 / CHAN)
        tilt = jnp.sum(scaled * unit, 1, keepdims=True) * (1.0 / CHAN)
        conv_grad = (inv_spread * (scaled - mean - unit * tilt)).astype(BF16).astype(F32)
        own, away = ordered(conv_grad[:, :LANES], conv_grad[:, LANES:])
        conv_send[at, :] = away.astype(BF16)
        conv_copy(k).start()
        for i in range(ROWS):
            to = pl.multiple_of((MARGIN + line * ROWS + i) * width + 8, 8)
            pg[pl.ds(to, side), :] = own[i * side : (i + 1) * side]
        filter_line(line)

        @pl.when(k == steps // 2)
        def _():
            take_conv(0)
            row_strips(pg)
            for copy in row_copies(1):
                copy.start()

        return 0

    lax.fori_loop(0, steps, mlp, 0)

    rs_core = remote(sums.at[1 - core], ring_core, rs_send.at[0], rs_recv.at[0], core_peer)
    rs_core.start()

    ident = lax.broadcasted_iota(jnp.int32, (CHAN, CHAN), 0) == lax.broadcasted_iota(jnp.int32, (CHAN, CHAN), 1)
    down_sums = sums[1]
    down_high = down_sums.astype(BF16)
    down_low = (down_sums - down_high.astype(F32)).astype(BF16)
    paired = jnp.zeros((CHAN, CHAN), F32)
    for slot in range(2):
        cols = slice(slot * HALF_HIDDEN, (slot + 1) * HALF_HIDDEN)
        paired = paired + nn(down_high[:, cols], wd[slot]) + nn(down_low[:, cols], wd[slot])
    scale_sum = jnp.sum(jnp.where(ident, paired, 0.0), 0, keepdims=True) / scale_row
    gamma_sum = jnp.sum(gamma_acc[...], 0, keepdims=True)
    bias_sum = bias_acc[0:1, :]
    small_peer[...] = jnp.zeros_like(small_peer)
    small_a[...] = jnp.zeros_like(small_a)
    n_taps = KERNEL * KERNEL

    def put_small(ref, at, value, n):
        own, away = ordered(value[:, : n * LANES], value[:, n * LANES :])
        for i in range(n):
            ref[0][ref[1] + at + i : ref[1] + at + i + 1, :] = own[:, i * LANES : (i + 1) * LANES]
            small_peer[at + i : at + i + 1, :] = away[:, i * LANES : (i + 1) * LANES]

    place = (small_a, n_taps)
    put_small(place, 0, gamma_sum, 1)
    put_small(place, 1, scale_sum, 1)
    put_small(place, 2, bias_sum, 4)
    small_chan = remote(small_peer, small_peer_in, sm_send.at[0], sm_recv.at[0], peer)
    small_chan.start()

    def input_block(line, c):
        row = line * ROWS
        col = pl.multiple_of(c * (8 * COLS), 8 * COLS)
        acc = conv_block(pg, row, col, True)
        for i in range(ROWS):
            at = pl.ds(pl.multiple_of((row + i) * side + col, 8 * COLS), 8 * COLS)
            wet = mask_ref[at, :].astype(F32)
            grad = c_ref[at, :].astype(F32)
            out_tile[at, :] = (wet * (grad + jnp.concatenate(acc[i], 0))).astype(BF16)

    inner_cols = col_steps - 2

    def own_inner(n, _):
        input_block(line_at(h, 1 + n // inner_cols), 1 + n % inner_cols)
        return 0

    def rest_inner(n, _):
        k = n // inner_cols
        input_block(jnp.where(k == 0, line_at(h, steps - 1), line_at(other, k)), 1 + n % inner_cols)
        return 0

    def out_copy(k):
        return pltpu.make_async_copy(out_tile.at[chunk_rows(k), :], out_ref.at[chunk_rows(k), :], out_sem.at[k])

    def input_edges(k, _):
        edge = jnp.logical_or(k == 0, k == row_steps - 1)

        def one(c, _):
            input_block(k, jnp.where(edge, c, c * (col_steps - 1)))
            return 0

        lax.fori_loop(0, jnp.where(edge, col_steps, 2), one, 0)
        out_copy(k).start()
        return 0

    def peer_line(k, _):
        @pl.when(k > 0)
        def _():
            take_conv(k)

        filter_line(line_at(other, k))
        return 0

    lax.fori_loop(0, (steps - 2) * inner_cols, own_inner, 0)

    rs_core.wait_recv()
    sums[core] = sums[core] + ring_core[...]
    a_rows, b_rows, y_rows = CHAN // n_x, CHAN // n_x // n_z, CHAN // n_x // n_z // 2
    rs_a = []
    for k, a in enumerate(a_peers):
        piece = sums.at[core, pl.ds(pl.multiple_of(a * a_rows, a_rows), a_rows), :]
        rs_a.append(remote(piece, ring_a.at[k], rs_send.at[1 + k], rs_recv.at[1 + k], dev(ring_tile(a, second))))
    for copy in rs_a:
        copy.start()

    lax.fori_loop(0, 2, peer_line, 0)
    lax.fori_loop(2, steps - 2, peer_line, 0)

    for copy in rs_a:
        copy.wait_recv()
    a_at = pl.ds(pl.multiple_of(first * a_rows, a_rows), a_rows)
    sums[core, a_at, :] = sums[core, a_at, :] + sum(ring_a[k] for k in range(n_x - 1))
    rs_b = []
    for k, b in enumerate(b_peers):
        piece = sums.at[core, pl.ds(pl.multiple_of(first * a_rows + b * b_rows, b_rows), b_rows), :]
        rs_b.append(remote(piece, ring_b.at[k], rs_send.at[4 + k], rs_recv.at[4 + k], dev(ring_tile(first, b))))
    for copy in rs_b:
        copy.start()

    lax.fori_loop(steps - 2, steps - 1, peer_line, 0)

    for copy in rs_b:
        copy.wait_recv()
    b_start = first * a_rows + second * b_rows
    b_at = pl.ds(pl.multiple_of(b_start, b_rows), b_rows)
    sums[core, b_at, :] = sums[core, b_at, :] + sum(ring_b[k] for k in range(n_x - 1))

    def y_piece(yh, chan):
        rows = pl.ds(pl.multiple_of(b_start + yh * y_rows, y_rows), y_rows)
        return (core, rows, pl.ds(pl.multiple_of(chan * HALF_HIDDEN, HALF_HIDDEN), HALF_HIDDEN))

    rs_y = []
    for k, (dy, dc) in enumerate(y_peers):
        piece = sums.at[y_piece((at_yh + dy) % 2, (h + dc) % 2)]
        rs_y.append(remote(piece, ring_y.at[k], rs_send.at[7 + k], rs_recv.at[7 + k], y_dev(dy, dc)))
    for copy in rs_y:
        copy.start()

    take_conv(steps - 1)
    col_strips(pg)
    last_halo = col_copies(1)
    for copy in last_halo:
        copy.start()
    filter_line(line_at(other, steps - 1))

    for n in range(n_taps):
        small_a[n : n + 1, :] = jnp.sum(taps_acc[n * 8 : n * 8 + 8, :], 0, keepdims=True)
    small_chan.wait_recv()
    for n in range(6):
        small_a[n_taps + n : n_taps + n + 1, :] += small_peer_in[n : n + 1, :]
    sm_core = remote(small_a, small_core, sm_send.at[1], sm_recv.at[1], core_peer)
    sm_core.start()

    for copy in rs_y:
        copy.wait_recv()
    y_start = b_start + at_yh * y_rows
    y_at = pl.ds(pl.multiple_of(y_start, y_rows), y_rows)
    total[core, y_at, :] = sums[y_piece(at_yh, h)] + (ring_y[0] + ring_y[1] + ring_y[2])
    y_mate = dev(tile_at((at_yh + 1) % 2, at_z, at_x, core))
    ag_y = remote(total.at[core, y_at, :], total.at[core, y_at, :], ag_send.at[0], ag_recv.at[0], y_mate)
    ag_y.start()

    rest = steps * inner_cols
    lax.fori_loop(0, rest // 2, rest_inner, 0)

    ag_y.wait_recv()
    ag_b = []
    for k, b in enumerate(b_peers):
        block = total.at[core, b_at, :]
        ag_b.append(remote(block, block, ag_send.at[1 + k], ag_recv.at[1 + k], dev(ring_tile(first, b))))
    for copy in ag_b:
        copy.start()

    sm_core.wait_recv()

    def small_stage(ref, value, at, size, base, tile):
        ref[at] = value
        copies = []
        for k in range(1, size):
            there = (at + k) % size
            copies.append(
                remote(ref.at[at], ref.at[at], sm_send.at[base + k - 1], sm_recv.at[base + k - 1], dev(tile(there)))
            )
        for copy in copies:
            copy.start()
        return copies

    sm_x = small_stage(
        small_x, small_a[...] + small_core[...], at_x, n_x, 2, lambda x: tile_at(at_yh, at_z, x, core)
    )
    lax.fori_loop(rest // 2, rest, rest_inner, 0)

    for copy in ag_b:
        copy.wait_recv()
    ag_a = []
    for k, a in enumerate(a_peers):
        block = total.at[core, a_at, :]
        ag_a.append(remote(block, block, ag_send.at[4 + k], ag_recv.at[4 + k], dev(ring_tile(a, second))))
    for copy in ag_a:
        copy.start()

    for copy in sm_x:
        copy.wait_recv()
    sm_z = small_stage(
        small_z, sum(small_x[k] for k in range(n_x)), at_z, n_z, 5, lambda z: tile_at(at_yh, z, at_x, core)
    )
    first_halo = row_copies(1)
    for copy in first_halo:
        copy.wait_recv()
    for copy in last_halo:
        copy.wait_recv()
    fill_halo(pg, 1)
    lax.fori_loop(0, row_steps // 2, input_edges, 0)

    for copy in ag_a:
        copy.wait_recv()
    ag_core = remote(total.at[core], total.at[core], ag_send.at[7], ag_recv.at[7], core_peer)
    ag_core.start()

    for copy in sm_z:
        copy.wait_recv()
    sm_y = small_stage(
        small_y, sum(small_z[k] for k in range(n_z)), at_yh, 2, 8, lambda yh: tile_at(yh, at_z, at_x, core)
    )
    lax.fori_loop(row_steps // 2, row_steps, input_edges, 0)

    @pl.when(core == 0)
    def _():
        up_sum_ref[...] = total[0] * q

    @pl.when(core == 1)
    def _():
        down_sum_ref[...] = total[1].T * q

    for copy in sm_y:
        copy.wait_recv()
    small = (small_y[0] + small_y[1]) * q
    for a in range(KERNEL):
        taps_ref[a] = small[a * KERNEL : (a + 1) * KERNEL]
    gain_ref[...] = small[n_taps : n_taps + 1].reshape(LANES)
    scale_sum_ref[...] = small[n_taps + 1 : n_taps + 2].reshape(LANES)
    for i in range(4):
        bias_sum_ref[i * LANES : (i + 1) * LANES] = small[n_taps + 2 + i : n_taps + 3 + i].reshape(LANES)
    ag_core.wait_recv()

    @pl.when(core == 1)
    def _():
        up_sum_ref[...] = total[0] * q

    @pl.when(core == 0)
    def _():
        down_sum_ref[...] = total[1].T * q

    for copy in weight_copies + forwards + first_halo + last_halo + [pars_copy, rs_core, small_chan, sm_core, ag_y, ag_core]:
        copy.wait_send()
    for copy in rs_a + rs_b + rs_y + ag_a + ag_b + sm_x + sm_z + sm_y:
        copy.wait_send()

    def finish(k, _):
        grad_copy(k).wait_send()
        y_copy(k).wait_send()
        conv_copy(k).wait_send()
        out_copy(k).wait()
        out_copy(k + steps).wait()
        return 0

    lax.fori_loop(0, steps, finish, 0)


SHAPES = {64: (2, 4, 4, 2), 16: (2, 2, 2, 2)}


def block_call(inputs, cotangent, wet, neighbours, depth_weight, gamma, up_weight, up_bias, down_weight, layer_scale):
    side = inputs.shape[1]
    half_chan = inputs.shape[3]
    flat = (side * side, half_chan)
    shape4 = SHAPES[lax.axis_size("tiles")]
    n_yh, n_z, n_x, n_core = shape4
    width = side + 16
    cells = side * side // 2
    row_steps = side // ROWS
    steps = row_steps // 2
    a_rows = CHAN // n_x
    vmem = pltpu.VMEM
    whole = pl.BlockSpec(memory_space=pltpu.VMEM)
    hbm = pl.BlockSpec(memory_space=pl.ANY)
    dma = pltpu.SemaphoreType.DMA
    padded = vmem(((side + 2 * MARGIN) * width, LANES), F32)
    taps = vmem((KERNEL * KERNEL * 8, LANES), F32)
    piece = vmem((cells, LANES), BF16)
    small = vmem((64, LANES), F32)
    pars = vmem((8, HALF_HIDDEN), F32)
    tile = vmem((side * side, LANES), BF16)
    scratch = [
        vmem(neighbours.shape, jnp.int32), tile, tile, tile, dma((5,)), dma((row_steps,)),
        padded, padded, taps, taps,
        vmem((4, MARGIN * side, LANES), BF16),
        vmem((2, MARGIN * 16, LANES), BF16),
        vmem((2, 2, 4, MARGIN * side, LANES), BF16),
        vmem((2, 2, MARGIN * side, LANES), BF16),
        vmem((2, 2, MARGIN * 16, LANES), BF16),
        vmem((2, CHAN, HALF_HIDDEN), BF16),
        vmem((2, HALF_HIDDEN, CHAN), BF16),
        pars, pars,
        tile, vmem((LANES, LANES), F32),
        piece, tile, piece, piece, piece,
        vmem((2, CHAN, HIDDEN), F32),
        vmem((8, CHAN), F32),
        vmem((8, HIDDEN), F32),
        vmem((CHAN, HIDDEN), F32),
        vmem((n_x - 1, a_rows, HIDDEN), F32),
        vmem((n_x - 1, a_rows // n_z, HIDDEN), F32),
        vmem((3, a_rows // n_z // 2, HALF_HIDDEN), F32),
        vmem((2, CHAN, HALF_HIDDEN), F32),
        small, vmem((8, LANES), F32), vmem((8, LANES), F32), small,
        vmem((n_x, 64, LANES), F32), vmem((n_z, 64, LANES), F32), vmem((2, 64, LANES), F32),
        dma((2, 12)), dma((2, 12)), dma((7,)), dma((7,)),
        dma((steps,)), dma((steps,)), dma((steps,)), dma((steps,)), dma((steps,)), dma((steps,)),
        dma((10,)), dma((10,)), dma((8,)), dma((8,)), dma((9,)), dma((9,)),
    ]
    return pl.pallas_call(
        functools.partial(kernel, side, shape4),
        out_shape=(
            jax.ShapeDtypeStruct(flat, BF16),
            jax.ShapeDtypeStruct((KERNEL, KERNEL, LANES), F32),
            jax.ShapeDtypeStruct((LANES,), F32),
            jax.ShapeDtypeStruct((CHAN, HALF_HIDDEN), F32),
            jax.ShapeDtypeStruct((HALF_HIDDEN,), F32),
            jax.ShapeDtypeStruct((HALF_HIDDEN, CHAN), F32),
            jax.ShapeDtypeStruct((LANES,), F32),
        ),
        in_specs=[hbm, hbm, hbm, whole, whole, whole, hbm, whole, hbm, whole],
        out_specs=(hbm, whole, whole, whole, whole, whole, whole),
        scratch_shapes=scratch,
        compiler_params=pltpu.CompilerParams(
            collective_id=0, has_side_effects=True, vmem_limit_bytes=60 * 1024 * 1024
        ),
    )(
        neighbours,
        inputs.reshape(flat),
        cotangent.reshape(flat),
        wet[0],
        depth_weight,
        gamma,
        up_weight,
        up_bias,
        down_weight,
        layer_scale,
    )


def body(
    inputs,
    cotangent,
    wet,
    neighbours,
    depth_weight,
    gamma,
    up_weight,
    up_bias,
    down_weight,
    layer_scale,
):
    grad, *sums = block_call(
        inputs, cotangent, wet, neighbours, depth_weight, gamma, up_weight, up_bias, down_weight, layer_scale
    )
    return (grad.reshape(inputs.shape), *sums)


def solution(mesh):
    return jax.shard_map(
        body,
        mesh=mesh,
        in_specs=(
            P("tiles", None, None, "chan"),
            P("tiles", None, None, "chan"),
            P("tiles", None, None),
            P(),
            P(None, None, "chan"),
            P("chan"),
            P(None, "chan"),
            P("chan"),
            P("chan", None),
            P("chan"),
        ),
        out_specs=(
            P("tiles", None, None, "chan"),
            P(None, None, "chan"),
            P("chan"),
            P(None, "chan"),
            P("chan"),
            P("chan", None),
            P("chan"),
        ),
        check_vma=False,
    )
```

```python
import functools
import math

import jax
import jax.numpy as jnp
from jax import lax
from jax.experimental import pallas as pl
from jax.experimental.pallas import tpu as pltpu
from jax.sharding import PartitionSpec as P

KERNEL = 7
MARGIN = 3
LANES = 128
CHAN = 256
HIDDEN = 1024
HALF_HIDDEN = 512
BLOCK = 256
ROWS = 8
COLS = 2
REACH = 5
F32 = jnp.float32
BF16 = jnp.bfloat16
MESH = pl.DeviceIdType.MESH
density = 0.3989422804014327
half_log2 = -0.7213475204444817


def gelu_pieces(hidden):
    size = jnp.abs(hidden)
    denom = 1.0 + 0.2316419 * size
    inverse = pl.reciprocal(denom, approx=True)
    inverse = inverse * (2.0 - denom * inverse)
    bell = jnp.exp2(hidden * hidden * half_log2)
    poly = 0.5 * 1.061405429
    for factor in (-1.453152027, 1.421413741, -0.284496736, 0.254829592):
        poly = poly * inverse + 0.5 * factor
    tail = poly * inverse * bell
    normal_cdf = jnp.where(hidden >= 0.0, 1.0 - tail, tail)
    activated = hidden * normal_cdf
    slope = normal_cdf + hidden * bell * density
    return activated, slope


def nn(a, b):
    return lax.dot_general(a, b, (((1,), (0,)), ((), ())), preferred_element_type=F32)


def nt(a, b):
    return lax.dot_general(a, b, (((1,), (1,)), ((), ())), preferred_element_type=F32)


def kernel(
    side, shape4,
    links_in, x_in, c_in, wet_ref, depth_ref, gamma_ref, up_ref, bias_ref, down_ref, scale_ref,
    out_ref, taps_ref, gain_ref, up_sum_ref, bias_sum_ref, down_sum_ref, scale_sum_ref,
    links, x_ref, c_ref, load_sem,
    pf, pg, taps, taps_acc, strips, corners, rows_in, cols_in, corners_in,
    wu, wd, pars, pars_in,
    mask_ref, wet_turned, grad_in, y_all, y_in, conv_send, conv_in,
    sums, gamma_acc, bias_acc, core_out, ring_out, ring_core, ring_a, ring_b, ring_y, total,
    small_a, small_peer, small_peer_in, small_core, small_x, small_z, small_y,
    halo_send, halo_recv, weight_sem, weight_recv, grad_sem, grad_recv, y_sem, y_recv, conv_sem, conv_recv,
    rs_send, rs_recv, ag_send, ag_recv, sm_send, sm_recv,
):
    n_yh, n_z, n_x, n_core = shape4
    tiles = n_yh * n_z * n_x * n_core
    width = side + 16
    row_steps = side // ROWS
    steps = row_steps // 2
    chunk = ROWS * side
    me = lax.axis_index("tiles")
    h = lax.axis_index("chan")
    other = 1 - h
    core = me % n_core
    at_x = (me // n_core) % n_x
    at_z = (me // (n_core * n_x)) % n_z
    at_yh = me // (n_core * n_x * n_z)
    q = 1.0 / (side * math.sqrt(tiles))

    def tile_at(yh, z, x, c):
        return ((yh * n_z + z) * n_x + x) * n_core + c

    def dev(tile, chan=None):
        return {"tiles": tile, "chan": h if chan is None else chan}

    def remote(src, dst, send, recv, device):
        return pltpu.make_async_remote_copy(
            src_ref=src, dst_ref=dst, send_sem=send, recv_sem=recv, device_id=device, device_id_type=MESH
        )

    def line_at(which, k):
        return k + which * (row_steps - 1 - 2 * k)

    def chunk_rows(line):
        return pl.ds(pl.multiple_of(line * chunk, chunk), chunk)

    first = core * at_z + (1 - core) * at_x
    second = core * at_x + (1 - core) * at_z

    def ring_tile(a, b):
        return tile_at(at_yh, core * a + (1 - core) * b, core * b + (1 - core) * a, core)

    peer = dev(me, other)
    core_peer = dev(tile_at(at_yh, at_z, at_x, 1 - core))
    halo = [(sign, d) for sign in (1, -1) for d in range(1, REACH + 1)]

    def halo_tile(sign, d):
        return (me + sign * d + tiles) % tiles

    a_peers = [(first + k) % n_x for k in range(1, n_x)]
    b_peers = [(second + k) % n_x for k in range(1, n_x)]
    y_peers = [(0, 1), (1, 0), (1, 1)]

    def y_dev(dy, dc):
        return dev(tile_at((at_yh + dy) % 2, at_z, at_x, core), (h + dc) % 2)

    barrier = pltpu.get_barrier_semaphore()
    targets = [dev(halo_tile(s, d)) for s, d in halo]
    targets += [core_peer]
    targets += [dev(ring_tile(a, second)) for a in a_peers]
    targets += [dev(ring_tile(first, b)) for b in b_peers]
    targets += [y_dev(dy, dc) for dy, dc in y_peers]
    for target in targets:
        pl.semaphore_signal(barrier, inc=1, device_id=target, device_id_type=MESH)
    loads = [
        pltpu.make_async_copy(x_in, x_ref, load_sem.at[0]),
        pltpu.make_async_copy(c_in, c_ref, load_sem.at[1]),
        pltpu.make_async_copy(up_ref, wu.at[h], load_sem.at[2]),
        pltpu.make_async_copy(down_ref, wd.at[h], load_sem.at[3]),
    ]
    for copy in loads:
        copy.start()
    pars[...] = jnp.zeros_like(pars)
    pars[0:1, :] = bias_ref[...].astype(F32).reshape(1, HALF_HIDDEN)
    pars[1:2, 0:LANES] = gamma_ref[...].astype(F32).reshape(1, LANES)
    pars[2:3, 0:LANES] = scale_ref[...].astype(F32).reshape(1, LANES)
    links[...] = jnp.zeros_like(links)
    links[0:8, 0:tiles] = links_in[...].astype(F32)
    links[...] = links[...].T
    wet_turned[...] = jnp.zeros_like(wet_turned)
    wet_turned[0:side, 0:side] = wet_ref[...].astype(F32)
    wet_turned[...] = wet_turned[...].T
    pl.semaphore_wait(barrier, len(targets))

    diagonal = y_dev(1, 1)
    up_part, down_part = CHAN // 4, HALF_HIDDEN // 4

    def part(ref, size, at, count=1):
        return ref.at[pl.ds(pl.multiple_of(at * size, size), count * size), :]

    def weight_copy(n, device, quarter, slot):
        up = remote(
            part(up_ref, up_part, quarter), part(wu.at[slot], up_part, quarter),
            weight_sem.at[n], weight_recv.at[n], device,
        )
        down = remote(
            part(down_ref, down_part, quarter), part(wd.at[slot], down_part, quarter),
            weight_sem.at[n + 1], weight_recv.at[n + 1], device,
        )
        return [up, down]

    pars_copy = remote(pars, pars_in, weight_sem.at[0], weight_recv.at[0], peer)
    weight_copies = weight_copy(1, peer, 2 * core, h) + weight_copy(3, diagonal, 2 * core + 1, h)
    weight_arrivals = weight_copy(1, peer, 2 * core, other) + weight_copy(3, diagonal, 2 * core + 1, other)

    def weight_forward(half_at):
        return [
            remote(
                part(wu.at[other], up_part, 2 * half_at, 2), part(wu.at[other], up_part, 2 * half_at, 2),
                weight_sem.at[5], weight_recv.at[5], core_peer,
            ),
            remote(
                part(wd.at[other], down_part, 2 * half_at, 2), part(wd.at[other], down_part, 2 * half_at, 2),
                weight_sem.at[6], weight_recv.at[6], core_peer,
            ),
        ]

    pars_copy.start()
    for copy in weight_copies:
        copy.start()

    early = min(4, steps)

    def grad_copy(k):
        return remote(
            c_in.at[chunk_rows(line_at(other, k)), :], grad_in.at[chunk_rows(k), :],
            grad_sem.at[k], grad_recv.at[k], peer,
        )

    grad_copy(0).start()

    loads[0].wait()
    def fill_input(g, _):
        columns = pltpu.roll(wet_turned[0:side, :], (LANES - g * ROWS) % LANES, 1)
        for t in range(ROWS):
            i = g * ROWS + t
            at = pl.ds(pl.multiple_of(i * side, side), side)
            to = pl.multiple_of((i + MARGIN) * width + 8, 8)
            wet = jnp.broadcast_to(columns[:, t : t + 1], (side, LANES))
            mask_ref[at, :] = wet.astype(BF16)
            pf[pl.ds(to, side), :] = x_ref[at, :].astype(F32) * wet
        return 0

    lax.fori_loop(0, side // ROWS, fill_input, 0)

    def row_strips(padded):
        for side_at, row in enumerate((MARGIN, side)):
            for k in range(MARGIN):
                base = (row + k) * width + 8
                strips[side_at, k * side : (k + 1) * side, :] = padded[base : base + side, :].astype(BF16)
                near = base if side_at == 0 else base + side - 16
                corners[side_at, k * 16 : (k + 1) * 16, :] = padded[near : near + 16, :].astype(BF16)

    def col_strips(padded):
        for side_at, col in enumerate((8, 8 + side - MARGIN)):
            for k in range(MARGIN):
                line = padded[pl.ds(MARGIN * width + col + k, side, stride=width), :]
                strips[2 + side_at, k * side : (k + 1) * side, :] = line.astype(BF16)

    def row_copies(phase):
        copies = []
        for n, (sign, d) in enumerate(halo):
            device = dev(halo_tile(sign, d))
            way = 0 if sign > 0 else 1
            send = halo_send.at[phase, n]
            recv = halo_recv.at[phase, n]
            if d < REACH:
                copies.append(remote(strips.at[1 - way], rows_in.at[phase, way, d - 1], send, recv, device))
            else:
                copies.append(remote(corners.at[1 - way], corners_in.at[phase, way], send, recv, device))
        return copies

    def col_copies(phase):
        copies = []
        for way, sign in enumerate((1, -1)):
            device = dev(halo_tile(sign, 1))
            n = len(halo) + way
            copies.append(
                remote(strips.at[3 - way], cols_in.at[phase, way], halo_send.at[phase, n], halo_recv.at[phase, n], device)
            )
        return copies

    def match(direction, source):
        link = links[pl.ds(me, 1), direction : direction + 1]
        return jnp.where(jnp.logical_and(link == lax.convert_element_type(source, F32), link >= 0.0), 1.0, 0.0)

    def fill_halo(padded, phase):
        for way, sign in enumerate((-1, 1)):
            straight, left, right, beside = ((0, 4, 5, 2), (1, 6, 7, 3))[way]
            row = 0 if way == 0 else side + MARGIN
            straight_hit = [match(straight, me + sign * d) for d in range(1, 5)]
            left_hit = [match(left, me + sign * d) for d in range(1, 6)]
            right_hit = [match(right, me + sign * d) for d in range(1, 6)]
            far_hit = left_hit[4] if way == 0 else right_hit[4]
            for k in range(MARGIN):
                base = (row + k) * width
                lines = [rows_in[phase, way, d, k * side : (k + 1) * side, :].astype(F32) for d in range(4)]
                far = corners_in[phase, way, k * 16 : (k + 1) * 16, :].astype(F32)
                middle = sum(hit * line for hit, line in zip(straight_hit, lines))
                west = sum(hit * line[side - 8 :] for hit, line in zip(left_hit[:4], lines))
                east = sum(hit * line[:8] for hit, line in zip(right_hit[:4], lines))
                if way == 0:
                    west = west + far_hit * far[8:]
                else:
                    east = east + far_hit * far[:8]
                padded[base : base + 8, :] = west
                padded[base + 8 : base + 8 + side, :] = middle
                padded[base + 8 + side : base + 16 + side, :] = east
            hit = match(beside, me + sign)
            col = 8 - MARGIN if way == 0 else 8 + side
            for k in range(MARGIN):
                line = cols_in[phase, way, k * side : (k + 1) * side, :].astype(F32)
                padded[pl.ds(MARGIN * width + col + k, side, stride=width), :] = line * hit

    row_strips(pf)
    col_strips(pf)
    forward_halo = row_copies(0) + col_copies(0)
    for copy in forward_halo:
        copy.start()
    for k in range(1, early):
        grad_copy(k).start()

    for a in range(KERNEL):
        for b in range(KERNEL):
            n = (a * KERNEL + b) * 8
            taps[n : n + 8, :] = jnp.broadcast_to(depth_ref[a, b : b + 1, :], (8, LANES))

    def conv_block(padded, row, col, flip):
        base = row * width + col + 8 - MARGIN
        acc = [[None] * COLS for _ in range(ROWS)]
        for b in range(KERNEL):
            weights = []
            for a in range(KERNEL):
                n = a * KERNEL + b
                n = (KERNEL * KERNEL - 1 - n if flip else n) * 8
                weights.append(taps[n : n + 8, :])
            for r in range(ROWS + KERNEL - 1):
                for v in range(COLS):
                    value = padded[pl.ds(base + (r * width + v * 8 + b), 8), :]
                    for a in range(KERNEL):
                        i = r - a
                        if 0 <= i < ROWS:
                            term = value * weights[a]
                            acc[i][v] = term if acc[i][v] is None else acc[i][v] + term
        return acc

    col_steps = side // (8 * COLS)

    def filter_forward(k, c):
        col = pl.multiple_of(c * (8 * COLS), 8 * COLS)
        acc = conv_block(pf, k * ROWS, col, False)
        for i in range(ROWS):
            at = pl.multiple_of((k * ROWS + i) * side + col, 8 * COLS)
            y_all[pl.ds(at, 8 * COLS), :] = jnp.concatenate(acc[i], 0).astype(BF16)

    def conv_inner(n, _):
        filter_forward(1 + n // (col_steps - 2), 1 + n % (col_steps - 2))
        return 0

    lax.fori_loop(0, (row_steps - 2) * (col_steps - 2), conv_inner, 0)
    for copy in weight_arrivals:
        copy.wait_recv()
    forwards = weight_forward(core)
    for copy in forwards:
        copy.start()
    for copy in forward_halo:
        copy.wait_recv()
    fill_halo(pf, 0)

    def y_copy(k):
        return remote(
            y_all.at[chunk_rows(line_at(other, k)), :], y_in.at[chunk_rows(k), :], y_sem.at[k], y_recv.at[k], peer
        )

    def conv_outer(n, _):
        away = n < steps
        k = jnp.where(away, line_at(other, n), line_at(h, n - steps))
        edge = jnp.logical_or(k == 0, k == row_steps - 1)

        def one(c, _):
            filter_forward(k, jnp.where(edge, c, c * (col_steps - 1)))
            return 0

        lax.fori_loop(0, jnp.where(edge, col_steps, 2), one, 0)

        @pl.when(away)
        def _():
            y_copy(n).start()

        @pl.when(jnp.logical_and(n + 1 >= early, n + 1 < steps))
        def _():
            grad_copy(n + 1).start()

        return 0

    lax.fori_loop(0, row_steps, conv_outer, 0)

    pars_copy.wait_recv()
    for copy in weight_forward(1 - core):
        copy.wait_recv()
    for copy in loads[1:4]:
        copy.wait()
    for copy in forward_halo:
        copy.wait_send()
    mine = h == 0

    def ordered(own, others):
        return jnp.where(mine, own, others), jnp.where(mine, others, own)

    def row_of(n):
        own, others = pars[n : n + 1, 0:LANES], pars_in[n : n + 1, 0:LANES]
        return jnp.concatenate(ordered(own, others), 1)

    gamma_row = row_of(1)
    scale_row = row_of(2)
    bias_rows = ordered(pars[0:1, :], pars_in[0:1, :])

    sums[...] = jnp.zeros_like(sums)
    gamma_acc[...] = jnp.zeros_like(gamma_acc)
    bias_acc[...] = jnp.zeros_like(bias_acc)
    taps_acc[...] = jnp.zeros_like(taps_acc)

    def conv_copy(k):
        at = chunk_rows(k)
        return remote(conv_send.at[at, :], conv_in.at[at, :], conv_sem.at[k], conv_recv.at[k], peer)

    def take_conv(k):
        conv_copy(k).wait_recv()
        for i in range(ROWS):
            at = pl.multiple_of((k * ROWS + i) * side, side)
            to = pl.multiple_of((MARGIN + line_at(other, k) * ROWS + i) * width + 8, 8)
            pg[pl.ds(to, side), :] = conv_in[pl.ds(at, side), :].astype(F32)

    def filter_line(line):
        row = line * ROWS

        def one(c, _):
            col = c * (8 * COLS)
            inner = (row + MARGIN) * width + col + 8
            base = row * width + col + 8 - MARGIN
            grads = [
                [pg[pl.ds(pl.multiple_of(inner, 8) + (i * width + v * 8), 8), :] for v in range(COLS)] for i in range(ROWS)
            ]
            for b in range(KERNEL):
                acc = [None] * KERNEL
                for r in range(ROWS + KERNEL - 1):
                    for v in range(COLS):
                        value = pf[pl.ds(base + (r * width + v * 8 + b), 8), :]
                        for a in range(KERNEL):
                            i = r - a
                            if 0 <= i < ROWS:
                                term = value * grads[i][v]
                                acc[a] = term if acc[a] is None else acc[a] + term
                for a in range(KERNEL):
                    n = (a * KERNEL + b) * 8
                    taps_acc[n : n + 8, :] += acc[a]
            return 0

        lax.fori_loop(0, col_steps, one, 0)

    def mlp(k, _):
        at = chunk_rows(k)
        line = line_at(h, k)
        own_at = chunk_rows(line)
        y_copy(k).wait_recv()
        grad_copy(k).wait_recv()
        low, high = ordered(y_all[own_at, :].astype(F32), y_in[at, :].astype(F32))
        y = jnp.concatenate((low, high), 1)
        centred = y - jnp.sum(y, 1, keepdims=True) * (1.0 / CHAN)
        spread = jnp.sum(centred * centred, 1, keepdims=True) * (1.0 / CHAN)
        inv_spread = lax.rsqrt(spread + 1e-06)
        unit = centred * inv_spread
        normed = (unit * gamma_row).astype(BF16)
        wet = mask_ref[own_at, :].astype(F32)
        low, high = ordered(c_ref[own_at, :].astype(F32), grad_in[at, :].astype(F32))
        branch_grad = (jnp.concatenate((low * wet, high * wet), 1) * scale_row).astype(BF16)
        branch_t = branch_grad.T
        normed_t = jnp.concatenate((normed.T, jnp.ones((16, chunk), BF16)), 0)
        norm_grad = jnp.zeros((chunk, CHAN), F32)
        for block in range(HIDDEN // BLOCK):
            slot, off = divmod(block * BLOCK, HALF_HIDDEN)
            w_up = wu[slot, :, off : off + BLOCK]
            w_down = wd[slot, off : off + BLOCK, :]
            cols = slice(block * BLOCK, (block + 1) * BLOCK)
            hidden = nn(normed, w_up) + bias_rows[slot][:, off : off + BLOCK]
            activated, slope = gelu_pieces(hidden)
            hidden_grad = (nt(branch_grad, w_down) * slope).astype(BF16)
            sums[1, :, cols] += nn(branch_t, activated.astype(BF16))
            up_terms = nn(normed_t, hidden_grad)
            sums[0, :, cols] += up_terms[:CHAN]
            bias_acc[:, cols] += up_terms[CHAN : CHAN + 8]
            norm_grad = norm_grad + nt(hidden_grad, w_up)
        gamma_acc[...] += jnp.sum((norm_grad * unit).reshape(chunk // 8, 8, CHAN), 0)
        scaled = norm_grad * gamma_row
        mean = jnp.sum(scaled, 1, keepdims=True) * (1.0 / CHAN)
        tilt = jnp.sum(scaled * unit, 1, keepdims=True) * (1.0 / CHAN)
        conv_grad = (inv_spread * (scaled - mean - unit * tilt)).astype(BF16).astype(F32)
        own, away = ordered(conv_grad[:, :LANES], conv_grad[:, LANES:])
        conv_send[at, :] = away.astype(BF16)
        conv_copy(k).start()
        for i in range(ROWS):
            to = pl.multiple_of((MARGIN + line * ROWS + i) * width + 8, 8)
            pg[pl.ds(to, side), :] = own[i * side : (i + 1) * side]
        filter_line(line)

        @pl.when(k == steps - 2)
        def _():
            take_conv(0)
            row_strips(pg)
            for copy in row_copies(1):
                copy.start()

        return 0

    lax.fori_loop(0, steps, mlp, 0)

    core_out[...] = sums[1 - core].astype(BF16)
    rs_core = remote(core_out, ring_core, rs_send.at[0], rs_recv.at[0], core_peer)
    rs_core.start()

    ident = lax.broadcasted_iota(jnp.int32, (CHAN, CHAN), 0) == lax.broadcasted_iota(jnp.int32, (CHAN, CHAN), 1)
    down_sums = sums[1]
    down_high = down_sums.astype(BF16)
    down_low = (down_sums - down_high.astype(F32)).astype(BF16)
    paired = jnp.zeros((CHAN, CHAN), F32)
    for slot in range(2):
        cols = slice(slot * HALF_HIDDEN, (slot + 1) * HALF_HIDDEN)
        paired = paired + nn(down_high[:, cols], wd[slot]) + nn(down_low[:, cols], wd[slot])
    scale_sum = jnp.sum(jnp.where(ident, paired, 0.0), 0, keepdims=True) / scale_row
    gamma_sum = jnp.sum(gamma_acc[...], 0, keepdims=True)
    bias_sum = bias_acc[0:1, :]
    small_peer[...] = jnp.zeros_like(small_peer)
    small_a[...] = jnp.zeros_like(small_a)
    n_taps = KERNEL * KERNEL

    def put_small(ref, at, value, n):
        own, away = ordered(value[:, : n * LANES], value[:, n * LANES :])
        for i in range(n):
            ref[0][ref[1] + at + i : ref[1] + at + i + 1, :] = own[:, i * LANES : (i + 1) * LANES]
            small_peer[at + i : at + i + 1, :] = away[:, i * LANES : (i + 1) * LANES]

    place = (small_a, n_taps)
    put_small(place, 0, gamma_sum, 1)
    put_small(place, 1, scale_sum, 1)
    put_small(place, 2, bias_sum, 4)
    small_chan = remote(small_peer, small_peer_in, sm_send.at[0], sm_recv.at[0], peer)
    small_chan.start()

    def input_block(line, c):
        row = line * ROWS
        col = pl.multiple_of(c * (8 * COLS), 8 * COLS)
        acc = conv_block(pg, row, col, True)
        for i in range(ROWS):
            at = pl.ds(pl.multiple_of((row + i) * side + col, 8 * COLS), 8 * COLS)
            wet = mask_ref[at, :].astype(F32)
            grad = c_ref[at, :].astype(F32)
            out_ref[at, :] = (wet * (grad + jnp.concatenate(acc[i], 0))).astype(BF16)

    inner_cols = col_steps - 2

    def own_inner(n, _):
        input_block(line_at(h, 1 + n // inner_cols), 1 + n % inner_cols)
        return 0

    def rest_inner(n, _):
        k = n // inner_cols
        input_block(jnp.where(k == 0, line_at(h, steps - 1), line_at(other, k)), 1 + n % inner_cols)
        return 0

    def input_edges(k, _):
        edge = jnp.logical_or(k == 0, k == row_steps - 1)

        def one(c, _):
            input_block(k, jnp.where(edge, c, c * (col_steps - 1)))
            return 0

        lax.fori_loop(0, jnp.where(edge, col_steps, 2), one, 0)
        return 0

    def peer_line(k, _):
        @pl.when(k > 0)
        def _():
            take_conv(k)

        filter_line(line_at(other, k))
        return 0

    own = (steps - 2) * inner_cols
    lax.fori_loop(0, own // 2, own_inner, 0)
    lax.fori_loop(0, 1, peer_line, 0)

    rs_core.wait_recv()
    sums[core] = sums[core] + ring_core[...].astype(F32)
    ring_out[...] = sums[core].astype(BF16)
    a_rows, b_rows, y_cols = CHAN // n_x, CHAN // n_x // n_z, HALF_HIDDEN // 2
    rs_a = []
    for k, a in enumerate(a_peers):
        piece = ring_out.at[pl.ds(pl.multiple_of(a * a_rows, a_rows), a_rows), :]
        rs_a.append(remote(piece, ring_a.at[k], rs_send.at[1 + k], rs_recv.at[1 + k], dev(ring_tile(a, second))))
    for copy in rs_a:
        copy.start()

    lax.fori_loop(own // 2, own, own_inner, 0)
    lax.fori_loop(1, steps - 2, peer_line, 0)

    for copy in rs_a:
        copy.wait_recv()
    a_at = pl.ds(pl.multiple_of(first * a_rows, a_rows), a_rows)
    sums[core, a_at, :] = sums[core, a_at, :] + sum(ring_a[k].astype(F32) for k in range(n_x - 1))
    rs_b = []
    for k, b in enumerate(b_peers):
        piece = sums.at[core, pl.ds(pl.multiple_of(first * a_rows + b * b_rows, b_rows), b_rows), :]
        rs_b.append(remote(piece, ring_b.at[k], rs_send.at[4 + k], rs_recv.at[4 + k], dev(ring_tile(first, b))))
    for copy in rs_b:
        copy.start()

    lax.fori_loop(steps - 2, steps - 1, peer_line, 0)

    take_conv(steps - 1)
    col_strips(pg)
    last_halo = col_copies(1)
    for copy in last_halo:
        copy.start()
    filter_line(line_at(other, steps - 1))

    for copy in rs_b:
        copy.wait_recv()
    b_start = first * a_rows + second * b_rows
    b_at = pl.ds(pl.multiple_of(b_start, b_rows), b_rows)
    sums[core, b_at, :] = sums[core, b_at, :] + sum(ring_b[k] for k in range(n_x - 1))

    def y_span(yh):
        return pl.ds(pl.multiple_of(yh * y_cols, y_cols), y_cols)

    def y_piece(yh, chan):
        return (core, b_at, pl.ds(pl.multiple_of(chan * HALF_HIDDEN + yh * y_cols, y_cols), y_cols))

    rs_y = []
    for k, (dy, dc) in enumerate(y_peers):
        piece = sums.at[y_piece((at_yh + dy) % 2, (h + dc) % 2)]
        rs_y.append(remote(piece, ring_y.at[k], rs_send.at[7 + k], rs_recv.at[7 + k], y_dev(dy, dc)))
    for copy in rs_y:
        copy.start()

    for n in range(n_taps):
        small_a[n : n + 1, :] = jnp.sum(taps_acc[n * 8 : n * 8 + 8, :], 0, keepdims=True)
    small_chan.wait_recv()
    for n in range(6):
        small_a[n_taps + n : n_taps + n + 1, :] += small_peer_in[n : n + 1, :]
    sm_core = remote(small_a, small_core, sm_send.at[1], sm_recv.at[1], core_peer)
    sm_core.start()

    rest = steps * inner_cols
    lax.fori_loop(0, rest // 2, rest_inner, 0)

    for copy in rs_y:
        copy.wait_recv()
    y_block = total.at[core, b_at, y_span(at_yh)]
    y_block[...] = (sums[y_piece(at_yh, h)] + (ring_y[0] + ring_y[1] + ring_y[2])).astype(BF16)
    y_mate = dev(tile_at((at_yh + 1) % 2, at_z, at_x, core))
    ag_y = remote(y_block, y_block, ag_send.at[0], ag_recv.at[0], y_mate)
    ag_y.start()

    sm_core.wait_recv()

    def small_stage(ref, value, at, size, base, tile):
        ref[at] = value
        copies = []
        for k in range(1, size):
            there = (at + k) % size
            copies.append(
                remote(ref.at[at], ref.at[at], sm_send.at[base + k - 1], sm_recv.at[base + k - 1], dev(tile(there)))
            )
        for copy in copies:
            copy.start()
        return copies

    sm_x = small_stage(
        small_x, small_a[...] + small_core[...], at_x, n_x, 2, lambda x: tile_at(at_yh, at_z, x, core)
    )
    lax.fori_loop(rest // 2, rest, rest_inner, 0)

    ag_y.wait_recv()
    ag_b = []
    for k, b in enumerate(b_peers):
        block = total.at[core, b_at, :]
        ag_b.append(remote(block, block, ag_send.at[1 + k], ag_recv.at[1 + k], dev(ring_tile(first, b))))
    for copy in ag_b:
        copy.start()

    for copy in sm_x:
        copy.wait_recv()
    sm_z = small_stage(
        small_z, sum(small_x[k] for k in range(n_x)), at_z, n_z, 5, lambda z: tile_at(at_yh, z, at_x, core)
    )
    first_halo = row_copies(1)
    for copy in first_halo:
        copy.wait_recv()
    for copy in last_halo:
        copy.wait_recv()
    fill_halo(pg, 1)
    lax.fori_loop(0, row_steps // 2, input_edges, 0)

    for copy in ag_b:
        copy.wait_recv()
    ag_a = []
    for k, a in enumerate(a_peers):
        block = total.at[core, a_at, :]
        ag_a.append(remote(block, block, ag_send.at[4 + k], ag_recv.at[4 + k], dev(ring_tile(a, second))))
    for copy in ag_a:
        copy.start()

    for copy in sm_z:
        copy.wait_recv()
    sm_y = small_stage(
        small_y, sum(small_z[k] for k in range(n_z)), at_yh, 2, 8, lambda yh: tile_at(yh, at_z, at_x, core)
    )
    lax.fori_loop(row_steps // 2, row_steps, input_edges, 0)

    for copy in ag_a:
        copy.wait_recv()
    ag_core = remote(total.at[core], total.at[core], ag_send.at[7], ag_recv.at[7], core_peer)
    ag_core.start()

    @pl.when(core == 0)
    def _():
        up_sum_ref[...] = total[0].astype(F32) * q

    @pl.when(core == 1)
    def _():
        down_sum_ref[...] = total[1].astype(F32).T * q

    for copy in sm_y:
        copy.wait_recv()
    small = (small_y[0] + small_y[1]) * q
    for a in range(KERNEL):
        taps_ref[a] = small[a * KERNEL : (a + 1) * KERNEL]
    gain_ref[...] = small[n_taps : n_taps + 1].reshape(LANES)
    scale_sum_ref[...] = small[n_taps + 1 : n_taps + 2].reshape(LANES)
    for i in range(4):
        bias_sum_ref[i * LANES : (i + 1) * LANES] = small[n_taps + 2 + i : n_taps + 3 + i].reshape(LANES)
    ag_core.wait_recv()

    @pl.when(core == 1)
    def _():
        up_sum_ref[...] = total[0].astype(F32) * q

    @pl.when(core == 0)
    def _():
        down_sum_ref[...] = total[1].astype(F32).T * q

    for copy in weight_copies + forwards + first_halo + last_halo + [pars_copy, rs_core, small_chan, sm_core, ag_y, ag_core]:
        copy.wait_send()
    for copy in rs_a + rs_b + rs_y + ag_a + ag_b + sm_x + sm_z + sm_y:
        copy.wait_send()

    def finish(k, _):
        grad_copy(k).wait_send()
        y_copy(k).wait_send()
        conv_copy(k).wait_send()
        return 0

    lax.fori_loop(0, steps, finish, 0)


SHAPES = {64: (2, 4, 4, 2), 16: (2, 2, 2, 2)}


def hand_over(*refs):
    count = (len(refs) - 1) // 2
    sems = refs[-1]
    copies = [pltpu.make_async_copy(refs[n], refs[count + n], sems.at[n]) for n in range(count)]
    for copy in copies:
        copy.start()
    for copy in copies:
        copy.wait()


def place(results):
    hbm = pl.BlockSpec(memory_space=pl.ANY)
    return pl.pallas_call(
        hand_over,
        out_shape=tuple(jax.ShapeDtypeStruct(r.shape, r.dtype) for r in results),
        in_specs=[hbm] * len(results),
        out_specs=(hbm,) * len(results),
        scratch_shapes=[pltpu.SemaphoreType.DMA((len(results),))],
    )(*results)


def block_call(inputs, cotangent, wet, neighbours, depth_weight, gamma, up_weight, up_bias, down_weight, layer_scale):
    side = inputs.shape[1]
    half_chan = inputs.shape[3]
    flat = (side * side, half_chan)
    shape4 = SHAPES[lax.axis_size("tiles")]
    n_yh, n_z, n_x, n_core = shape4
    width = side + 16
    cells = side * side // 2
    row_steps = side // ROWS
    steps = row_steps // 2
    a_rows = CHAN // n_x
    vmem = pltpu.VMEM
    whole = pl.BlockSpec(memory_space=pltpu.VMEM)
    hbm = pl.BlockSpec(memory_space=pl.ANY)
    dma = pltpu.SemaphoreType.DMA
    padded = vmem(((side + 2 * MARGIN) * width, LANES), F32)
    taps = vmem((KERNEL * KERNEL * 8, LANES), F32)
    piece = vmem((cells, LANES), BF16)
    small = vmem((64, LANES), F32)
    pars = vmem((8, HALF_HIDDEN), F32)
    tile = vmem((side * side, LANES), BF16)
    scratch = [
        vmem((LANES, LANES), F32), tile, tile, dma((4,)),
        padded, padded, taps, taps,
        vmem((4, MARGIN * side, LANES), BF16),
        vmem((2, MARGIN * 16, LANES), BF16),
        vmem((2, 2, 4, MARGIN * side, LANES), BF16),
        vmem((2, 2, MARGIN * side, LANES), BF16),
        vmem((2, 2, MARGIN * 16, LANES), BF16),
        vmem((2, CHAN, HALF_HIDDEN), BF16),
        vmem((2, HALF_HIDDEN, CHAN), BF16),
        pars, pars,
        tile, vmem((LANES, LANES), F32),
        piece, tile, piece, piece, piece,
        vmem((2, CHAN, HIDDEN), F32),
        vmem((8, CHAN), F32),
        vmem((8, HIDDEN), F32),
        vmem((CHAN, HIDDEN), BF16), vmem((CHAN, HIDDEN), BF16), vmem((CHAN, HIDDEN), BF16),
        vmem((n_x - 1, a_rows, HIDDEN), BF16),
        vmem((n_x - 1, a_rows // n_z, HIDDEN), F32),
        vmem((3, a_rows // n_z, HALF_HIDDEN // 2), F32),
        vmem((2, CHAN, HALF_HIDDEN), BF16),
        small, vmem((8, LANES), F32), vmem((8, LANES), F32), small,
        vmem((n_x, 64, LANES), F32), vmem((n_z, 64, LANES), F32), vmem((2, 64, LANES), F32),
        dma((2, 12)), dma((2, 12)), dma((7,)), dma((7,)),
        dma((steps,)), dma((steps,)), dma((steps,)), dma((steps,)), dma((steps,)), dma((steps,)),
        dma((10,)), dma((10,)), dma((8,)), dma((8,)), dma((9,)), dma((9,)),
    ]
    return pl.pallas_call(
        functools.partial(kernel, side, shape4),
        out_shape=(
            jax.ShapeDtypeStruct(flat, BF16),
            jax.ShapeDtypeStruct((KERNEL, KERNEL, LANES), F32),
            jax.ShapeDtypeStruct((LANES,), F32),
            jax.ShapeDtypeStruct((CHAN, HALF_HIDDEN), F32),
            jax.ShapeDtypeStruct((HALF_HIDDEN,), F32),
            jax.ShapeDtypeStruct((HALF_HIDDEN, CHAN), F32),
            jax.ShapeDtypeStruct((LANES,), F32),
        ),
        in_specs=[whole, hbm, hbm, whole, whole, whole, hbm, whole, hbm, whole],
        out_specs=(whole, whole, whole, whole, whole, whole, whole),
        scratch_shapes=scratch,
        compiler_params=pltpu.CompilerParams(
            collective_id=0, has_side_effects=True, vmem_limit_bytes=60 * 1024 * 1024
        ),
    )(
        neighbours.T,
        inputs.reshape(flat),
        cotangent.reshape(flat),
        wet[0],
        depth_weight,
        gamma,
        up_weight,
        up_bias,
        down_weight,
        layer_scale,
    )


def body(
    inputs,
    cotangent,
    wet,
    neighbours,
    depth_weight,
    gamma,
    up_weight,
    up_bias,
    down_weight,
    layer_scale,
):
    results = block_call(
        inputs, cotangent, wet, neighbours, depth_weight, gamma, up_weight, up_bias, down_weight, layer_scale
    )
    grad, *sums = place(results)
    return (grad.reshape(inputs.shape), *sums)


def solution(mesh):
    return jax.shard_map(
        body,
        mesh=mesh,
        in_specs=(
            P("tiles", None, None, "chan"),
            P("tiles", None, None, "chan"),
            P("tiles", None, None),
            P(),
            P(None, None, "chan"),
            P("chan"),
            P(None, "chan"),
            P("chan"),
            P("chan", None),
            P("chan"),
        ),
        out_specs=(
            P("tiles", None, None, "chan"),
            P(None, None, "chan"),
            P("chan"),
            P(None, "chan"),
            P("chan"),
            P("chan", None),
            P("chan"),
        ),
        check_vma=False,
    )
```

```python
import functools
import math

import jax
import jax.numpy as jnp
from jax import lax
from jax.experimental import pallas as pl
from jax.experimental.pallas import tpu as pltpu
from jax.sharding import PartitionSpec as P

KERNEL = 7
MARGIN = 3
LANES = 128
CHAN = 256
HIDDEN = 1024
HALF_HIDDEN = 512
BLOCK = 256
ROWS = 8
COLS = 2
REACH = 5
F32 = jnp.float32
BF16 = jnp.bfloat16
MESH = pl.DeviceIdType.MESH
density = 0.3989422804014327
half_log2 = -0.7213475204444817


def gelu_pieces(hidden):
    size = jnp.abs(hidden)
    denom = 1.0 + 0.2316419 * size
    inverse = pl.reciprocal(denom, approx=True)
    inverse = inverse * (2.0 - denom * inverse)
    bell = jnp.exp2(hidden * hidden * half_log2)
    poly = 0.5 * 1.061405429
    for factor in (-1.453152027, 1.421413741, -0.284496736, 0.254829592):
        poly = poly * inverse + 0.5 * factor
    tail = poly * inverse * bell
    normal_cdf = jnp.where(hidden >= 0.0, 1.0 - tail, tail)
    activated = hidden * normal_cdf
    slope = normal_cdf + hidden * bell * density
    return activated, slope


def nn(a, b):
    return lax.dot_general(a, b, (((1,), (0,)), ((), ())), preferred_element_type=F32)


def nt(a, b):
    return lax.dot_general(a, b, (((1,), (1,)), ((), ())), preferred_element_type=F32)


def kernel(
    side, shape4,
    links_in, x_in, c_in, wet_ref, depth_ref, gamma_ref, up_ref, bias_ref, down_ref, scale_ref,
    out_ref, taps_ref, gain_ref, up_sum_ref, bias_sum_ref, down_sum_ref, scale_sum_ref,
    links, x_ref, c_ref, load_sem,
    pf, pg, taps, taps_acc, strips, corners, rows_in, cols_in, corners_in,
    wu, wd, pars, pars_in,
    mask_ref, wet_turned, grad_in, y_all, y_in, conv_send, conv_in,
    sums, gamma_acc, bias_acc, core_out, ring_out, ring_core, ring_a, ring_b, ring_y, total,
    small_a, small_peer, small_peer_in, small_core, small_x, small_z, small_y,
    halo_send, halo_recv, relay_send, weight_sem, weight_recv, grad_sem, grad_recv, y_sem, y_recv, conv_sem, conv_recv,
    rs_send, rs_recv, ag_send, ag_recv, sm_send, sm_recv,
):
    n_yh, n_z, n_x, n_core = shape4
    tiles = n_yh * n_z * n_x * n_core
    width = side + 16
    row_steps = side // ROWS
    steps = row_steps // 2
    chunk = ROWS * side
    me = lax.axis_index("tiles")
    h = lax.axis_index("chan")
    other = 1 - h
    core = me % n_core
    at_x = (me // n_core) % n_x
    at_z = (me // (n_core * n_x)) % n_z
    at_yh = me // (n_core * n_x * n_z)
    q = 1.0 / (side * math.sqrt(tiles))

    def tile_at(yh, z, x, c):
        return ((yh * n_z + z) * n_x + x) * n_core + c

    def dev(tile, chan=None):
        return {"tiles": tile, "chan": h if chan is None else chan}

    def remote(src, dst, send, recv, device):
        return pltpu.make_async_remote_copy(
            src_ref=src, dst_ref=dst, send_sem=send, recv_sem=recv, device_id=device, device_id_type=MESH
        )

    def line_at(which, k):
        return k + which * (row_steps - 1 - 2 * k)

    def chunk_rows(line):
        return pl.ds(pl.multiple_of(line * chunk, chunk), chunk)

    first = core * at_z + (1 - core) * at_x
    second = core * at_x + (1 - core) * at_z

    def ring_tile(a, b):
        return tile_at(at_yh, core * a + (1 - core) * b, core * b + (1 - core) * a, core)

    peer = dev(me, other)
    core_peer = dev(tile_at(at_yh, at_z, at_x, 1 - core))
    halo = [(sign, d) for sign in (1, -1) for d in range(1, REACH + 1)]

    def halo_tile(sign, d):
        return (me + sign * d + tiles) % tiles

    a_peers = [(first + k) % n_x for k in range(1, n_x)]
    b_peers = [(second + k) % n_x for k in range(1, n_x)]
    y_peers = [(0, 1), (1, 0), (1, 1)]

    def y_dev(dy, dc):
        return dev(tile_at((at_yh + dy) % 2, at_z, at_x, core), (h + dc) % 2)

    barrier = pltpu.get_barrier_semaphore()
    targets = [dev(halo_tile(s, d)) for s, d in halo]
    targets += [core_peer]
    targets += [dev(ring_tile(a, second)) for a in a_peers]
    targets += [dev(ring_tile(first, b)) for b in b_peers]
    targets += [y_dev(dy, dc) for dy, dc in y_peers]
    for target in targets:
        pl.semaphore_signal(barrier, inc=1, device_id=target, device_id_type=MESH)
    loads = [
        pltpu.make_async_copy(x_in, x_ref, load_sem.at[0]),
        pltpu.make_async_copy(c_in, c_ref, load_sem.at[1]),
        pltpu.make_async_copy(up_ref, wu.at[h], load_sem.at[2]),
        pltpu.make_async_copy(down_ref, wd.at[h], load_sem.at[3]),
    ]
    for copy in loads:
        copy.start()
    pars[...] = jnp.zeros_like(pars)
    pars[0:1, :] = bias_ref[...].astype(F32).reshape(1, HALF_HIDDEN)
    pars[1:2, 0:LANES] = gamma_ref[...].astype(F32).reshape(1, LANES)
    pars[2:3, 0:LANES] = scale_ref[...].astype(F32).reshape(1, LANES)
    links[...] = jnp.zeros_like(links)
    links[0:8, 0:tiles] = links_in[...].astype(F32)
    links[...] = links[...].T
    wet_turned[...] = jnp.zeros_like(wet_turned)
    wet_turned[0:side, 0:side] = wet_ref[...].astype(F32)
    wet_turned[...] = wet_turned[...].T
    pl.semaphore_wait(barrier, len(targets))

    diagonal = y_dev(1, 1)
    up_part, down_part = CHAN // 4, HALF_HIDDEN // 4

    def part(ref, size, at, count=1):
        return ref.at[pl.ds(pl.multiple_of(at * size, size), count * size), :]

    def weight_copy(n, device, quarter, slot):
        up = remote(
            part(up_ref, up_part, quarter), part(wu.at[slot], up_part, quarter),
            weight_sem.at[n], weight_recv.at[n], device,
        )
        down = remote(
            part(down_ref, down_part, quarter), part(wd.at[slot], down_part, quarter),
            weight_sem.at[n + 1], weight_recv.at[n + 1], device,
        )
        return [up, down]

    pars_copy = remote(pars, pars_in, weight_sem.at[0], weight_recv.at[0], peer)
    weight_copies = weight_copy(1, peer, 2 * core, h) + weight_copy(3, diagonal, 2 * core + 1, h)
    weight_arrivals = weight_copy(1, peer, 2 * core, other) + weight_copy(3, diagonal, 2 * core + 1, other)

    def weight_forward(half_at):
        return [
            remote(
                part(wu.at[other], up_part, 2 * half_at, 2), part(wu.at[other], up_part, 2 * half_at, 2),
                weight_sem.at[5], weight_recv.at[5], core_peer,
            ),
            remote(
                part(wd.at[other], down_part, 2 * half_at, 2), part(wd.at[other], down_part, 2 * half_at, 2),
                weight_sem.at[6], weight_recv.at[6], core_peer,
            ),
        ]

    pars_copy.start()
    for copy in weight_copies:
        copy.start()

    early = min(4, steps)

    def grad_copy(k):
        return remote(
            c_in.at[chunk_rows(line_at(other, k)), :], grad_in.at[chunk_rows(k), :],
            grad_sem.at[k], grad_recv.at[k], peer,
        )

    grad_copy(0).start()

    loads[0].wait()
    def fill_input(g, _):
        columns = pltpu.roll(wet_turned[0:side, :], (LANES - g * ROWS) % LANES, 1)
        for t in range(ROWS):
            i = g * ROWS + t
            at = pl.ds(pl.multiple_of(i * side, side), side)
            to = pl.multiple_of((i + MARGIN) * width + 8, 8)
            wet = jnp.broadcast_to(columns[:, t : t + 1], (side, LANES))
            mask_ref[at, :] = wet.astype(BF16)
            pf[pl.ds(to, side), :] = x_ref[at, :].astype(F32) * wet
        return 0

    lax.fori_loop(0, side // ROWS, fill_input, 0)

    def row_strips(padded):
        for side_at, row in enumerate((MARGIN, side)):
            for k in range(MARGIN):
                base = (row + k) * width + 8
                strips[side_at, k * side : (k + 1) * side, :] = padded[base : base + side, :].astype(BF16)
                near = base if side_at == 0 else base + side - 16
                corners[side_at, k * 16 : (k + 1) * 16, :] = padded[near : near + 16, :].astype(BF16)

    def col_strips(padded):
        for side_at, col in enumerate((8, 8 + side - MARGIN)):
            for k in range(MARGIN):
                line = padded[pl.ds(MARGIN * width + col + k, side, stride=width), :]
                strips[2 + side_at, k * side : (k + 1) * side, :] = line.astype(BF16)

    def halo_copy(src, dst, phase, n, sign, d):
        copy = remote(src, dst, halo_send.at[phase, n], halo_recv.at[phase, n], dev(halo_tile(sign, d)))
        to, source = me + sign * d, me - sign * d
        leaves = jnp.logical_and(to >= 0, to < tiles)
        comes = jnp.logical_and(source >= 0, source < tiles)
        return copy, dst, leaves, comes

    span = tiles // n_yh
    farthest = REACH - 1
    beyond = (me - span, span - 1 - me)

    def hands_on(way, steps_back):
        return jnp.logical_and(beyond[way] >= steps_back, beyond[way] < farthest)

    def crosses(sign, d):
        return (me + sign * d + tiles) // span != (me + tiles) // span

    def row_copy(phase, n, sign, d, way):
        copy, dst, leaves, comes = halo_copy(strips.at[1 - way], rows_in.at[phase, way, d - 1], phase, n, sign, d)
        if d < farthest:
            leaves = jnp.logical_and(leaves, jnp.logical_not(crosses(sign, d)))
        return copy, dst, leaves, comes

    def row_copies(phase):
        copies = []
        for n, (sign, d) in enumerate(halo):
            way = 0 if sign > 0 else 1
            if d < REACH:
                copies.append(row_copy(phase, n, sign, d, way))
            else:
                copies.append(halo_copy(corners.at[1 - way], corners_in.at[phase, way], phase, n, sign, d))
        return copies

    def col_copies(phase):
        copies = []
        for way, sign in enumerate((1, -1)):
            copies.append(halo_copy(strips.at[3 - way], cols_in.at[phase, way], phase, len(halo) + way, sign, 1))
        return copies

    def halo_start(copies):
        for copy, _, leaves, _ in copies:
            pl.when(leaves)(copy.start)

    def rows_start(copies, crossing):
        for (sign, d), (copy, _, leaves, _) in zip(halo, copies):
            over = crosses(sign, d)
            pl.when(jnp.logical_and(leaves, over if crossing else jnp.logical_not(over)))(copy.start)

    def relay_copies(phase, way):
        sign = 1 - 2 * way
        return [
            remote(
                rows_in.at[phase, way, farthest - 1], rows_in.at[phase, way, farthest - i - 1],
                relay_send.at[phase, i - 1], halo_recv.at[phase, way * REACH + farthest - i - 1],
                dev(halo_tile(-sign, i)),
            )
            for i in range(1, farthest)
        ]

    def relay(phase):
        for way in range(2):

            @pl.when(hands_on(way, 1))
            def _(way=way):
                row_copies(phase)[way * REACH + farthest - 1][0].wait_recv()

            for i, copy in enumerate(relay_copies(phase, way)):
                pl.when(hands_on(way, i + 1))(copy.start)

    def relay_left(phase):
        for way in range(2):
            for i, copy in enumerate(relay_copies(phase, way)):
                pl.when(hands_on(way, i + 1))(copy.wait_send)

    def halo_arrive(copies):
        for n, (copy, dst, _, comes) in enumerate(copies):
            waits = comes
            if n < len(halo) and n % REACH == farthest - 1:
                waits = jnp.logical_and(comes, jnp.logical_not(hands_on(n // REACH, 1)))
            pl.when(waits)(copy.wait_recv)

            @pl.when(jnp.logical_not(comes))
            def _(dst=dst):
                dst[...] = jnp.zeros(dst.shape, BF16)

    def halo_left(copies):
        for copy, _, leaves, _ in copies:
            pl.when(leaves)(copy.wait_send)

    def match(direction, source):
        link = links[pl.ds(me, 1), direction : direction + 1]
        return jnp.where(jnp.logical_and(link == lax.convert_element_type(source, F32), link >= 0.0), 1.0, 0.0)

    def fill_halo(padded, phase):
        for way, sign in enumerate((-1, 1)):
            straight, left, right, beside = ((0, 4, 5, 2), (1, 6, 7, 3))[way]
            row = 0 if way == 0 else side + MARGIN
            straight_hit = [match(straight, me + sign * d) for d in range(1, 5)]
            left_hit = [match(left, me + sign * d) for d in range(1, 6)]
            right_hit = [match(right, me + sign * d) for d in range(1, 6)]
            far_hit = left_hit[4] if way == 0 else right_hit[4]
            for k in range(MARGIN):
                base = (row + k) * width
                lines = [rows_in[phase, way, d, k * side : (k + 1) * side, :].astype(F32) for d in range(4)]
                far = corners_in[phase, way, k * 16 : (k + 1) * 16, :].astype(F32)
                middle = sum(hit * line for hit, line in zip(straight_hit, lines))
                west = sum(hit * line[side - 8 :] for hit, line in zip(left_hit[:4], lines))
                east = sum(hit * line[:8] for hit, line in zip(right_hit[:4], lines))
                if way == 0:
                    west = west + far_hit * far[8:]
                else:
                    east = east + far_hit * far[:8]
                padded[base : base + 8, :] = west
                padded[base + 8 : base + 8 + side, :] = middle
                padded[base + 8 + side : base + 16 + side, :] = east
            hit = match(beside, me + sign)
            col = 8 - MARGIN if way == 0 else 8 + side
            for k in range(MARGIN):
                line = cols_in[phase, way, k * side : (k + 1) * side, :].astype(F32)
                padded[pl.ds(MARGIN * width + col + k, side, stride=width), :] = line * hit

    row_strips(pf)
    col_strips(pf)
    forward_halo = row_copies(0) + col_copies(0)
    halo_start(forward_halo)
    for k in range(1, early):
        grad_copy(k).start()

    for a in range(KERNEL):
        for b in range(KERNEL):
            n = (a * KERNEL + b) * 8
            taps[n : n + 8, :] = jnp.broadcast_to(depth_ref[a, b : b + 1, :], (8, LANES))

    def conv_block(padded, row, col, flip):
        base = row * width + col + 8 - MARGIN
        acc = [[None] * COLS for _ in range(ROWS)]
        for b in range(KERNEL):
            weights = []
            for a in range(KERNEL):
                n = a * KERNEL + b
                n = (KERNEL * KERNEL - 1 - n if flip else n) * 8
                weights.append(taps[n : n + 8, :])
            for r in range(ROWS + KERNEL - 1):
                for v in range(COLS):
                    value = padded[pl.ds(base + (r * width + v * 8 + b), 8), :]
                    for a in range(KERNEL):
                        i = r - a
                        if 0 <= i < ROWS:
                            term = value * weights[a]
                            acc[i][v] = term if acc[i][v] is None else acc[i][v] + term
        return acc

    col_steps = side // (8 * COLS)

    def filter_forward(k, c):
        col = pl.multiple_of(c * (8 * COLS), 8 * COLS)
        acc = conv_block(pf, k * ROWS, col, False)
        for i in range(ROWS):
            at = pl.multiple_of((k * ROWS + i) * side + col, 8 * COLS)
            y_all[pl.ds(at, 8 * COLS), :] = jnp.concatenate(acc[i], 0).astype(BF16)

    def conv_inner(n, _):
        filter_forward(1 + n // (col_steps - 2), 1 + n % (col_steps - 2))
        return 0

    inner = (row_steps - 2) * (col_steps - 2)
    lax.fori_loop(0, inner // 2, conv_inner, 0)
    relay(0)
    lax.fori_loop(inner // 2, inner, conv_inner, 0)
    for copy in weight_arrivals:
        copy.wait_recv()
    forwards = weight_forward(core)
    for copy in forwards:
        copy.start()
    halo_arrive(forward_halo)
    fill_halo(pf, 0)

    def y_copy(k):
        return remote(
            y_all.at[chunk_rows(line_at(other, k)), :], y_in.at[chunk_rows(k), :], y_sem.at[k], y_recv.at[k], peer
        )

    def conv_outer(n, _):
        away = n < steps
        k = jnp.where(away, line_at(other, n), line_at(h, n - steps))
        edge = jnp.logical_or(k == 0, k == row_steps - 1)

        def one(c, _):
            filter_forward(k, jnp.where(edge, c, c * (col_steps - 1)))
            return 0

        lax.fori_loop(0, jnp.where(edge, col_steps, 2), one, 0)

        @pl.when(away)
        def _():
            y_copy(n).start()

        @pl.when(jnp.logical_and(n + 1 >= early, n + 1 < steps))
        def _():
            grad_copy(n + 1).start()

        return 0

    lax.fori_loop(0, row_steps, conv_outer, 0)

    pars_copy.wait_recv()
    for copy in weight_forward(1 - core):
        copy.wait_recv()
    for copy in loads[1:4]:
        copy.wait()
    halo_left(forward_halo)
    mine = h == 0

    def ordered(own, others):
        return jnp.where(mine, own, others), jnp.where(mine, others, own)

    def row_of(n):
        own, others = pars[n : n + 1, 0:LANES], pars_in[n : n + 1, 0:LANES]
        return jnp.concatenate(ordered(own, others), 1)

    gamma_row = row_of(1)
    scale_row = row_of(2)
    bias_rows = ordered(pars[0:1, :], pars_in[0:1, :])

    sums[...] = jnp.zeros_like(sums)
    gamma_acc[...] = jnp.zeros_like(gamma_acc)
    bias_acc[...] = jnp.zeros_like(bias_acc)
    taps_acc[...] = jnp.zeros_like(taps_acc)

    def conv_copy(k):
        at = chunk_rows(k)
        return remote(conv_send.at[at, :], conv_in.at[at, :], conv_sem.at[k], conv_recv.at[k], peer)

    def take_conv(k):
        conv_copy(k).wait_recv()
        for i in range(ROWS):
            at = pl.multiple_of((k * ROWS + i) * side, side)
            to = pl.multiple_of((MARGIN + line_at(other, k) * ROWS + i) * width + 8, 8)
            pg[pl.ds(to, side), :] = conv_in[pl.ds(at, side), :].astype(F32)

    def filter_line(line):
        row = line * ROWS

        def one(c, _):
            col = c * (8 * COLS)
            inner = (row + MARGIN) * width + col + 8
            base = row * width + col + 8 - MARGIN
            grads = [
                [pg[pl.ds(pl.multiple_of(inner, 8) + (i * width + v * 8), 8), :] for v in range(COLS)] for i in range(ROWS)
            ]
            for b in range(KERNEL):
                acc = [None] * KERNEL
                for r in range(ROWS + KERNEL - 1):
                    for v in range(COLS):
                        value = pf[pl.ds(base + (r * width + v * 8 + b), 8), :]
                        for a in range(KERNEL):
                            i = r - a
                            if 0 <= i < ROWS:
                                term = value * grads[i][v]
                                acc[a] = term if acc[a] is None else acc[a] + term
                for a in range(KERNEL):
                    n = (a * KERNEL + b) * 8
                    taps_acc[n : n + 8, :] += acc[a]
            return 0

        lax.fori_loop(0, col_steps, one, 0)

    def mlp(k, _):
        at = chunk_rows(k)
        line = line_at(h, k)
        own_at = chunk_rows(line)
        y_copy(k).wait_recv()
        grad_copy(k).wait_recv()
        low, high = ordered(y_all[own_at, :].astype(F32), y_in[at, :].astype(F32))
        y = jnp.concatenate((low, high), 1)
        centred = y - jnp.sum(y, 1, keepdims=True) * (1.0 / CHAN)
        spread = jnp.sum(centred * centred, 1, keepdims=True) * (1.0 / CHAN)
        inv_spread = lax.rsqrt(spread + 1e-06)
        unit = centred * inv_spread
        normed = (unit * gamma_row).astype(BF16)
        wet = mask_ref[own_at, :].astype(F32)
        low, high = ordered(c_ref[own_at, :].astype(F32), grad_in[at, :].astype(F32))
        branch_grad = (jnp.concatenate((low * wet, high * wet), 1) * scale_row).astype(BF16)
        branch_t = branch_grad.T
        normed_t = jnp.concatenate((normed.T, jnp.ones((16, chunk), BF16)), 0)
        norm_grad = jnp.zeros((chunk, CHAN), F32)
        for block in range(HIDDEN // BLOCK):
            slot, off = divmod(block * BLOCK, HALF_HIDDEN)
            w_up = wu[slot, :, off : off + BLOCK]
            w_down = wd[slot, off : off + BLOCK, :]
            cols = slice(block * BLOCK, (block + 1) * BLOCK)
            hidden = nn(normed, w_up) + bias_rows[slot][:, off : off + BLOCK]
            activated, slope = gelu_pieces(hidden)
            hidden_grad = (nt(branch_grad, w_down) * slope).astype(BF16)
            sums[1, :, cols] += nn(branch_t, activated.astype(BF16))
            up_terms = nn(normed_t, hidden_grad)
            sums[0, :, cols] += up_terms[:CHAN]
            bias_acc[:, cols] += up_terms[CHAN : CHAN + 8]
            norm_grad = norm_grad + nt(hidden_grad, w_up)
        gamma_acc[...] += jnp.sum((norm_grad * unit).reshape(chunk // 8, 8, CHAN), 0)
        scaled = norm_grad * gamma_row
        mean = jnp.sum(scaled, 1, keepdims=True) * (1.0 / CHAN)
        tilt = jnp.sum(scaled * unit, 1, keepdims=True) * (1.0 / CHAN)
        conv_grad = (inv_spread * (scaled - mean - unit * tilt)).astype(BF16).astype(F32)
        own, away = ordered(conv_grad[:, :LANES], conv_grad[:, LANES:])
        conv_send[at, :] = away.astype(BF16)
        conv_copy(k).start()
        for i in range(ROWS):
            to = pl.multiple_of((MARGIN + line * ROWS + i) * width + 8, 8)
            pg[pl.ds(to, side), :] = own[i * side : (i + 1) * side]
        filter_line(line)

        @pl.when(k == steps - 2)
        def _():
            take_conv(0)
            row_strips(pg)
            rows_start(row_copies(1), False)

        @pl.when(k == steps - 1)
        def _():
            rows_start(row_copies(1), True)

        return 0

    lax.fori_loop(0, steps, mlp, 0)

    core_out[...] = sums[1 - core].astype(BF16)
    rs_core = remote(core_out, ring_core, rs_send.at[0], rs_recv.at[0], core_peer)
    rs_core.start()

    ident = lax.broadcasted_iota(jnp.int32, (CHAN, CHAN), 0) == lax.broadcasted_iota(jnp.int32, (CHAN, CHAN), 1)
    down_sums = sums[1]
    down_high = down_sums.astype(BF16)
    down_low = (down_sums - down_high.astype(F32)).astype(BF16)
    paired = jnp.zeros((CHAN, CHAN), F32)
    for slot in range(2):
        cols = slice(slot * HALF_HIDDEN, (slot + 1) * HALF_HIDDEN)
        paired = paired + nn(down_high[:, cols], wd[slot]) + nn(down_low[:, cols], wd[slot])
    scale_sum = jnp.sum(jnp.where(ident, paired, 0.0), 0, keepdims=True) / scale_row
    gamma_sum = jnp.sum(gamma_acc[...], 0, keepdims=True)
    bias_sum = bias_acc[0:1, :]
    small_peer[...] = jnp.zeros_like(small_peer)
    small_a[...] = jnp.zeros_like(small_a)
    n_taps = KERNEL * KERNEL

    def put_small(ref, at, value, n):
        own, away = ordered(value[:, : n * LANES], value[:, n * LANES :])
        for i in range(n):
            ref[0][ref[1] + at + i : ref[1] + at + i + 1, :] = own[:, i * LANES : (i + 1) * LANES]
            small_peer[at + i : at + i + 1, :] = away[:, i * LANES : (i + 1) * LANES]

    place = (small_a, n_taps)
    put_small(place, 0, gamma_sum, 1)
    put_small(place, 1, scale_sum, 1)
    put_small(place, 2, bias_sum, 4)
    small_chan = remote(small_peer, small_peer_in, sm_send.at[0], sm_recv.at[0], peer)
    small_chan.start()

    def input_block(line, c):
        row = line * ROWS
        col = pl.multiple_of(c * (8 * COLS), 8 * COLS)
        acc = conv_block(pg, row, col, True)
        for i in range(ROWS):
            at = pl.ds(pl.multiple_of((row + i) * side + col, 8 * COLS), 8 * COLS)
            wet = mask_ref[at, :].astype(F32)
            grad = c_ref[at, :].astype(F32)
            out_ref[at, :] = (wet * (grad + jnp.concatenate(acc[i], 0))).astype(BF16)

    inner_cols = col_steps - 2

    def own_inner(n, _):
        input_block(line_at(h, 1 + n // inner_cols), 1 + n % inner_cols)
        return 0

    def rest_inner(n, _):
        k = 1 + n // inner_cols
        input_block(jnp.where(k == steps, line_at(h, steps - 1), line_at(other, k)), 1 + n % inner_cols)
        return 0

    def input_edges(k, _):
        edge = jnp.logical_or(k == 0, k == row_steps - 1)

        def one(c, _):
            input_block(k, jnp.where(edge, c, c * (col_steps - 1)))
            return 0

        lax.fori_loop(0, jnp.where(edge, col_steps, 2), one, 0)
        return 0

    def peer_line(k, _):
        @pl.when(k > 0)
        def _():
            take_conv(k)

        filter_line(line_at(other, k))
        return 0

    own = (steps - 2) * inner_cols
    lax.fori_loop(0, own // 2, own_inner, 0)
    lax.fori_loop(0, 1, peer_line, 0)

    rs_core.wait_recv()
    sums[core] = sums[core] + ring_core[...].astype(F32)
    ring_out[...] = sums[core].astype(BF16)
    a_rows, b_rows, y_cols = CHAN // n_x, CHAN // n_x // n_z, HALF_HIDDEN // 2
    rs_a = []
    for k, a in enumerate(a_peers):
        piece = ring_out.at[pl.ds(pl.multiple_of(a * a_rows, a_rows), a_rows), :]
        rs_a.append(remote(piece, ring_a.at[k], rs_send.at[1 + k], rs_recv.at[1 + k], dev(ring_tile(a, second))))
    for copy in rs_a:
        copy.start()

    lax.fori_loop(own // 2, own, own_inner, 0)
    lax.fori_loop(1, steps - 2, peer_line, 0)

    for copy in rs_a:
        copy.wait_recv()
    a_at = pl.ds(pl.multiple_of(first * a_rows, a_rows), a_rows)
    sums[core, a_at, :] = sums[core, a_at, :] + sum(ring_a[k].astype(F32) for k in range(n_x - 1))
    rs_b = []
    for k, b in enumerate(b_peers):
        piece = sums.at[core, pl.ds(pl.multiple_of(first * a_rows + b * b_rows, b_rows), b_rows), :]
        rs_b.append(remote(piece, ring_b.at[k], rs_send.at[4 + k], rs_recv.at[4 + k], dev(ring_tile(first, b))))
    for copy in rs_b:
        copy.start()

    relay(1)
    lax.fori_loop(steps - 2, steps - 1, peer_line, 0)
    rest = steps * inner_cols
    lax.fori_loop(0, rest // 2, rest_inner, 0)

    for copy in rs_b:
        copy.wait_recv()
    b_start = first * a_rows + second * b_rows
    b_at = pl.ds(pl.multiple_of(b_start, b_rows), b_rows)
    sums[core, b_at, :] = sums[core, b_at, :] + sum(ring_b[k] for k in range(n_x - 1))

    def y_span(yh):
        return pl.ds(pl.multiple_of(yh * y_cols, y_cols), y_cols)

    def y_piece(yh, chan):
        return (core, b_at, pl.ds(pl.multiple_of(chan * HALF_HIDDEN + yh * y_cols, y_cols), y_cols))

    rs_y = []
    for k, (dy, dc) in enumerate(y_peers):
        piece = sums.at[y_piece((at_yh + dy) % 2, (h + dc) % 2)]
        rs_y.append(remote(piece, ring_y.at[k], rs_send.at[7 + k], rs_recv.at[7 + k], y_dev(dy, dc)))
    for copy in rs_y:
        copy.start()

    take_conv(steps - 1)
    col_strips(pg)
    last_halo = col_copies(1)
    halo_start(last_halo)
    filter_line(line_at(other, steps - 1))

    for n in range(n_taps):
        small_a[n : n + 1, :] = jnp.sum(taps_acc[n * 8 : n * 8 + 8, :], 0, keepdims=True)
    small_chan.wait_recv()
    for n in range(6):
        small_a[n_taps + n : n_taps + n + 1, :] += small_peer_in[n : n + 1, :]
    sm_core = remote(small_a, small_core, sm_send.at[1], sm_recv.at[1], core_peer)
    sm_core.start()

    lax.fori_loop(rest // 2, rest, rest_inner, 0)

    for copy in rs_y:
        copy.wait_recv()
    y_block = total.at[core, b_at, y_span(at_yh)]
    y_block[...] = (sums[y_piece(at_yh, h)] + (ring_y[0] + ring_y[1] + ring_y[2])).astype(BF16)
    y_mate = dev(tile_at((at_yh + 1) % 2, at_z, at_x, core))
    ag_y = remote(y_block, y_block, ag_send.at[0], ag_recv.at[0], y_mate)
    ag_y.start()

    sm_core.wait_recv()

    def small_stage(ref, value, at, size, base, tile):
        ref[at] = value
        copies = []
        for k in range(1, size):
            there = (at + k) % size
            copies.append(
                remote(ref.at[at], ref.at[at], sm_send.at[base + k - 1], sm_recv.at[base + k - 1], dev(tile(there)))
            )
        for copy in copies:
            copy.start()
        return copies

    sm_x = small_stage(
        small_x, small_a[...] + small_core[...], at_x, n_x, 2, lambda x: tile_at(at_yh, at_z, x, core)
    )
    first_halo = row_copies(1)
    halo_arrive(first_halo + last_halo)
    fill_halo(pg, 1)
    marks = [row_steps * n // 4 for n in range(5)]
    lax.fori_loop(marks[0], marks[1], input_edges, 0)

    ag_y.wait_recv()
    ag_b = []
    for k, b in enumerate(b_peers):
        block = total.at[core, b_at, :]
        ag_b.append(remote(block, block, ag_send.at[1 + k], ag_recv.at[1 + k], dev(ring_tile(first, b))))
    for copy in ag_b:
        copy.start()

    lax.fori_loop(marks[1], marks[2], input_edges, 0)

    for copy in sm_x:
        copy.wait_recv()
    sm_z = small_stage(
        small_z, sum(small_x[k] for k in range(n_x)), at_z, n_z, 5, lambda z: tile_at(at_yh, z, at_x, core)
    )
    lax.fori_loop(marks[2], marks[3], input_edges, 0)

    for copy in ag_b:
        copy.wait_recv()
    ag_a = []
    for k, a in enumerate(a_peers):
        block = total.at[core, a_at, :]
        ag_a.append(remote(block, block, ag_send.at[4 + k], ag_recv.at[4 + k], dev(ring_tile(a, second))))
    for copy in ag_a:
        copy.start()

    lax.fori_loop(marks[3], marks[4], input_edges, 0)

    for copy in sm_z:
        copy.wait_recv()
    sm_y = small_stage(
        small_y, sum(small_z[k] for k in range(n_z)), at_yh, 2, 8, lambda yh: tile_at(yh, at_z, at_x, core)
    )
    for copy in ag_a:
        copy.wait_recv()
    ag_core = remote(total.at[core], total.at[core], ag_send.at[7], ag_recv.at[7], core_peer)
    ag_core.start()

    @pl.when(core == 0)
    def _():
        up_sum_ref[...] = total[0].astype(F32) * q

    @pl.when(core == 1)
    def _():
        down_sum_ref[...] = total[1].astype(F32).T * q

    for copy in sm_y:
        copy.wait_recv()
    small = (small_y[0] + small_y[1]) * q
    for a in range(KERNEL):
        taps_ref[a] = small[a * KERNEL : (a + 1) * KERNEL]
    gain_ref[...] = small[n_taps : n_taps + 1].reshape(LANES)
    scale_sum_ref[...] = small[n_taps + 1 : n_taps + 2].reshape(LANES)
    for i in range(4):
        bias_sum_ref[i * LANES : (i + 1) * LANES] = small[n_taps + 2 + i : n_taps + 3 + i].reshape(LANES)
    ag_core.wait_recv()

    @pl.when(core == 1)
    def _():
        up_sum_ref[...] = total[0].astype(F32) * q

    @pl.when(core == 0)
    def _():
        down_sum_ref[...] = total[1].astype(F32).T * q

    halo_left(first_halo + last_halo)
    relay_left(0)
    relay_left(1)
    for copy in weight_copies + forwards + [pars_copy, rs_core, small_chan, sm_core, ag_y, ag_core]:
        copy.wait_send()
    for copy in rs_a + rs_b + rs_y + ag_a + ag_b + sm_x + sm_z + sm_y:
        copy.wait_send()

    def finish(k, _):
        grad_copy(k).wait_send()
        y_copy(k).wait_send()
        conv_copy(k).wait_send()
        return 0

    lax.fori_loop(0, steps, finish, 0)


SHAPES = {64: (2, 4, 4, 2), 16: (2, 2, 2, 2)}


def hand_over(*refs):
    count = len(refs) // 2
    for source, result in zip(refs[:count], refs[count:]):
        result[...] = source[...]


def place(results):
    whole = pl.BlockSpec(memory_space=pltpu.VMEM)
    return pl.pallas_call(
        hand_over,
        out_shape=tuple(jax.ShapeDtypeStruct(r.shape, r.dtype) for r in results),
        in_specs=[whole] * len(results),
        out_specs=(whole,) * len(results),
    )(*results)


def block_call(inputs, cotangent, wet, neighbours, depth_weight, gamma, up_weight, up_bias, down_weight, layer_scale):
    side = inputs.shape[1]
    half_chan = inputs.shape[3]
    flat = (side * side, half_chan)
    shape4 = SHAPES[lax.axis_size("tiles")]
    n_yh, n_z, n_x, n_core = shape4
    width = side + 16
    cells = side * side // 2
    row_steps = side // ROWS
    steps = row_steps // 2
    a_rows = CHAN // n_x
    vmem = pltpu.VMEM
    whole = pl.BlockSpec(memory_space=pltpu.VMEM)
    hbm = pl.BlockSpec(memory_space=pl.ANY)
    dma = pltpu.SemaphoreType.DMA
    padded = vmem(((side + 2 * MARGIN) * width, LANES), F32)
    taps = vmem((KERNEL * KERNEL * 8, LANES), F32)
    piece = vmem((cells, LANES), BF16)
    small = vmem((64, LANES), F32)
    pars = vmem((8, HALF_HIDDEN), F32)
    tile = vmem((side * side, LANES), BF16)
    scratch = [
        vmem((LANES, LANES), F32), tile, tile, dma((4,)),
        padded, padded, taps, taps,
        vmem((4, MARGIN * side, LANES), BF16),
        vmem((2, MARGIN * 16, LANES), BF16),
        vmem((2, 2, 4, MARGIN * side, LANES), BF16),
        vmem((2, 2, MARGIN * side, LANES), BF16),
        vmem((2, 2, MARGIN * 16, LANES), BF16),
        vmem((2, CHAN, HALF_HIDDEN), BF16),
        vmem((2, HALF_HIDDEN, CHAN), BF16),
        pars, pars,
        tile, vmem((LANES, LANES), F32),
        piece, tile, piece, piece, piece,
        vmem((2, CHAN, HIDDEN), F32),
        vmem((8, CHAN), F32),
        vmem((8, HIDDEN), F32),
        vmem((CHAN, HIDDEN), BF16), vmem((CHAN, HIDDEN), BF16), vmem((CHAN, HIDDEN), BF16),
        vmem((n_x - 1, a_rows, HIDDEN), BF16),
        vmem((n_x - 1, a_rows // n_z, HIDDEN), F32),
        vmem((3, a_rows // n_z, HALF_HIDDEN // 2), F32),
        vmem((2, CHAN, HALF_HIDDEN), BF16),
        small, vmem((8, LANES), F32), vmem((8, LANES), F32), small,
        vmem((n_x, 64, LANES), F32), vmem((n_z, 64, LANES), F32), vmem((2, 64, LANES), F32),
        dma((2, 12)), dma((2, 12)), dma((2, 3)), dma((7,)), dma((7,)),
        dma((steps,)), dma((steps,)), dma((steps,)), dma((steps,)), dma((steps,)), dma((steps,)),
        dma((10,)), dma((10,)), dma((8,)), dma((8,)), dma((9,)), dma((9,)),
    ]
    return pl.pallas_call(
        functools.partial(kernel, side, shape4),
        out_shape=(
            jax.ShapeDtypeStruct(flat, BF16),
            jax.ShapeDtypeStruct((KERNEL, KERNEL, LANES), F32),
            jax.ShapeDtypeStruct((LANES,), F32),
            jax.ShapeDtypeStruct((CHAN, HALF_HIDDEN), F32),
            jax.ShapeDtypeStruct((HALF_HIDDEN,), F32),
            jax.ShapeDtypeStruct((HALF_HIDDEN, CHAN), F32),
            jax.ShapeDtypeStruct((LANES,), F32),
        ),
        in_specs=[whole, hbm, hbm, whole, whole, whole, hbm, whole, hbm, whole],
        out_specs=(whole, whole, whole, whole, whole, whole, whole),
        scratch_shapes=scratch,
        compiler_params=pltpu.CompilerParams(
            collective_id=0, has_side_effects=True, vmem_limit_bytes=60 * 1024 * 1024
        ),
    )(
        neighbours.T,
        inputs.reshape(flat),
        cotangent.reshape(flat),
        wet[0],
        depth_weight,
        gamma,
        up_weight,
        up_bias,
        down_weight,
        layer_scale,
    )


def body(
    inputs,
    cotangent,
    wet,
    neighbours,
    depth_weight,
    gamma,
    up_weight,
    up_bias,
    down_weight,
    layer_scale,
):
    grad, *sums = block_call(
        inputs, cotangent, wet, neighbours, depth_weight, gamma, up_weight, up_bias, down_weight, layer_scale
    )
    return (grad.reshape(inputs.shape), *place(sums))


def solution(mesh):
    return jax.shard_map(
        body,
        mesh=mesh,
        in_specs=(
            P("tiles", None, None, "chan"),
            P("tiles", None, None, "chan"),
            P("tiles", None, None),
            P(),
            P(None, None, "chan"),
            P("chan"),
            P(None, "chan"),
            P("chan"),
            P("chan", None),
            P("chan"),
        ),
        out_specs=(
            P("tiles", None, None, "chan"),
            P(None, None, "chan"),
            P("chan"),
            P(None, "chan"),
            P("chan"),
            P("chan", None),
            P("chan"),
        ),
        check_vma=False,
    )
```

```python
import functools
import math

import jax
import jax.numpy as jnp
from jax import lax
from jax.experimental import pallas as pl
from jax.experimental.pallas import tpu as pltpu
from jax.sharding import PartitionSpec as P

KERNEL = 7
MARGIN = 3
LANES = 128
CHAN = 256
HIDDEN = 1024
HALF_HIDDEN = 512
BLOCK = 256
ROWS = 8
COLS = 2
REACH = 5
F32 = jnp.float32
BF16 = jnp.bfloat16
MESH = pl.DeviceIdType.MESH
half_log2 = -0.7213475204444817
log2_density = -0.3257480647361593
rise_fit = (
    0.7978803240566237, 0.036352056236426934, -5.1744776236202565e-05, -4.809871843393557e-05,
    2.8097794756336268e-06, -5.43899168917672e-08,
)


def gelu_pieces(hidden):
    square = hidden * hidden
    bounded = jnp.minimum(square, 36.0)
    poly = rise_fit[-1]
    for factor in rise_fit[-2::-1]:
        poly = poly * bounded + factor
    rise = 1.0 + jnp.tanh(poly * hidden)
    bell = jnp.exp2(square * half_log2 + log2_density)
    return hidden * rise, rise + hidden * bell


def nn(a, b):
    return lax.dot_general(a, b, (((1,), (0,)), ((), ())), preferred_element_type=F32)


def nt(a, b):
    return lax.dot_general(a, b, (((1,), (1,)), ((), ())), preferred_element_type=F32)


def kernel(
    side, shape4,
    links_in, x_in, c_in, wet_ref, depth_ref, gamma_ref, up_ref, bias_ref, down_ref, scale_ref,
    out_ref, taps_ref, gain_ref, up_sum_ref, bias_sum_ref, down_sum_ref, scale_sum_ref,
    links, x_ref, c_ref, load_sem,
    pf, pg, taps, taps_acc, strips, corners, rows_in, cols_in, corners_in,
    wu, wd, pars, pars_in,
    mask_ref, wet_turned, grad_in, y_all, y_in, conv_send, conv_in,
    sums, gamma_acc, bias_acc, core_out, ring_out, ring_core, ring_a, ring_b, ring_y, total,
    small_a, small_peer, small_peer_in, small_core, small_x, small_z, small_y,
    halo_send, halo_recv, relay_send, weight_sem, weight_recv, grad_sem, grad_recv, y_sem, y_recv, conv_sem, conv_recv,
    rs_send, rs_recv, ag_send, ag_recv, sm_send, sm_recv,
):
    n_yh, n_z, n_x, n_core = shape4
    tiles = n_yh * n_z * n_x * n_core
    width = side + 16
    row_steps = side // ROWS
    steps = row_steps // 2
    chunk = ROWS * side
    me = lax.axis_index("tiles")
    h = lax.axis_index("chan")
    other = 1 - h
    core = me % n_core
    at_x = (me // n_core) % n_x
    at_z = (me // (n_core * n_x)) % n_z
    at_yh = me // (n_core * n_x * n_z)
    q = 1.0 / (side * math.sqrt(tiles))

    def tile_at(yh, z, x, c):
        return ((yh * n_z + z) * n_x + x) * n_core + c

    def dev(tile, chan=None):
        return {"tiles": tile, "chan": h if chan is None else chan}

    def remote(src, dst, send, recv, device):
        return pltpu.make_async_remote_copy(
            src_ref=src, dst_ref=dst, send_sem=send, recv_sem=recv, device_id=device, device_id_type=MESH
        )

    def line_at(which, k):
        return k + which * (row_steps - 1 - 2 * k)

    def chunk_rows(line):
        return pl.ds(pl.multiple_of(line * chunk, chunk), chunk)

    first = core * at_z + (1 - core) * at_x
    second = core * at_x + (1 - core) * at_z

    def ring_tile(a, b):
        return tile_at(at_yh, core * a + (1 - core) * b, core * b + (1 - core) * a, core)

    peer = dev(me, other)
    core_peer = dev(tile_at(at_yh, at_z, at_x, 1 - core))
    halo = [(sign, d) for sign in (1, -1) for d in range(1, REACH + 1)]

    def halo_tile(sign, d):
        return (me + sign * d + tiles) % tiles

    a_peers = [(first + k) % n_x for k in range(1, n_x)]
    b_peers = [(second + k) % n_x for k in range(1, n_x)]
    y_peers = [(0, 1), (1, 0), (1, 1)]

    def y_dev(dy, dc):
        return dev(tile_at((at_yh + dy) % 2, at_z, at_x, core), (h + dc) % 2)

    barrier = pltpu.get_barrier_semaphore()
    targets = [dev(halo_tile(s, d)) for s, d in halo]
    targets += [core_peer]
    targets += [dev(ring_tile(a, second)) for a in a_peers]
    targets += [dev(ring_tile(first, b)) for b in b_peers]
    targets += [y_dev(dy, dc) for dy, dc in y_peers]
    for target in targets:
        pl.semaphore_signal(barrier, inc=1, device_id=target, device_id_type=MESH)
    loads = [
        pltpu.make_async_copy(x_in, x_ref, load_sem.at[0]),
        pltpu.make_async_copy(c_in, c_ref, load_sem.at[1]),
        pltpu.make_async_copy(up_ref, wu.at[h], load_sem.at[2]),
        pltpu.make_async_copy(down_ref, wd.at[h], load_sem.at[3]),
    ]
    for copy in loads:
        copy.start()
    pars[...] = jnp.zeros_like(pars)
    pars[0:1, :] = bias_ref[...].astype(F32).reshape(1, HALF_HIDDEN)
    pars[1:2, 0:LANES] = gamma_ref[...].astype(F32).reshape(1, LANES)
    pars[2:3, 0:LANES] = scale_ref[...].astype(F32).reshape(1, LANES)
    links[...] = jnp.zeros_like(links)
    links[0:8, 0:tiles] = links_in[...].astype(F32)
    links[...] = links[...].T
    wet_turned[...] = jnp.zeros_like(wet_turned)
    wet_turned[0:side, 0:side] = wet_ref[...].astype(F32)
    wet_turned[...] = wet_turned[...].T
    pl.semaphore_wait(barrier, len(targets))

    diagonal = y_dev(1, 1)
    up_part, down_part = CHAN // 4, HALF_HIDDEN // 4

    def part(ref, size, at, count=1):
        return ref.at[pl.ds(pl.multiple_of(at * size, size), count * size), :]

    def weight_copy(n, device, quarter, slot):
        up = remote(
            part(up_ref, up_part, quarter), part(wu.at[slot], up_part, quarter),
            weight_sem.at[n], weight_recv.at[n], device,
        )
        down = remote(
            part(down_ref, down_part, quarter), part(wd.at[slot], down_part, quarter),
            weight_sem.at[n + 1], weight_recv.at[n + 1], device,
        )
        return [up, down]

    pars_copy = remote(pars, pars_in, weight_sem.at[0], weight_recv.at[0], peer)
    weight_copies = weight_copy(1, peer, 2 * core, h) + weight_copy(3, diagonal, 2 * core + 1, h)
    weight_arrivals = weight_copy(1, peer, 2 * core, other) + weight_copy(3, diagonal, 2 * core + 1, other)

    def weight_forward(half_at):
        return [
            remote(
                part(wu.at[other], up_part, 2 * half_at, 2), part(wu.at[other], up_part, 2 * half_at, 2),
                weight_sem.at[5], weight_recv.at[5], core_peer,
            ),
            remote(
                part(wd.at[other], down_part, 2 * half_at, 2), part(wd.at[other], down_part, 2 * half_at, 2),
                weight_sem.at[6], weight_recv.at[6], core_peer,
            ),
        ]

    pars_copy.start()
    for copy in weight_copies:
        copy.start()

    early = min(4, steps)

    def grad_copy(k):
        return remote(
            c_in.at[chunk_rows(line_at(other, k)), :], grad_in.at[chunk_rows(k), :],
            grad_sem.at[k], grad_recv.at[k], peer,
        )

    grad_copy(0).start()

    loads[0].wait()
    def fill_input(g, _):
        columns = pltpu.roll(wet_turned[0:side, :], (LANES - g * ROWS) % LANES, 1)
        for t in range(ROWS):
            i = g * ROWS + t
            at = pl.ds(pl.multiple_of(i * side, side), side)
            to = pl.multiple_of((i + MARGIN) * width + 8, 8)
            wet = jnp.broadcast_to(columns[:, t : t + 1], (side, LANES))
            mask_ref[at, :] = wet.astype(BF16)
            pf[pl.ds(to, side), :] = x_ref[at, :].astype(F32) * wet
        return 0

    lax.fori_loop(0, side // ROWS, fill_input, 0)

    def row_strips(padded):
        for side_at, row in enumerate((MARGIN, side)):
            for k in range(MARGIN):
                base = (row + k) * width + 8
                strips[side_at, k * side : (k + 1) * side, :] = padded[base : base + side, :].astype(BF16)
                near = base if side_at == 0 else base + side - 16
                corners[side_at, k * 16 : (k + 1) * 16, :] = padded[near : near + 16, :].astype(BF16)

    def col_strips(padded):
        for side_at, col in enumerate((8, 8 + side - MARGIN)):
            for k in range(MARGIN):
                line = padded[pl.ds(MARGIN * width + col + k, side, stride=width), :]
                strips[2 + side_at, k * side : (k + 1) * side, :] = line.astype(BF16)

    def halo_copy(src, dst, phase, n, sign, d):
        copy = remote(src, dst, halo_send.at[phase, n], halo_recv.at[phase, n], dev(halo_tile(sign, d)))
        to, source = me + sign * d, me - sign * d
        leaves = jnp.logical_and(to >= 0, to < tiles)
        comes = jnp.logical_and(source >= 0, source < tiles)
        return copy, dst, leaves, comes

    span = tiles // n_yh
    farthest = REACH - 1
    beyond = (me - span, span - 1 - me)

    def hands_on(way, steps_back):
        return jnp.logical_and(beyond[way] >= steps_back, beyond[way] < farthest)

    def crosses(sign, d):
        return (me + sign * d + tiles) // span != (me + tiles) // span

    def row_copy(phase, n, sign, d, way):
        copy, dst, leaves, comes = halo_copy(strips.at[1 - way], rows_in.at[phase, way, d - 1], phase, n, sign, d)
        if d < farthest:
            leaves = jnp.logical_and(leaves, jnp.logical_not(crosses(sign, d)))
        return copy, dst, leaves, comes

    def row_copies(phase):
        copies = []
        for n, (sign, d) in enumerate(halo):
            way = 0 if sign > 0 else 1
            if d < REACH:
                copies.append(row_copy(phase, n, sign, d, way))
            else:
                copies.append(halo_copy(corners.at[1 - way], corners_in.at[phase, way], phase, n, sign, d))
        return copies

    def col_copies(phase):
        copies = []
        for way, sign in enumerate((1, -1)):
            copies.append(halo_copy(strips.at[3 - way], cols_in.at[phase, way], phase, len(halo) + way, sign, 1))
        return copies

    def halo_start(copies):
        for copy, _, leaves, _ in copies:
            pl.when(leaves)(copy.start)

    def rows_start(copies, crossing):
        for (sign, d), (copy, _, leaves, _) in zip(halo, copies):
            over = crosses(sign, d)
            pl.when(jnp.logical_and(leaves, over if crossing else jnp.logical_not(over)))(copy.start)

    def relay_copies(phase, way):
        sign = 1 - 2 * way
        return [
            remote(
                rows_in.at[phase, way, farthest - 1], rows_in.at[phase, way, farthest - i - 1],
                relay_send.at[phase, i - 1], halo_recv.at[phase, way * REACH + farthest - i - 1],
                dev(halo_tile(-sign, i)),
            )
            for i in range(1, farthest)
        ]

    def relay(phase):
        for way in range(2):

            @pl.when(hands_on(way, 1))
            def _(way=way):
                row_copies(phase)[way * REACH + farthest - 1][0].wait_recv()

            for i, copy in enumerate(relay_copies(phase, way)):
                pl.when(hands_on(way, i + 1))(copy.start)

    def relay_left(phase):
        for way in range(2):
            for i, copy in enumerate(relay_copies(phase, way)):
                pl.when(hands_on(way, i + 1))(copy.wait_send)

    def halo_arrive(copies):
        for n, (copy, dst, _, comes) in enumerate(copies):
            waits = comes
            if n < len(halo) and n % REACH == farthest - 1:
                waits = jnp.logical_and(comes, jnp.logical_not(hands_on(n // REACH, 1)))
            pl.when(waits)(copy.wait_recv)

            @pl.when(jnp.logical_not(comes))
            def _(dst=dst):
                dst[...] = jnp.zeros(dst.shape, BF16)

    def halo_left(copies):
        for copy, _, leaves, _ in copies:
            pl.when(leaves)(copy.wait_send)

    def match(direction, source):
        link = links[pl.ds(me, 1), direction : direction + 1]
        return jnp.where(jnp.logical_and(link == lax.convert_element_type(source, F32), link >= 0.0), 1.0, 0.0)

    def fill_halo(padded, phase):
        for way, sign in enumerate((-1, 1)):
            straight, left, right, beside = ((0, 4, 5, 2), (1, 6, 7, 3))[way]
            row = 0 if way == 0 else side + MARGIN
            straight_hit = [match(straight, me + sign * d) for d in range(1, 5)]
            left_hit = [match(left, me + sign * d) for d in range(1, 6)]
            right_hit = [match(right, me + sign * d) for d in range(1, 6)]
            far_hit = left_hit[4] if way == 0 else right_hit[4]
            for k in range(MARGIN):
                base = (row + k) * width
                lines = [rows_in[phase, way, d, k * side : (k + 1) * side, :].astype(F32) for d in range(4)]
                far = corners_in[phase, way, k * 16 : (k + 1) * 16, :].astype(F32)
                middle = sum(hit * line for hit, line in zip(straight_hit, lines))
                west = sum(hit * line[side - 8 :] for hit, line in zip(left_hit[:4], lines))
                east = sum(hit * line[:8] for hit, line in zip(right_hit[:4], lines))
                if way == 0:
                    west = west + far_hit * far[8:]
                else:
                    east = east + far_hit * far[:8]
                padded[base : base + 8, :] = west
                padded[base + 8 : base + 8 + side, :] = middle
                padded[base + 8 + side : base + 16 + side, :] = east
            hit = match(beside, me + sign)
            col = 8 - MARGIN if way == 0 else 8 + side
            for k in range(MARGIN):
                line = cols_in[phase, way, k * side : (k + 1) * side, :].astype(F32)
                padded[pl.ds(MARGIN * width + col + k, side, stride=width), :] = line * hit

    row_strips(pf)
    col_strips(pf)
    forward_halo = row_copies(0) + col_copies(0)
    halo_start(forward_halo)
    for k in range(1, early):
        grad_copy(k).start()

    for a in range(KERNEL):
        for b in range(KERNEL):
            n = (a * KERNEL + b) * 8
            taps[n : n + 8, :] = jnp.broadcast_to(depth_ref[a, b : b + 1, :], (8, LANES))

    def conv_block(padded, row, col, flip):
        base = row * width + col + 8 - MARGIN
        acc = [[None] * COLS for _ in range(ROWS)]
        for b in range(KERNEL):
            weights = []
            for a in range(KERNEL):
                n = a * KERNEL + b
                n = (KERNEL * KERNEL - 1 - n if flip else n) * 8
                weights.append(taps[n : n + 8, :])
            for r in range(ROWS + KERNEL - 1):
                for v in range(COLS):
                    value = padded[pl.ds(base + (r * width + v * 8 + b), 8), :]
                    for a in range(KERNEL):
                        i = r - a
                        if 0 <= i < ROWS:
                            term = value * weights[a]
                            acc[i][v] = term if acc[i][v] is None else acc[i][v] + term
        return acc

    col_steps = side // (8 * COLS)

    def filter_forward(k, c):
        col = pl.multiple_of(c * (8 * COLS), 8 * COLS)
        acc = conv_block(pf, k * ROWS, col, False)
        for i in range(ROWS):
            at = pl.multiple_of((k * ROWS + i) * side + col, 8 * COLS)
            y_all[pl.ds(at, 8 * COLS), :] = jnp.concatenate(acc[i], 0).astype(BF16)

    def conv_inner(n, _):
        filter_forward(1 + n // (col_steps - 2), 1 + n % (col_steps - 2))
        return 0

    inner = (row_steps - 2) * (col_steps - 2)
    lax.fori_loop(0, inner // 2, conv_inner, 0)
    relay(0)
    lax.fori_loop(inner // 2, inner, conv_inner, 0)
    for copy in weight_arrivals:
        copy.wait_recv()
    forwards = weight_forward(core)
    for copy in forwards:
        copy.start()
    halo_arrive(forward_halo)
    fill_halo(pf, 0)

    def y_copy(k):
        return remote(
            y_all.at[chunk_rows(line_at(other, k)), :], y_in.at[chunk_rows(k), :], y_sem.at[k], y_recv.at[k], peer
        )

    def conv_outer(n, _):
        away = n < steps
        k = jnp.where(away, line_at(other, n), line_at(h, n - steps))
        edge = jnp.logical_or(k == 0, k == row_steps - 1)

        def one(c, _):
            filter_forward(k, jnp.where(edge, c, c * (col_steps - 1)))
            return 0

        lax.fori_loop(0, jnp.where(edge, col_steps, 2), one, 0)

        @pl.when(away)
        def _():
            y_copy(n).start()

        @pl.when(jnp.logical_and(n + 1 >= early, n + 1 < steps))
        def _():
            grad_copy(n + 1).start()

        return 0

    lax.fori_loop(0, row_steps, conv_outer, 0)

    pars_copy.wait_recv()
    for copy in weight_forward(1 - core):
        copy.wait_recv()
    for copy in loads[1:4]:
        copy.wait()
    halo_left(forward_halo)
    mine = h == 0

    def ordered(own, others):
        return jnp.where(mine, own, others), jnp.where(mine, others, own)

    def row_of(n):
        own, others = pars[n : n + 1, 0:LANES], pars_in[n : n + 1, 0:LANES]
        return jnp.concatenate(ordered(own, others), 1)

    gamma_row = row_of(1)
    half_gamma = 0.5 * gamma_row
    scale_row = row_of(2)
    bias_rows = ordered(pars[0:1, :], pars_in[0:1, :])

    sums[...] = jnp.zeros_like(sums)
    gamma_acc[...] = jnp.zeros_like(gamma_acc)
    bias_acc[...] = jnp.zeros_like(bias_acc)
    taps_acc[...] = jnp.zeros_like(taps_acc)

    def conv_copy(k):
        at = chunk_rows(k)
        return remote(conv_send.at[at, :], conv_in.at[at, :], conv_sem.at[k], conv_recv.at[k], peer)

    def take_conv(k):
        conv_copy(k).wait_recv()
        for i in range(ROWS):
            at = pl.multiple_of((k * ROWS + i) * side, side)
            to = pl.multiple_of((MARGIN + line_at(other, k) * ROWS + i) * width + 8, 8)
            pg[pl.ds(to, side), :] = conv_in[pl.ds(at, side), :].astype(F32)

    def filter_line(line):
        row = line * ROWS

        def one(c, _):
            col = c * (8 * COLS)
            inner = (row + MARGIN) * width + col + 8
            base = row * width + col + 8 - MARGIN
            grads = [
                [pg[pl.ds(pl.multiple_of(inner, 8) + (i * width + v * 8), 8), :] for v in range(COLS)] for i in range(ROWS)
            ]
            for b in range(KERNEL):
                acc = [None] * KERNEL
                for r in range(ROWS + KERNEL - 1):
                    for v in range(COLS):
                        value = pf[pl.ds(base + (r * width + v * 8 + b), 8), :]
                        for a in range(KERNEL):
                            i = r - a
                            if 0 <= i < ROWS:
                                term = value * grads[i][v]
                                acc[a] = term if acc[a] is None else acc[a] + term
                for a in range(KERNEL):
                    n = (a * KERNEL + b) * 8
                    taps_acc[n : n + 8, :] += acc[a]
            return 0

        lax.fori_loop(0, col_steps, one, 0)

    def mlp(k, _):
        at = chunk_rows(k)
        line = line_at(h, k)
        own_at = chunk_rows(line)
        y_copy(k).wait_recv()
        grad_copy(k).wait_recv()
        low, high = ordered(y_all[own_at, :].astype(F32), y_in[at, :].astype(F32))
        y = jnp.concatenate((low, high), 1)
        centred = y - jnp.sum(y, 1, keepdims=True) * (1.0 / CHAN)
        spread = jnp.sum(centred * centred, 1, keepdims=True) * (1.0 / CHAN)
        inv_spread = lax.rsqrt(spread + 1e-06)
        unit = centred * inv_spread
        normed = (unit * gamma_row).astype(BF16)
        wet = mask_ref[own_at, :].astype(F32)
        low, high = ordered(c_ref[own_at, :].astype(F32), grad_in[at, :].astype(F32))
        branch_grad = (jnp.concatenate((low * wet, high * wet), 1) * scale_row).astype(BF16)
        branch_t = branch_grad.T
        normed_t = jnp.concatenate((normed.T, jnp.ones((16, chunk), BF16)), 0)
        norm_grad = jnp.zeros((chunk, CHAN), F32)
        for block in range(HIDDEN // BLOCK):
            slot, off = divmod(block * BLOCK, HALF_HIDDEN)
            w_up = wu[slot, :, off : off + BLOCK]
            w_down = wd[slot, off : off + BLOCK, :]
            cols = slice(block * BLOCK, (block + 1) * BLOCK)
            hidden = nn(normed, w_up) + bias_rows[slot][:, off : off + BLOCK]
            activated, slope = gelu_pieces(hidden)
            hidden_grad = (nt(branch_grad, w_down) * slope).astype(BF16)
            sums[1, :, cols] += nn(branch_t, activated.astype(BF16))
            up_terms = nn(normed_t, hidden_grad)
            sums[0, :, cols] += up_terms[:CHAN]
            bias_acc[:, cols] += up_terms[CHAN : CHAN + 8]
            norm_grad = norm_grad + nt(hidden_grad, w_up)
        gamma_acc[...] += jnp.sum((norm_grad * unit).reshape(chunk // 8, 8, CHAN), 0)
        scaled = norm_grad * half_gamma
        mean = jnp.sum(scaled, 1, keepdims=True) * (1.0 / CHAN)
        tilt = jnp.sum(scaled * unit, 1, keepdims=True) * (1.0 / CHAN)
        conv_grad = (inv_spread * (scaled - mean - unit * tilt)).astype(BF16).astype(F32)
        own, away = ordered(conv_grad[:, :LANES], conv_grad[:, LANES:])
        conv_send[at, :] = away.astype(BF16)
        conv_copy(k).start()
        for i in range(ROWS):
            to = pl.multiple_of((MARGIN + line * ROWS + i) * width + 8, 8)
            pg[pl.ds(to, side), :] = own[i * side : (i + 1) * side]
        filter_line(line)

        @pl.when(k == steps - 1)
        def _():
            take_conv(0)
            row_strips(pg)
            rows = row_copies(1)
            rows_start(rows, False)
            rows_start(rows, True)

        return 0

    lax.fori_loop(0, steps, mlp, 0)

    core_out[...] = sums[1 - core].astype(BF16)
    rs_core = remote(core_out, ring_core, rs_send.at[0], rs_recv.at[0], core_peer)
    rs_core.start()

    ident = lax.broadcasted_iota(jnp.int32, (CHAN, CHAN), 0) == lax.broadcasted_iota(jnp.int32, (CHAN, CHAN), 1)
    down_sums = sums[1]
    down_high = down_sums.astype(BF16)
    down_low = (down_sums - down_high.astype(F32)).astype(BF16)
    paired = jnp.zeros((CHAN, CHAN), F32)
    for slot in range(2):
        cols = slice(slot * HALF_HIDDEN, (slot + 1) * HALF_HIDDEN)
        paired = paired + nn(down_high[:, cols], wd[slot]) + nn(down_low[:, cols], wd[slot])
    scale_sum = 0.5 * jnp.sum(jnp.where(ident, paired, 0.0), 0, keepdims=True) / scale_row
    gamma_sum = 0.5 * jnp.sum(gamma_acc[...], 0, keepdims=True)
    bias_sum = 0.5 * bias_acc[0:1, :]
    small_peer[...] = jnp.zeros_like(small_peer)
    small_a[...] = jnp.zeros_like(small_a)
    n_taps = KERNEL * KERNEL

    def put_small(ref, at, value, n):
        own, away = ordered(value[:, : n * LANES], value[:, n * LANES :])
        for i in range(n):
            ref[0][ref[1] + at + i : ref[1] + at + i + 1, :] = own[:, i * LANES : (i + 1) * LANES]
            small_peer[at + i : at + i + 1, :] = away[:, i * LANES : (i + 1) * LANES]

    place = (small_a, n_taps)
    put_small(place, 0, gamma_sum, 1)
    put_small(place, 1, scale_sum, 1)
    put_small(place, 2, bias_sum, 4)
    small_chan = remote(small_peer, small_peer_in, sm_send.at[0], sm_recv.at[0], peer)
    small_chan.start()

    def input_block(line, c):
        row = line * ROWS
        col = pl.multiple_of(c * (8 * COLS), 8 * COLS)
        acc = conv_block(pg, row, col, True)
        for i in range(ROWS):
            at = pl.ds(pl.multiple_of((row + i) * side + col, 8 * COLS), 8 * COLS)
            wet = mask_ref[at, :].astype(F32)
            grad = c_ref[at, :].astype(F32)
            out_ref[at, :] = (wet * (grad + jnp.concatenate(acc[i], 0))).astype(BF16)

    inner_cols = col_steps - 2

    def own_inner(n, _):
        input_block(line_at(h, 1 + n // inner_cols), 1 + n % inner_cols)
        return 0

    def rest_inner(n, _):
        k = 1 + n // inner_cols
        input_block(jnp.where(k == steps, line_at(h, steps - 1), line_at(other, k)), 1 + n % inner_cols)
        return 0

    def input_edges(k, _):
        edge = jnp.logical_or(k == 0, k == row_steps - 1)

        def one(c, _):
            input_block(k, jnp.where(edge, c, c * (col_steps - 1)))
            return 0

        lax.fori_loop(0, jnp.where(edge, col_steps, 2), one, 0)
        return 0

    def peer_line(k, _):
        @pl.when(k > 0)
        def _():
            take_conv(k)

        filter_line(line_at(other, k))
        return 0

    own = (steps - 2) * inner_cols
    lax.fori_loop(0, own // 2, own_inner, 0)
    lax.fori_loop(0, 1, peer_line, 0)

    rs_core.wait_recv()
    sums[core] = sums[core] + ring_core[...].astype(F32)
    ring_out[...] = sums[core].astype(BF16)
    a_rows, b_rows = CHAN // n_x, CHAN // n_x // n_z
    rs_a = []
    for k, a in enumerate(a_peers):
        piece = ring_out.at[pl.ds(pl.multiple_of(a * a_rows, a_rows), a_rows), :]
        rs_a.append(remote(piece, ring_a.at[k], rs_send.at[1 + k], rs_recv.at[1 + k], dev(ring_tile(a, second))))
    for copy in rs_a:
        copy.start()

    lax.fori_loop(own // 2, own, own_inner, 0)
    lax.fori_loop(1, steps - 2, peer_line, 0)

    for copy in rs_a:
        copy.wait_recv()
    a_at = pl.ds(pl.multiple_of(first * a_rows, a_rows), a_rows)
    sums[core, a_at, :] = sums[core, a_at, :] + sum(ring_a[k].astype(F32) for k in range(n_x - 1))
    rs_b = []
    for k, b in enumerate(b_peers):
        piece = sums.at[core, pl.ds(pl.multiple_of(first * a_rows + b * b_rows, b_rows), b_rows), :]
        rs_b.append(remote(piece, ring_b.at[k], rs_send.at[4 + k], rs_recv.at[4 + k], dev(ring_tile(first, b))))
    for copy in rs_b:
        copy.start()

    relay(1)
    lax.fori_loop(steps - 2, steps - 1, peer_line, 0)
    rest = steps * inner_cols
    lax.fori_loop(0, rest // 2, rest_inner, 0)

    for copy in rs_b:
        copy.wait_recv()
    b_start = first * a_rows + second * b_rows
    b_at = pl.ds(pl.multiple_of(b_start, b_rows), b_rows)
    sums[core, b_at, :] = sums[core, b_at, :] + sum(ring_b[k] for k in range(n_x - 1))

    def y_piece(chan):
        return (core, b_at, pl.ds(pl.multiple_of(chan * HALF_HIDDEN, HALF_HIDDEN), HALF_HIDDEN))

    y_slot = 2 * at_yh + h
    ring_y[y_slot] = sums[y_piece(h)]
    rs_y = []
    for k, (dy, dc) in enumerate(y_peers):
        piece = sums.at[y_piece((h + dc) % 2)]
        rs_y.append(remote(piece, ring_y.at[y_slot], rs_send.at[7 + k], rs_recv.at[7 + k], y_dev(dy, dc)))
    for copy in rs_y:
        copy.start()

    take_conv(steps - 1)
    col_strips(pg)
    last_halo = col_copies(1)
    halo_start(last_halo)
    filter_line(line_at(other, steps - 1))

    for n in range(n_taps):
        small_a[n : n + 1, :] = jnp.sum(taps_acc[n * 8 : n * 8 + 8, :], 0, keepdims=True)
    small_chan.wait_recv()
    for n in range(6):
        small_a[n_taps + n : n_taps + n + 1, :] += small_peer_in[n : n + 1, :]
    sm_core = remote(small_a, small_core, sm_send.at[1], sm_recv.at[1], core_peer)
    sm_core.start()

    lax.fori_loop(rest // 2, rest * 3 // 4, rest_inner, 0)

    sm_core.wait_recv()

    def small_stage(ref, value, at, size, base, tile):
        ref[at] = value
        copies = []
        for k in range(1, size):
            there = (at + k) % size
            copies.append(
                remote(ref.at[at], ref.at[at], sm_send.at[base + k - 1], sm_recv.at[base + k - 1], dev(tile(there)))
            )
        for copy in copies:
            copy.start()
        return copies

    sm_x = small_stage(
        small_x, small_a[...] + small_core[...], at_x, n_x, 2, lambda x: tile_at(at_yh, at_z, x, core)
    )
    lax.fori_loop(rest * 3 // 4, rest, rest_inner, 0)

    for copy in rs_y:
        copy.wait_recv()
    total[core, b_at, :] = ((ring_y[0] + ring_y[1]) + (ring_y[2] + ring_y[3])).astype(BF16)
    ag_b = []
    for k, b in enumerate(b_peers):
        block = total.at[core, b_at, :]
        ag_b.append(remote(block, block, ag_send.at[1 + k], ag_recv.at[1 + k], dev(ring_tile(first, b))))
    for copy in ag_b:
        copy.start()

    first_halo = row_copies(1)
    halo_arrive(first_halo + last_halo)
    fill_halo(pg, 1)
    marks = [row_steps * n // 4 for n in range(5)]
    lax.fori_loop(marks[0], marks[1], input_edges, 0)

    for copy in sm_x:
        copy.wait_recv()
    sm_z = small_stage(
        small_z, sum(small_x[k] for k in range(n_x)), at_z, n_z, 5, lambda z: tile_at(at_yh, z, at_x, core)
    )
    for copy in ag_b:
        copy.wait_recv()
    ag_a = []
    for k, a in enumerate(a_peers):
        block = total.at[core, a_at, :]
        ag_a.append(remote(block, block, ag_send.at[4 + k], ag_recv.at[4 + k], dev(ring_tile(a, second))))
    for copy in ag_a:
        copy.start()

    lax.fori_loop(marks[1], marks[3], input_edges, 0)

    for copy in sm_z:
        copy.wait_recv()
    sm_y = small_stage(
        small_y, sum(small_z[k] for k in range(n_z)), at_yh, 2, 8, lambda yh: tile_at(yh, at_z, at_x, core)
    )
    for copy in ag_a:
        copy.wait_recv()
    ag_core = remote(total.at[core], total.at[core], ag_send.at[7], ag_recv.at[7], core_peer)
    ag_core.start()

    lax.fori_loop(marks[3], marks[4], input_edges, 0)

    @pl.when(core == 0)
    def _():
        up_sum_ref[...] = total[0].astype(F32) * (0.5 * q)

    @pl.when(core == 1)
    def _():
        down_sum_ref[...] = total[1].astype(F32).T * (0.5 * q)

    for copy in sm_y:
        copy.wait_recv()
    small = (small_y[0] + small_y[1]) * q
    for a in range(KERNEL):
        taps_ref[a] = small[a * KERNEL : (a + 1) * KERNEL]
    gain_ref[...] = small[n_taps : n_taps + 1].reshape(LANES)
    scale_sum_ref[...] = small[n_taps + 1 : n_taps + 2].reshape(LANES)
    for i in range(4):
        bias_sum_ref[i * LANES : (i + 1) * LANES] = small[n_taps + 2 + i : n_taps + 3 + i].reshape(LANES)
    ag_core.wait_recv()

    @pl.when(core == 1)
    def _():
        up_sum_ref[...] = total[0].astype(F32) * (0.5 * q)

    @pl.when(core == 0)
    def _():
        down_sum_ref[...] = total[1].astype(F32).T * (0.5 * q)

    halo_left(first_halo + last_halo)
    relay_left(0)
    relay_left(1)
    for copy in weight_copies + forwards + [pars_copy, rs_core, small_chan, sm_core, ag_core]:
        copy.wait_send()
    for copy in rs_a + rs_b + rs_y + ag_a + ag_b + sm_x + sm_z + sm_y:
        copy.wait_send()

    def finish(k, _):
        grad_copy(k).wait_send()
        y_copy(k).wait_send()
        conv_copy(k).wait_send()
        return 0

    lax.fori_loop(0, steps, finish, 0)


SHAPES = {64: (2, 4, 4, 2), 16: (2, 2, 2, 2)}


def hand_over(*refs):
    count = len(refs) // 2
    for source, result in zip(refs[:count], refs[count:]):
        result[...] = source[...]


def place(results):
    whole = pl.BlockSpec(memory_space=pltpu.VMEM)
    return pl.pallas_call(
        hand_over,
        out_shape=tuple(jax.ShapeDtypeStruct(r.shape, r.dtype) for r in results),
        in_specs=[whole] * len(results),
        out_specs=(whole,) * len(results),
    )(*results)


def block_call(inputs, cotangent, wet, neighbours, depth_weight, gamma, up_weight, up_bias, down_weight, layer_scale):
    side = inputs.shape[1]
    half_chan = inputs.shape[3]
    flat = (side * side, half_chan)
    shape4 = SHAPES[lax.axis_size("tiles")]
    n_yh, n_z, n_x, n_core = shape4
    width = side + 16
    cells = side * side // 2
    row_steps = side // ROWS
    steps = row_steps // 2
    a_rows = CHAN // n_x
    vmem = pltpu.VMEM
    whole = pl.BlockSpec(memory_space=pltpu.VMEM)
    hbm = pl.BlockSpec(memory_space=pl.ANY)
    dma = pltpu.SemaphoreType.DMA
    padded = vmem(((side + 2 * MARGIN) * width, LANES), F32)
    taps = vmem((KERNEL * KERNEL * 8, LANES), F32)
    piece = vmem((cells, LANES), BF16)
    small = vmem((64, LANES), F32)
    pars = vmem((8, HALF_HIDDEN), F32)
    tile = vmem((side * side, LANES), BF16)
    scratch = [
        vmem((LANES, LANES), F32), tile, tile, dma((4,)),
        padded, padded, taps, taps,
        vmem((4, MARGIN * side, LANES), BF16),
        vmem((2, MARGIN * 16, LANES), BF16),
        vmem((2, 2, 4, MARGIN * side, LANES), BF16),
        vmem((2, 2, MARGIN * side, LANES), BF16),
        vmem((2, 2, MARGIN * 16, LANES), BF16),
        vmem((2, CHAN, HALF_HIDDEN), BF16),
        vmem((2, HALF_HIDDEN, CHAN), BF16),
        pars, pars,
        tile, vmem((LANES, LANES), F32),
        piece, tile, piece, piece, piece,
        vmem((2, CHAN, HIDDEN), F32),
        vmem((8, CHAN), F32),
        vmem((8, HIDDEN), F32),
        vmem((CHAN, HIDDEN), BF16), vmem((CHAN, HIDDEN), BF16), vmem((CHAN, HIDDEN), BF16),
        vmem((n_x - 1, a_rows, HIDDEN), BF16),
        vmem((n_x - 1, a_rows // n_z, HIDDEN), F32),
        vmem((4, a_rows // n_z, HALF_HIDDEN), F32),
        vmem((2, CHAN, HALF_HIDDEN), BF16),
        small, vmem((8, LANES), F32), vmem((8, LANES), F32), small,
        vmem((n_x, 64, LANES), F32), vmem((n_z, 64, LANES), F32), vmem((2, 64, LANES), F32),
        dma((2, 12)), dma((2, 12)), dma((2, 3)), dma((7,)), dma((7,)),
        dma((steps,)), dma((steps,)), dma((steps,)), dma((steps,)), dma((steps,)), dma((steps,)),
        dma((10,)), dma((10,)), dma((8,)), dma((8,)), dma((9,)), dma((9,)),
    ]
    return pl.pallas_call(
        functools.partial(kernel, side, shape4),
        out_shape=(
            vmem(flat, BF16),
            jax.ShapeDtypeStruct((KERNEL, KERNEL, LANES), F32),
            jax.ShapeDtypeStruct((LANES,), F32),
            jax.ShapeDtypeStruct((CHAN, HALF_HIDDEN), F32),
            jax.ShapeDtypeStruct((HALF_HIDDEN,), F32),
            jax.ShapeDtypeStruct((HALF_HIDDEN, CHAN), F32),
            jax.ShapeDtypeStruct((LANES,), F32),
        ),
        in_specs=[whole, hbm, hbm, whole, whole, whole, hbm, whole, hbm, whole],
        out_specs=(whole, whole, whole, whole, whole, whole, whole),
        scratch_shapes=scratch,
        compiler_params=pltpu.CompilerParams(
            collective_id=0, has_side_effects=True, vmem_limit_bytes=58 * 1024 * 1024
        ),
    )(
        neighbours.T,
        inputs.reshape(flat),
        cotangent.reshape(flat),
        wet[0],
        depth_weight,
        gamma,
        up_weight,
        up_bias,
        down_weight,
        layer_scale,
    )


def body(
    inputs,
    cotangent,
    wet,
    neighbours,
    depth_weight,
    gamma,
    up_weight,
    up_bias,
    down_weight,
    layer_scale,
):
    grad, *sums = block_call(
        inputs, cotangent, wet, neighbours, depth_weight, gamma, up_weight, up_bias, down_weight, layer_scale
    )
    return (grad.reshape(inputs.shape), *place(sums))


def solution(mesh):
    return jax.shard_map(
        body,
        mesh=mesh,
        in_specs=(
            P("tiles", None, None, "chan"),
            P("tiles", None, None, "chan"),
            P("tiles", None, None),
            P(),
            P(None, None, "chan"),
            P("chan"),
            P(None, "chan"),
            P("chan"),
            P("chan", None),
            P("chan"),
        ),
        out_specs=(
            P("tiles", None, None, "chan"),
            P(None, None, "chan"),
            P("chan"),
            P(None, "chan"),
            P("chan"),
            P("chan", None),
            P("chan"),
        ),
        check_vma=False,
    )
```

```python
import functools
import math

import jax
import jax.numpy as jnp
from jax import lax
from jax.experimental import pallas as pl
from jax.experimental.pallas import tpu as pltpu
from jax.sharding import PartitionSpec as P

KERNEL = 7
MARGIN = 3
LANES = 128
CHAN = 256
HIDDEN = 1024
HALF_HIDDEN = 512
BLOCK = 256
ROWS = 8
COLS = 2
REACH = 5
F32 = jnp.float32
BF16 = jnp.bfloat16
MESH = pl.DeviceIdType.MESH
half_log2 = -0.7213475204444817
log2_density = -0.3257480647361593
rise_fit = (
    0.7978803240566237, 0.036352056236426934, -5.1744776236202565e-05, -4.809871843393557e-05,
    2.8097794756336268e-06, -5.43899168917672e-08,
)


def gelu_pieces(hidden):
    square = hidden * hidden
    bounded = jnp.minimum(square, 36.0)
    poly = rise_fit[-1]
    for factor in rise_fit[-2::-1]:
        poly = poly * bounded + factor
    rise = 1.0 + jnp.tanh(poly * hidden)
    bell = jnp.exp2(square * half_log2 + log2_density)
    return hidden * rise, rise + hidden * bell


def nn(a, b):
    return lax.dot_general(a, b, (((1,), (0,)), ((), ())), preferred_element_type=F32)


def nt(a, b):
    return lax.dot_general(a, b, (((1,), (1,)), ((), ())), preferred_element_type=F32)


def kernel(
    side, shape4,
    links_in, x_in, c_in, wet_ref, depth_ref, gamma_ref, up_ref, bias_ref, down_ref, scale_ref,
    out_ref, taps_ref, gain_ref, up_sum_ref, bias_sum_ref, down_sum_ref, scale_sum_ref,
    links, x_ref, c_ref, load_sem,
    pf, pg, taps, taps_acc, strips, corners, rows_in, cols_in, corners_in,
    wu, wd, pars, pars_in,
    mask_ref, wet_turned, grad_in, y_all, y_in, conv_send, conv_in,
    sums, gamma_acc, bias_acc, core_out, ring_out, ring_core, ring_a, ring_b, ring_y, total,
    small_a, small_peer, small_peer_in, small_core, small_x, small_z, small_y,
    halo_send, halo_recv, relay_send, weight_sem, weight_recv, grad_sem, grad_recv, y_sem, y_recv, conv_sem, conv_recv,
    rs_send, rs_recv, ag_send, ag_recv, sm_send, sm_recv,
):
    n_yh, n_z, n_x, n_core = shape4
    tiles = n_yh * n_z * n_x * n_core
    width = side + 16
    row_steps = side // ROWS
    steps = row_steps // 2
    chunk = ROWS * side
    me = lax.axis_index("tiles")
    h = lax.axis_index("chan")
    other = 1 - h
    core = me % n_core
    at_x = (me // n_core) % n_x
    at_z = (me // (n_core * n_x)) % n_z
    at_yh = me // (n_core * n_x * n_z)
    q = 1.0 / (side * math.sqrt(tiles))

    def tile_at(yh, z, x, c):
        return ((yh * n_z + z) * n_x + x) * n_core + c

    def dev(tile, chan=None):
        return {"tiles": tile, "chan": h if chan is None else chan}

    def remote(src, dst, send, recv, device):
        return pltpu.make_async_remote_copy(
            src_ref=src, dst_ref=dst, send_sem=send, recv_sem=recv, device_id=device, device_id_type=MESH
        )

    def line_at(which, k):
        return k + which * (row_steps - 1 - 2 * k)

    def chunk_rows(line):
        return pl.ds(pl.multiple_of(line * chunk, chunk), chunk)

    first = core * at_z + (1 - core) * at_x
    second = core * at_x + (1 - core) * at_z

    def ring_tile(a, b):
        return tile_at(at_yh, core * a + (1 - core) * b, core * b + (1 - core) * a, core)

    peer = dev(me, other)
    core_peer = dev(tile_at(at_yh, at_z, at_x, 1 - core))
    halo = [(sign, d) for sign in (1, -1) for d in range(1, REACH + 1)]

    def halo_tile(sign, d):
        return (me + sign * d + tiles) % tiles

    a_peers = [(first + k) % n_x for k in range(1, n_x)]
    b_peers = [(second + k) % n_x for k in range(1, n_x)]
    y_peers = [(0, 1), (1, 0), (1, 1)]

    def y_dev(dy, dc):
        return dev(tile_at((at_yh + dy) % 2, at_z, at_x, core), (h + dc) % 2)

    barrier = pltpu.get_barrier_semaphore()
    targets = [dev(halo_tile(s, d)) for s, d in halo]
    targets += [core_peer]
    targets += [dev(ring_tile(a, second)) for a in a_peers]
    targets += [dev(ring_tile(first, b)) for b in b_peers]
    targets += [y_dev(dy, dc) for dy, dc in y_peers]
    for target in targets:
        pl.semaphore_signal(barrier, inc=1, device_id=target, device_id_type=MESH)
    loads = [
        pltpu.make_async_copy(x_in, x_ref, load_sem.at[0]),
        pltpu.make_async_copy(c_in, c_ref, load_sem.at[1]),
        pltpu.make_async_copy(up_ref, wu.at[h], load_sem.at[2]),
        pltpu.make_async_copy(down_ref, wd.at[h], load_sem.at[3]),
    ]
    for copy in loads:
        copy.start()
    pars[...] = jnp.zeros_like(pars)
    pars[0:1, :] = bias_ref[...].astype(F32).reshape(1, HALF_HIDDEN)
    pars[1:2, 0:LANES] = gamma_ref[...].astype(F32).reshape(1, LANES)
    pars[2:3, 0:LANES] = scale_ref[...].astype(F32).reshape(1, LANES)
    links[...] = jnp.zeros_like(links)
    links[0:8, 0:tiles] = links_in[...].astype(F32)
    links[...] = links[...].T
    wet_turned[...] = jnp.zeros_like(wet_turned)
    wet_turned[0:side, 0:side] = wet_ref[...].astype(F32)
    wet_turned[...] = wet_turned[...].T
    pl.semaphore_wait(barrier, len(targets))

    diagonal = y_dev(1, 1)
    up_part, down_part = CHAN // 4, HALF_HIDDEN // 4

    def part(ref, size, at, count=1):
        return ref.at[pl.ds(pl.multiple_of(at * size, size), count * size), :]

    def weight_copy(n, device, quarter, slot):
        up = remote(
            part(up_ref, up_part, quarter), part(wu.at[slot], up_part, quarter),
            weight_sem.at[n], weight_recv.at[n], device,
        )
        down = remote(
            part(down_ref, down_part, quarter), part(wd.at[slot], down_part, quarter),
            weight_sem.at[n + 1], weight_recv.at[n + 1], device,
        )
        return [up, down]

    pars_copy = remote(pars, pars_in, weight_sem.at[0], weight_recv.at[0], peer)
    weight_copies = weight_copy(1, peer, 2 * core, h) + weight_copy(3, diagonal, 2 * core + 1, h)
    weight_arrivals = weight_copy(1, peer, 2 * core, other) + weight_copy(3, diagonal, 2 * core + 1, other)

    def weight_forward(half_at):
        return [
            remote(
                part(wu.at[other], up_part, 2 * half_at, 2), part(wu.at[other], up_part, 2 * half_at, 2),
                weight_sem.at[5], weight_recv.at[5], core_peer,
            ),
            remote(
                part(wd.at[other], down_part, 2 * half_at, 2), part(wd.at[other], down_part, 2 * half_at, 2),
                weight_sem.at[6], weight_recv.at[6], core_peer,
            ),
        ]

    pars_copy.start()
    for copy in weight_copies:
        copy.start()

    early = min(4, steps)

    def grad_copy(k):
        return remote(
            c_in.at[chunk_rows(line_at(other, k)), :], grad_in.at[chunk_rows(k), :],
            grad_sem.at[k], grad_recv.at[k], peer,
        )

    grad_copy(0).start()

    loads[0].wait()
    def fill_input(g, _):
        columns = pltpu.roll(wet_turned[0:side, :], (LANES - g * ROWS) % LANES, 1)
        for t in range(ROWS):
            i = g * ROWS + t
            at = pl.ds(pl.multiple_of(i * side, side), side)
            to = pl.multiple_of((i + MARGIN) * width + 8, 8)
            wet = jnp.broadcast_to(columns[:, t : t + 1], (side, LANES))
            mask_ref[at, :] = wet.astype(BF16)
            pf[pl.ds(to, side), :] = x_ref[at, :].astype(F32) * wet
        return 0

    lax.fori_loop(0, side // ROWS, fill_input, 0)

    def row_strips(padded):
        for side_at, row in enumerate((MARGIN, side)):
            for k in range(MARGIN):
                base = (row + k) * width + 8
                strips[side_at, k * side : (k + 1) * side, :] = padded[base : base + side, :].astype(BF16)
                near = base if side_at == 0 else base + side - 16
                corners[side_at, k * 16 : (k + 1) * 16, :] = padded[near : near + 16, :].astype(BF16)

    def col_strips(padded):
        for side_at, col in enumerate((8, 8 + side - MARGIN)):
            for k in range(MARGIN):
                line = padded[pl.ds(MARGIN * width + col + k, side, stride=width), :]
                strips[2 + side_at, k * side : (k + 1) * side, :] = line.astype(BF16)

    def halo_copy(src, dst, phase, n, sign, d):
        copy = remote(src, dst, halo_send.at[phase, n], halo_recv.at[phase, n], dev(halo_tile(sign, d)))
        to, source = me + sign * d, me - sign * d
        leaves = jnp.logical_and(to >= 0, to < tiles)
        comes = jnp.logical_and(source >= 0, source < tiles)
        return copy, dst, leaves, comes

    span = tiles // n_yh
    farthest = REACH - 1
    beyond = (me - span, span - 1 - me)

    def hands_on(way, steps_back):
        return jnp.logical_and(beyond[way] >= steps_back, beyond[way] < farthest)

    def crosses(sign, d):
        return (me + sign * d + tiles) // span != (me + tiles) // span

    def row_copy(phase, n, sign, d, way):
        copy, dst, leaves, comes = halo_copy(strips.at[1 - way], rows_in.at[phase, way, d - 1], phase, n, sign, d)
        if d < farthest:
            leaves = jnp.logical_and(leaves, jnp.logical_not(crosses(sign, d)))
        return copy, dst, leaves, comes

    def row_copies(phase):
        copies = []
        for n, (sign, d) in enumerate(halo):
            way = 0 if sign > 0 else 1
            if d < REACH:
                copies.append(row_copy(phase, n, sign, d, way))
            else:
                copies.append(halo_copy(corners.at[1 - way], corners_in.at[phase, way], phase, n, sign, d))
        return copies

    def col_copies(phase):
        copies = []
        for way, sign in enumerate((1, -1)):
            copies.append(halo_copy(strips.at[3 - way], cols_in.at[phase, way], phase, len(halo) + way, sign, 1))
        return copies

    def halo_start(copies):
        for copy, _, leaves, _ in copies:
            pl.when(leaves)(copy.start)

    def rows_start(copies, crossing):
        for (sign, d), (copy, _, leaves, _) in zip(halo, copies):
            over = crosses(sign, d)
            pl.when(jnp.logical_and(leaves, over if crossing else jnp.logical_not(over)))(copy.start)

    def relay_copies(phase, way):
        sign = 1 - 2 * way
        return [
            remote(
                rows_in.at[phase, way, farthest - 1], rows_in.at[phase, way, farthest - i - 1],
                relay_send.at[phase, i - 1], halo_recv.at[phase, way * REACH + farthest - i - 1],
                dev(halo_tile(-sign, i)),
            )
            for i in range(1, farthest)
        ]

    def relay(phase):
        for way in range(2):

            @pl.when(hands_on(way, 1))
            def _(way=way):
                row_copies(phase)[way * REACH + farthest - 1][0].wait_recv()

            for i, copy in enumerate(relay_copies(phase, way)):
                pl.when(hands_on(way, i + 1))(copy.start)

    def relay_left(phase):
        for way in range(2):
            for i, copy in enumerate(relay_copies(phase, way)):
                pl.when(hands_on(way, i + 1))(copy.wait_send)

    def halo_arrive(copies):
        for n, (copy, dst, _, comes) in enumerate(copies):
            waits = comes
            if n < len(halo) and n % REACH == farthest - 1:
                waits = jnp.logical_and(comes, jnp.logical_not(hands_on(n // REACH, 1)))
            pl.when(waits)(copy.wait_recv)

            @pl.when(jnp.logical_not(comes))
            def _(dst=dst):
                dst[...] = jnp.zeros(dst.shape, BF16)

    def halo_left(copies):
        for copy, _, leaves, _ in copies:
            pl.when(leaves)(copy.wait_send)

    def match(direction, source):
        link = links[pl.ds(me, 1), direction : direction + 1]
        return jnp.where(jnp.logical_and(link == lax.convert_element_type(source, F32), link >= 0.0), 1.0, 0.0)

    def fill_halo(padded, phase):
        for way, sign in enumerate((-1, 1)):
            straight, left, right, beside = ((0, 4, 5, 2), (1, 6, 7, 3))[way]
            row = 0 if way == 0 else side + MARGIN
            straight_hit = [match(straight, me + sign * d) for d in range(1, 5)]
            left_hit = [match(left, me + sign * d) for d in range(1, 6)]
            right_hit = [match(right, me + sign * d) for d in range(1, 6)]
            far_hit = left_hit[4] if way == 0 else right_hit[4]
            for k in range(MARGIN):
                base = (row + k) * width
                lines = [rows_in[phase, way, d, k * side : (k + 1) * side, :].astype(F32) for d in range(4)]
                far = corners_in[phase, way, k * 16 : (k + 1) * 16, :].astype(F32)
                middle = sum(hit * line for hit, line in zip(straight_hit, lines))
                west = sum(hit * line[side - 8 :] for hit, line in zip(left_hit[:4], lines))
                east = sum(hit * line[:8] for hit, line in zip(right_hit[:4], lines))
                if way == 0:
                    west = west + far_hit * far[8:]
                else:
                    east = east + far_hit * far[:8]
                padded[base : base + 8, :] = west
                padded[base + 8 : base + 8 + side, :] = middle
                padded[base + 8 + side : base + 16 + side, :] = east
            hit = match(beside, me + sign)
            col = 8 - MARGIN if way == 0 else 8 + side
            for k in range(MARGIN):
                line = cols_in[phase, way, k * side : (k + 1) * side, :].astype(F32)
                padded[pl.ds(MARGIN * width + col + k, side, stride=width), :] = line * hit

    row_strips(pf)
    col_strips(pf)
    forward_halo = row_copies(0) + col_copies(0)
    halo_start(forward_halo)
    for k in range(1, early):
        grad_copy(k).start()

    for a in range(KERNEL):
        for b in range(KERNEL):
            n = (a * KERNEL + b) * 8
            taps[n : n + 8, :] = jnp.broadcast_to(depth_ref[a, b : b + 1, :], (8, LANES))

    def conv_block(padded, row, col, flip):
        base = row * width + col + 8 - MARGIN
        acc = [[None] * COLS for _ in range(ROWS)]
        for b in range(KERNEL):
            weights = []
            for a in range(KERNEL):
                n = a * KERNEL + b
                n = (KERNEL * KERNEL - 1 - n if flip else n) * 8
                weights.append(taps[n : n + 8, :])
            for r in range(ROWS + KERNEL - 1):
                for v in range(COLS):
                    value = padded[pl.ds(base + (r * width + v * 8 + b), 8), :]
                    for a in range(KERNEL):
                        i = r - a
                        if 0 <= i < ROWS:
                            term = value * weights[a]
                            acc[i][v] = term if acc[i][v] is None else acc[i][v] + term
        return acc

    col_steps = side // (8 * COLS)

    def filter_forward(k, c):
        col = pl.multiple_of(c * (8 * COLS), 8 * COLS)
        acc = conv_block(pf, k * ROWS, col, False)
        for i in range(ROWS):
            at = pl.multiple_of((k * ROWS + i) * side + col, 8 * COLS)
            y_all[pl.ds(at, 8 * COLS), :] = jnp.concatenate(acc[i], 0).astype(BF16)

    def conv_inner(n, _):
        filter_forward(1 + n // (col_steps - 2), 1 + n % (col_steps - 2))
        return 0

    inner = (row_steps - 2) * (col_steps - 2)
    lax.fori_loop(0, inner // 2, conv_inner, 0)
    relay(0)
    lax.fori_loop(inner // 2, inner, conv_inner, 0)
    for copy in weight_arrivals:
        copy.wait_recv()
    forwards = weight_forward(core)
    for copy in forwards:
        copy.start()
    halo_arrive(forward_halo)
    fill_halo(pf, 0)

    def y_copy(k):
        return remote(
            y_all.at[chunk_rows(line_at(other, k)), :], y_in.at[chunk_rows(k), :], y_sem.at[k], y_recv.at[k], peer
        )

    def conv_outer(n, _):
        away = n < steps
        k = jnp.where(away, line_at(other, n), line_at(h, n - steps))
        edge = jnp.logical_or(k == 0, k == row_steps - 1)

        def one(c, _):
            filter_forward(k, jnp.where(edge, c, c * (col_steps - 1)))
            return 0

        lax.fori_loop(0, jnp.where(edge, col_steps, 2), one, 0)

        @pl.when(away)
        def _():
            y_copy(n).start()

        @pl.when(jnp.logical_and(n + 1 >= early, n + 1 < steps))
        def _():
            grad_copy(n + 1).start()

        return 0

    lax.fori_loop(0, row_steps, conv_outer, 0)

    pars_copy.wait_recv()
    for copy in weight_forward(1 - core):
        copy.wait_recv()
    for copy in loads[1:4]:
        copy.wait()
    halo_left(forward_halo)
    mine = h == 0

    def ordered(own, others):
        return jnp.where(mine, own, others), jnp.where(mine, others, own)

    def row_of(n):
        own, others = pars[n : n + 1, 0:LANES], pars_in[n : n + 1, 0:LANES]
        return jnp.concatenate(ordered(own, others), 1)

    gamma_row = row_of(1)
    half_gamma = 0.5 * gamma_row
    scale_row = row_of(2)
    bias_rows = ordered(pars[0:1, :], pars_in[0:1, :])

    sums[...] = jnp.zeros_like(sums)
    gamma_acc[...] = jnp.zeros_like(gamma_acc)
    bias_acc[...] = jnp.zeros_like(bias_acc)
    taps_acc[...] = jnp.zeros_like(taps_acc)

    def conv_copy(k):
        at = chunk_rows(k)
        return remote(conv_send.at[at, :], conv_in.at[at, :], conv_sem.at[k], conv_recv.at[k], peer)

    def take_conv(k):
        conv_copy(k).wait_recv()
        for i in range(ROWS):
            at = pl.multiple_of((k * ROWS + i) * side, side)
            to = pl.multiple_of((MARGIN + line_at(other, k) * ROWS + i) * width + 8, 8)
            pg[pl.ds(to, side), :] = conv_in[pl.ds(at, side), :].astype(F32)

    def filter_line(line):
        row = line * ROWS

        def one(c, _):
            col = c * (8 * COLS)
            inner = (row + MARGIN) * width + col + 8
            base = row * width + col + 8 - MARGIN
            grads = [
                [pg[pl.ds(pl.multiple_of(inner, 8) + (i * width + v * 8), 8), :] for v in range(COLS)] for i in range(ROWS)
            ]
            for b in range(KERNEL):
                acc = [None] * KERNEL
                for r in range(ROWS + KERNEL - 1):
                    for v in range(COLS):
                        value = pf[pl.ds(base + (r * width + v * 8 + b), 8), :]
                        for a in range(KERNEL):
                            i = r - a
                            if 0 <= i < ROWS:
                                term = value * grads[i][v]
                                acc[a] = term if acc[a] is None else acc[a] + term
                for a in range(KERNEL):
                    n = (a * KERNEL + b) * 8
                    taps_acc[n : n + 8, :] += acc[a]
            return 0

        lax.fori_loop(0, col_steps, one, 0)

    def mlp(k, _):
        at = chunk_rows(k)
        line = line_at(h, k)
        own_at = chunk_rows(line)
        y_copy(k).wait_recv()
        grad_copy(k).wait_recv()
        low, high = ordered(y_all[own_at, :].astype(F32), y_in[at, :].astype(F32))
        y = jnp.concatenate((low, high), 1)
        centred = y - jnp.sum(y, 1, keepdims=True) * (1.0 / CHAN)
        spread = jnp.sum(centred * centred, 1, keepdims=True) * (1.0 / CHAN)
        inv_spread = lax.rsqrt(spread + 1e-06)
        unit = centred * inv_spread
        normed = (unit * gamma_row).astype(BF16)
        wet = mask_ref[own_at, :].astype(F32)
        low, high = ordered(c_ref[own_at, :].astype(F32), grad_in[at, :].astype(F32))
        branch_grad = (jnp.concatenate((low * wet, high * wet), 1) * scale_row).astype(BF16)
        branch_t = branch_grad.T
        normed_t = jnp.concatenate((normed.T, jnp.ones((16, chunk), BF16)), 0)
        norm_grad = jnp.zeros((chunk, CHAN), F32)
        for block in range(HIDDEN // BLOCK):
            slot, off = divmod(block * BLOCK, HALF_HIDDEN)
            w_up = wu[slot, :, off : off + BLOCK]
            w_down = wd[slot, off : off + BLOCK, :]
            cols = slice(block * BLOCK, (block + 1) * BLOCK)
            hidden = nn(normed, w_up) + bias_rows[slot][:, off : off + BLOCK]
            activated, slope = gelu_pieces(hidden)
            hidden_grad = (nt(branch_grad, w_down) * slope).astype(BF16)
            sums[1, :, cols] += nn(branch_t, activated.astype(BF16))
            up_terms = nn(normed_t, hidden_grad)
            sums[0, :, cols] += up_terms[:CHAN]
            bias_acc[:, cols] += up_terms[CHAN : CHAN + 8]
            norm_grad = norm_grad + nt(hidden_grad, w_up)
        gamma_acc[...] += jnp.sum((norm_grad * unit).reshape(chunk // 8, 8, CHAN), 0)
        scaled = norm_grad * half_gamma
        mean = jnp.sum(scaled, 1, keepdims=True) * (1.0 / CHAN)
        tilt = jnp.sum(scaled * unit, 1, keepdims=True) * (1.0 / CHAN)
        conv_grad = (inv_spread * (scaled - mean - unit * tilt)).astype(BF16).astype(F32)
        own, away = ordered(conv_grad[:, :LANES], conv_grad[:, LANES:])
        conv_send[at, :] = away.astype(BF16)
        conv_copy(k).start()
        for i in range(ROWS):
            to = pl.multiple_of((MARGIN + line * ROWS + i) * width + 8, 8)
            pg[pl.ds(to, side), :] = own[i * side : (i + 1) * side]
        filter_line(line)

        @pl.when(k == steps - 1)
        def _():
            take_conv(0)
            row_strips(pg)
            rows = row_copies(1)
            rows_start(rows, False)
            rows_start(rows, True)

        return 0

    lax.fori_loop(0, steps, mlp, 0)

    core_out[...] = sums[1 - core].astype(BF16)
    rs_core = remote(core_out, ring_core, rs_send.at[0], rs_recv.at[0], core_peer)
    rs_core.start()

    ident = lax.broadcasted_iota(jnp.int32, (CHAN, CHAN), 0) == lax.broadcasted_iota(jnp.int32, (CHAN, CHAN), 1)
    down_sums = sums[1]
    down_high = down_sums.astype(BF16)
    down_low = (down_sums - down_high.astype(F32)).astype(BF16)
    paired = jnp.zeros((CHAN, CHAN), F32)
    for slot in range(2):
        cols = slice(slot * HALF_HIDDEN, (slot + 1) * HALF_HIDDEN)
        paired = paired + nn(down_high[:, cols], wd[slot]) + nn(down_low[:, cols], wd[slot])
    scale_sum = 0.5 * jnp.sum(jnp.where(ident, paired, 0.0), 0, keepdims=True) / scale_row
    gamma_sum = 0.5 * jnp.sum(gamma_acc[...], 0, keepdims=True)
    bias_sum = 0.5 * bias_acc[0:1, :]
    small_peer[...] = jnp.zeros_like(small_peer)
    small_a[...] = jnp.zeros_like(small_a)
    n_taps = KERNEL * KERNEL

    def put_small(ref, at, value, n):
        own, away = ordered(value[:, : n * LANES], value[:, n * LANES :])
        for i in range(n):
            ref[0][ref[1] + at + i : ref[1] + at + i + 1, :] = own[:, i * LANES : (i + 1) * LANES]
            small_peer[at + i : at + i + 1, :] = away[:, i * LANES : (i + 1) * LANES]

    place = (small_a, n_taps)
    put_small(place, 0, gamma_sum, 1)
    put_small(place, 1, scale_sum, 1)
    put_small(place, 2, bias_sum, 4)
    small_chan = remote(small_peer, small_peer_in, sm_send.at[0], sm_recv.at[0], peer)
    small_chan.start()

    def input_block(line, c):
        row = line * ROWS
        col = pl.multiple_of(c * (8 * COLS), 8 * COLS)
        acc = conv_block(pg, row, col, True)
        for i in range(ROWS):
            at = pl.ds(pl.multiple_of((row + i) * side + col, 8 * COLS), 8 * COLS)
            wet = mask_ref[at, :].astype(F32)
            grad = c_ref[at, :].astype(F32)
            out_ref[at, :] = (wet * (grad + jnp.concatenate(acc[i], 0))).astype(BF16)

    inner_cols = col_steps - 2

    def own_inner(n, _):
        input_block(line_at(h, 1 + n // inner_cols), 1 + n % inner_cols)
        return 0

    def rest_inner(n, _):
        k = 1 + n // inner_cols
        input_block(jnp.where(k == steps, line_at(h, steps - 1), line_at(other, k)), 1 + n % inner_cols)
        return 0

    def input_edges(k, _):
        edge = jnp.logical_or(k == 0, k == row_steps - 1)

        def one(c, _):
            input_block(k, jnp.where(edge, c, c * (col_steps - 1)))
            return 0

        lax.fori_loop(0, jnp.where(edge, col_steps, 2), one, 0)
        return 0

    def peer_line(k, _):
        @pl.when(k > 0)
        def _():
            take_conv(k)

        filter_line(line_at(other, k))
        return 0

    own = (steps - 2) * inner_cols
    lax.fori_loop(0, own // 2, own_inner, 0)
    lax.fori_loop(0, 1, peer_line, 0)

    rs_core.wait_recv()
    sums[core] = sums[core] + ring_core[...].astype(F32)
    ring_out[...] = sums[core].astype(BF16)
    a_rows, b_rows = CHAN // n_x, CHAN // n_x // n_z
    rs_a = []
    for k, a in enumerate(a_peers):
        piece = ring_out.at[pl.ds(pl.multiple_of(a * a_rows, a_rows), a_rows), :]
        rs_a.append(remote(piece, ring_a.at[k], rs_send.at[1 + k], rs_recv.at[1 + k], dev(ring_tile(a, second))))
    for copy in rs_a:
        copy.start()

    lax.fori_loop(own // 2, own, own_inner, 0)
    lax.fori_loop(1, steps - 2, peer_line, 0)

    for copy in rs_a:
        copy.wait_recv()
    a_at = pl.ds(pl.multiple_of(first * a_rows, a_rows), a_rows)
    sums[core, a_at, :] = sums[core, a_at, :] + sum(ring_a[k].astype(F32) for k in range(n_x - 1))
    rs_b = []
    for k, b in enumerate(b_peers):
        piece = sums.at[core, pl.ds(pl.multiple_of(first * a_rows + b * b_rows, b_rows), b_rows), :]
        rs_b.append(remote(piece, ring_b.at[k], rs_send.at[4 + k], rs_recv.at[4 + k], dev(ring_tile(first, b))))
    for copy in rs_b:
        copy.start()

    relay(1)
    lax.fori_loop(steps - 2, steps - 1, peer_line, 0)
    rest = steps * inner_cols
    lax.fori_loop(0, rest // 2, rest_inner, 0)

    for copy in rs_b:
        copy.wait_recv()
    b_start = first * a_rows + second * b_rows
    b_at = pl.ds(pl.multiple_of(b_start, b_rows), b_rows)
    sums[core, b_at, :] = sums[core, b_at, :] + sum(ring_b[k] for k in range(n_x - 1))

    def y_piece(chan):
        return (core, b_at, pl.ds(pl.multiple_of(chan * HALF_HIDDEN, HALF_HIDDEN), HALF_HIDDEN))

    y_slot = 2 * at_yh + h
    ring_y[y_slot] = sums[y_piece(h)]
    rs_y = []
    for k, (dy, dc) in enumerate(y_peers):
        piece = sums.at[y_piece((h + dc) % 2)]
        rs_y.append(remote(piece, ring_y.at[y_slot], rs_send.at[7 + k], rs_recv.at[7 + k], y_dev(dy, dc)))
    for copy in rs_y:
        copy.start()

    take_conv(steps - 1)
    col_strips(pg)
    last_halo = col_copies(1)
    halo_start(last_halo)
    filter_line(line_at(other, steps - 1))

    for n in range(n_taps):
        small_a[n : n + 1, :] = jnp.sum(taps_acc[n * 8 : n * 8 + 8, :], 0, keepdims=True)
    small_chan.wait_recv()
    for n in range(6):
        small_a[n_taps + n : n_taps + n + 1, :] += small_peer_in[n : n + 1, :]
    sm_core = remote(small_a, small_core, sm_send.at[1], sm_recv.at[1], core_peer)
    sm_core.start()

    lax.fori_loop(rest // 2, rest * 3 // 4, rest_inner, 0)

    sm_core.wait_recv()

    def small_stage(ref, value, at, size, base, tile):
        ref[at] = value
        copies = []
        for k in range(1, size):
            there = (at + k) % size
            copies.append(
                remote(ref.at[at], ref.at[at], sm_send.at[base + k - 1], sm_recv.at[base + k - 1], dev(tile(there)))
            )
        for copy in copies:
            copy.start()
        return copies

    sm_x = small_stage(
        small_x, small_a[...] + small_core[...], at_x, n_x, 2, lambda x: tile_at(at_yh, at_z, x, core)
    )
    lax.fori_loop(rest * 3 // 4, rest, rest_inner, 0)

    for copy in rs_y:
        copy.wait_recv()
    total[core, b_at, :] = ((ring_y[0] + ring_y[1]) + (ring_y[2] + ring_y[3])).astype(BF16)
    ag_b = []
    for k, b in enumerate(b_peers):
        block = total.at[core, b_at, :]
        ag_b.append(remote(block, block, ag_send.at[1 + k], ag_recv.at[1 + k], dev(ring_tile(first, b))))
    for copy in ag_b:
        copy.start()

    first_halo = row_copies(1)
    halo_arrive(first_halo + last_halo)
    fill_halo(pg, 1)
    marks = [row_steps * n // 4 for n in range(5)]
    lax.fori_loop(marks[0], marks[1], input_edges, 0)

    for copy in sm_x:
        copy.wait_recv()
    sm_z = small_stage(
        small_z, sum(small_x[k] for k in range(n_x)), at_z, n_z, 5, lambda z: tile_at(at_yh, z, at_x, core)
    )
    for copy in ag_b:
        copy.wait_recv()
    ag_a = []
    for k, a in enumerate(a_peers):
        block = total.at[core, a_at, :]
        ag_a.append(remote(block, block, ag_send.at[4 + k], ag_recv.at[4 + k], dev(ring_tile(a, second))))
    for copy in ag_a:
        copy.start()

    lax.fori_loop(marks[1], marks[3], input_edges, 0)

    for copy in sm_z:
        copy.wait_recv()
    sm_y = small_stage(
        small_y, sum(small_z[k] for k in range(n_z)), at_yh, 2, 8, lambda yh: tile_at(yh, at_z, at_x, core)
    )
    for copy in ag_a:
        copy.wait_recv()
    ag_core = remote(total.at[core], total.at[core], ag_send.at[7], ag_recv.at[7], core_peer)
    ag_core.start()

    lax.fori_loop(marks[3], marks[4], input_edges, 0)

    @pl.when(core == 0)
    def _():
        up_sum_ref[...] = total[0].astype(F32) * (0.5 * q)

    @pl.when(core == 1)
    def _():
        down_sum_ref[...] = total[1].astype(F32).T * (0.5 * q)

    for copy in sm_y:
        copy.wait_recv()
    small = (small_y[0] + small_y[1]) * q
    for a in range(KERNEL):
        taps_ref[a] = small[a * KERNEL : (a + 1) * KERNEL]
    gain_ref[...] = small[n_taps : n_taps + 1].reshape(LANES)
    scale_sum_ref[...] = small[n_taps + 1 : n_taps + 2].reshape(LANES)
    for i in range(4):
        bias_sum_ref[i * LANES : (i + 1) * LANES] = small[n_taps + 2 + i : n_taps + 3 + i].reshape(LANES)
    ag_core.wait_recv()

    @pl.when(core == 1)
    def _():
        up_sum_ref[...] = total[0].astype(F32) * (0.5 * q)

    @pl.when(core == 0)
    def _():
        down_sum_ref[...] = total[1].astype(F32).T * (0.5 * q)

    halo_left(first_halo + last_halo)
    relay_left(0)
    relay_left(1)
    for copy in weight_copies + forwards + [pars_copy, rs_core, small_chan, sm_core, ag_core]:
        copy.wait_send()
    for copy in rs_a + rs_b + rs_y + ag_a + ag_b + sm_x + sm_z + sm_y:
        copy.wait_send()

    def finish(k, _):
        grad_copy(k).wait_send()
        y_copy(k).wait_send()
        conv_copy(k).wait_send()
        return 0

    lax.fori_loop(0, steps, finish, 0)


SHAPES = {64: (2, 4, 4, 2), 16: (2, 2, 2, 2)}


def hand_over(*refs):
    count = len(refs) // 2
    for source, result in zip(refs[:count], refs[count:]):
        result[...] = source[...]


def place(results):
    whole = pl.BlockSpec(memory_space=pltpu.VMEM)
    return pl.pallas_call(
        hand_over,
        out_shape=tuple(jax.ShapeDtypeStruct(r.shape, r.dtype) for r in results),
        in_specs=[whole] * len(results),
        out_specs=(whole,) * len(results),
    )(*(pltpu.with_memory_space_constraint(r, pltpu.VMEM) for r in results))


def block_call(inputs, cotangent, wet, neighbours, depth_weight, gamma, up_weight, up_bias, down_weight, layer_scale):
    side = inputs.shape[1]
    half_chan = inputs.shape[3]
    flat = (side * side, half_chan)
    shape4 = SHAPES[lax.axis_size("tiles")]
    n_yh, n_z, n_x, n_core = shape4
    width = side + 16
    cells = side * side // 2
    row_steps = side // ROWS
    steps = row_steps // 2
    a_rows = CHAN // n_x
    vmem = pltpu.VMEM
    whole = pl.BlockSpec(memory_space=pltpu.VMEM)
    hbm = pl.BlockSpec(memory_space=pl.ANY)
    dma = pltpu.SemaphoreType.DMA
    padded = vmem(((side + 2 * MARGIN) * width, LANES), F32)
    taps = vmem((KERNEL * KERNEL * 8, LANES), F32)
    piece = vmem((cells, LANES), BF16)
    small = vmem((64, LANES), F32)
    pars = vmem((8, HALF_HIDDEN), F32)
    tile = vmem((side * side, LANES), BF16)
    scratch = [
        vmem((LANES, LANES), F32), tile, tile, dma((4,)),
        padded, padded, taps, taps,
        vmem((4, MARGIN * side, LANES), BF16),
        vmem((2, MARGIN * 16, LANES), BF16),
        vmem((2, 2, 4, MARGIN * side, LANES), BF16),
        vmem((2, 2, MARGIN * side, LANES), BF16),
        vmem((2, 2, MARGIN * 16, LANES), BF16),
        vmem((2, CHAN, HALF_HIDDEN), BF16),
        vmem((2, HALF_HIDDEN, CHAN), BF16),
        pars, pars,
        tile, vmem((LANES, LANES), F32),
        piece, tile, piece, piece, piece,
        vmem((2, CHAN, HIDDEN), F32),
        vmem((8, CHAN), F32),
        vmem((8, HIDDEN), F32),
        vmem((CHAN, HIDDEN), BF16), vmem((CHAN, HIDDEN), BF16), vmem((CHAN, HIDDEN), BF16),
        vmem((n_x - 1, a_rows, HIDDEN), BF16),
        vmem((n_x - 1, a_rows // n_z, HIDDEN), F32),
        vmem((4, a_rows // n_z, HALF_HIDDEN), F32),
        vmem((2, CHAN, HALF_HIDDEN), BF16),
        small, vmem((8, LANES), F32), vmem((8, LANES), F32), small,
        vmem((n_x, 64, LANES), F32), vmem((n_z, 64, LANES), F32), vmem((2, 64, LANES), F32),
        dma((2, 12)), dma((2, 12)), dma((2, 3)), dma((7,)), dma((7,)),
        dma((steps,)), dma((steps,)), dma((steps,)), dma((steps,)), dma((steps,)), dma((steps,)),
        dma((10,)), dma((10,)), dma((8,)), dma((8,)), dma((9,)), dma((9,)),
    ]
    return pl.pallas_call(
        functools.partial(kernel, side, shape4),
        out_shape=(
            vmem(flat, BF16),
            vmem((KERNEL, KERNEL, LANES), F32),
            vmem((LANES,), F32),
            vmem((CHAN, HALF_HIDDEN), F32),
            vmem((HALF_HIDDEN,), F32),
            vmem((HALF_HIDDEN, CHAN), F32),
            vmem((LANES,), F32),
        ),
        in_specs=[whole, hbm, hbm, whole, whole, whole, hbm, whole, hbm, whole],
        out_specs=(whole, whole, whole, whole, whole, whole, whole),
        scratch_shapes=scratch,
        compiler_params=pltpu.CompilerParams(
            collective_id=0, has_side_effects=True, vmem_limit_bytes=58 * 1024 * 1024
        ),
    )(
        neighbours.T,
        inputs.reshape(flat),
        cotangent.reshape(flat),
        wet[0],
        depth_weight,
        gamma,
        up_weight,
        up_bias,
        down_weight,
        layer_scale,
    )


def body(
    inputs,
    cotangent,
    wet,
    neighbours,
    depth_weight,
    gamma,
    up_weight,
    up_bias,
    down_weight,
    layer_scale,
):
    grad, *sums = block_call(
        inputs, cotangent, wet, neighbours, depth_weight, gamma, up_weight, up_bias, down_weight, layer_scale
    )
    return (grad.reshape(inputs.shape), *place(sums))


def solution(mesh):
    return jax.shard_map(
        body,
        mesh=mesh,
        in_specs=(
            P("tiles", None, None, "chan"),
            P("tiles", None, None, "chan"),
            P("tiles", None, None),
            P(),
            P(None, None, "chan"),
            P("chan"),
            P(None, "chan"),
            P("chan"),
            P("chan", None),
            P("chan"),
        ),
        out_specs=(
            P("tiles", None, None, "chan"),
            P(None, None, "chan"),
            P("chan"),
            P(None, "chan"),
            P("chan"),
            P("chan", None),
            P("chan"),
        ),
        check_vma=False,
    )
```
